128 devices in a mesh: seq: 32 (over x, z, core), exp: 4 (over y).
Axes of the slice: x: 4, y: 4, z: 4, core: 2. Of those that a mesh axis runs over, the one named last changes fastest.
Arguments:
- candidate: bfloat16 [4096, 4096], P('seq'), may hold values from -2 to 2
- in_proj: bfloat16 [4096, 4096], P(None, 'exp'), may hold values from -0.09375 to 0.09375
- bc_proj: bfloat16 [4096, 256], replicated, may hold values from -0.0078125 to 0.0078125
- step_proj: bfloat16 [4096, 32], P(None, 'exp'), may hold values from -0.875 to 0.875
- step_bias: float32 [32], P('exp'), may hold values from -1 to 1
- decay_rate: float32 [32], P('exp'), may hold values from 2e-05 to 0.04
- skip_gain: float32 [32], P('exp'), may hold values from 0.5 to 1.5
- out_proj: bfloat16 [4096, 4096], P('exp'), may hold values from -0.09375 to 0.09375
- expert_ids: int32 [4096, 2], P('seq'), may hold values from 0 to 15, all different within a row; in each aligned block of 128 rows (0 to 127, 128 to 255, ...) at most 24 rows name the same one
- gate_weights: bfloat16 [4096, 2], P('seq'), may hold values from 0.099609375 to 0.8984375
- expert_gate: bfloat16 [4, 4096, 8192], P('exp', None, 'seq'), may hold values from -0.09375 to 0.09375
- expert_up: bfloat16 [4, 4096, 8192], P('exp', None, 'seq'), may hold values from -0.09375 to 0.09375
- expert_down: bfloat16 [4, 8192, 4096], P('exp', 'seq'), may hold values from -0.0625 to 0.0625
- energy_head: float32 [4096], replicated, may hold values from -6 to 6
Outputs:
- new_candidate: bfloat16 [4096, 4096], P('seq', 'exp')
The draws below stay inside these ranges and needn't reach their ends.
Inputs may be any that keep to these rules, and one draw needn't show every extreme that they name: `expert_ids`: each row names 2 different experts. In the rows of one device no expert is named by more than 24 rows, a bound that some block reaches. Experts 4 and above are not computed in this layer and add nothing.
All inputs are finite; a program needn't handle non-finite values.
Results may differ from the reference program's by a relative error of at most 0.011.
Values may be sent and summed in bfloat16 or wider, within the bound.
No kernel may reach another device: no remote copies, remote signals or barrier semaphores. Data moves between devices by JAX's collectives and lax.ppermute only.
A program may use at most 128 MiB of HBM per device.

```python
import math
from functools import partial
import jax
import jax.numpy as jnp
import numpy as np
from jax import lax

D = 4096
HEADS = 32
HEAD_DIM = 128
STATE = 128
FF = 8192
ROUTED = 16
TOP = 2
EXPERTS = 4
TOK_DEV = 128
CAP = 24
TOKENS = 4096
N_SEQ = 32


def draw_candidate(key, part):
    key = jax.random.fold_in(key, 7)
    noise_key = jax.random.fold_in(key, 1)
    block_key = jax.random.fold_in(key, 2)
    noise = 0.33 * jax.random.normal(noise_key, (TOKENS, D), jnp.float32)
    shared = 0.3 * jax.random.normal(block_key, (TOKENS // TOK_DEV, D), jnp.float32)
    values = noise + jnp.repeat(shared, TOK_DEV, axis=0)
    return jnp.clip(values, -2.0, 2.0).astype(jnp.bfloat16)


def block_scale(key, extent, pieces, low, high):
    gain, own = 1.0, jax.random.fold_in(key, 6)
    for axis_at, blocks in pieces:
        steps = jnp.exp(jax.random.uniform(jax.random.fold_in(own, axis_at), (blocks,), jnp.float32, low / len(pieces), high / len(pieces)))
        gain = gain * jnp.repeat(steps, extent[axis_at] // blocks).reshape([-1 if axis == axis_at else 1 for axis in range(len(extent))])
    return gain


def shared_out(key, own, number, rows, count, top, limit, lean):
    order = jax.random.permutation(key, count)
    packed, ordinary = load_shares(count, rows * top, limit, lean, True), load_shares(count, rows * top, limit, lean, False)
    places = jnp.arange(count)

    def named(lengths, rotation):
        used = int((lengths > 0).sum())
        fixed = max(1, used // 4)
        passed = fixed + (places - fixed + rotation * (used - fixed)) % max(1, count - fixed)
        return jnp.zeros((count,), jnp.int32).at[order[jnp.where(places < fixed, places, passed)]].set(jnp.asarray(lengths, jnp.int32))

    lengths = jnp.where(number % 4 == 0, named(packed, number // 4), named(ordinary, number - number // 4 - 1))
    mixed = jax.random.permutation(jax.random.fold_in(own, 3), count)
    source_of, taker = mixed[0:count // 2 * 2:2], mixed[1:count // 2 * 2:2]
    slack = jnp.minimum(lengths[source_of] - 1, limit - lengths[taker]) // 2
    slack = jnp.where((source_of == order[0]) | (taker == order[0]) | (lengths[taker] == 0), 0, jnp.maximum(slack, 0))
    passed = jax.random.randint(jax.random.fold_in(own, 4), (count // 2,), 0, 1 << 20) % (slack + 1)
    lengths = lengths.at[source_of].add(-passed).at[taker].add(passed)
    items = jnp.searchsorted(jnp.cumsum(lengths), jnp.arange(rows * top), side="right").astype(jnp.int32)
    listing = items.reshape(top, rows).T
    listing = listing[jax.random.permutation(jax.random.fold_in(own, 1), rows)]
    rotation = jax.random.randint(jax.random.fold_in(own, 2), (rows, 1), 0, top)
    return jnp.take_along_axis(listing, (jnp.arange(top)[None, :] + rotation) % top, axis=1)


def load_shares(amount, total, bound, slope, full):
    portions = [(1 << 20) // math.isqrt(rank ** slope) + 1 for rank in range(1, amount + 1)]
    largest = bound if full else min(bound, max(-(-total // amount), total * portions[0] // sum(portions)))
    least = 1 if total - largest >= amount - 1 else 0
    holding, rest = [largest] + [least] * (amount - 1), total - largest - least * (amount - 1)
    while rest > 0:
        candidates = [i for i in range(1, amount) if holding[i] < largest] or [i for i in range(1, amount) if holding[i] < bound]
        mass, remaining = sum([portions[i] for i in candidates]), rest
        for i in candidates:
            more = min(bound - holding[i], max(1, remaining * portions[i] // mass), rest)
            holding[i] = holding[i] + more
            rest = rest - more
    return np.array(holding)


def bell_draw(key, shape, deviation, limit, split=(), dtype=jnp.bfloat16):
    factor_of = block_scale(key, shape, split, -0.22, 0.18) if split else 1.0
    values = jax.random.normal(key, shape, jnp.float32) * deviation * factor_of
    return jnp.minimum(jnp.maximum(values, -limit), limit).astype(dtype)


def setup_inputs(seed: int = 0) -> dict:
    arg_keys = jax.random.split(jax.random.key(seed), 15)
    candidate = draw_candidate(jax.random.fold_in(arg_keys[14], 71), 0)
    in_proj = bell_draw(arg_keys[1], (D, HEADS * HEAD_DIM), D ** -0.5, 0.09375, ((1, 4),))
    bc_proj = bell_draw(arg_keys[2], (D, 2 * STATE), (D * 112) ** -0.5, 0.0078125)
    step_proj = bell_draw(arg_keys[3], (D, HEADS), (max(D // 81, 1)) ** -0.5, 0.875, ((1, 4),))
    step_bias = jnp.clip(jax.random.uniform(arg_keys[4], (HEADS,), jnp.float32, -1.0, 1.0) * block_scale(arg_keys[4], (HEADS,), ((0, 4),), -0.4, 0.0), -1.0, 1.0)
    decay_rate = jnp.clip(jnp.exp(math.log(0.04) - 7.6009025 * jax.random.uniform(arg_keys[5], (HEADS,), jnp.float32) ** block_scale(arg_keys[5], (HEADS,), ((0, 4),), -0.2, 0.2)), 1.9999999494757503e-05, 0.04)
    skip_gain = jnp.clip(0.5 + 1.0 * jax.random.uniform(arg_keys[6], (HEADS,), jnp.float32) ** block_scale(arg_keys[6], (HEADS,), ((0, 4),), -0.2, 0.2), 0.5, 1.5)
    out_proj = bell_draw(arg_keys[7], (HEADS * HEAD_DIM, D), (HEADS * HEAD_DIM) ** -0.5, 0.09375, ((0, 4),))
    expert_ids_keys = jax.random.split(jax.random.fold_in(arg_keys[8], 1), TOKENS // TOK_DEV)
    expert_ids_turns = jax.random.permutation(jax.random.fold_in(arg_keys[8], 3), TOKENS // TOK_DEV)
    expert_ids = jax.vmap(lambda own, number: shared_out(jax.random.fold_in(arg_keys[8], 2), own, number, TOK_DEV, ROUTED, TOP, CAP, 2))(expert_ids_keys, expert_ids_turns).reshape((TOKENS, TOP))
    gate_weights = jnp.clip(0.099609375 + 0.7988281 * jax.random.uniform(arg_keys[9], (TOKENS, TOP), jnp.float32) ** block_scale(arg_keys[9], (TOKENS, TOP), ((0, 32),), -0.2, 0.2), 0.099609375, 0.8984375).astype(jnp.bfloat16)
    expert_gate = bell_draw(arg_keys[10], (EXPERTS, D, FF), D ** -0.5, 0.09375, ((0, 4), (2, 32)))
    expert_up = bell_draw(arg_keys[11], (EXPERTS, D, FF), D ** -0.5, 0.09375, ((0, 4), (2, 32)))
    expert_down = bell_draw(arg_keys[12], (EXPERTS, FF, D), FF ** -0.5, 0.0625, ((0, 4), (1, 32)))
    energy_head = bell_draw(arg_keys[13], (D,), 1.0, 6.0, (), jnp.float32)
    return {"candidate": candidate, "in_proj": in_proj, "bc_proj": bc_proj, "step_proj": step_proj, "step_bias": step_bias, "decay_rate": decay_rate, "skip_gain": skip_gain, "out_proj": out_proj, "expert_ids": expert_ids, "gate_weights": gate_weights, "expert_gate": expert_gate, "expert_up": expert_up, "expert_down": expert_down, "energy_head": energy_head}


EPS = 1e-05
DESCENT = 0.5
HIGH = lax.Precision.HIGHEST

def chain_terms(b_rows, step, inner, rate):
    tlen = step.shape[0]
    rowpos = lax.broadcasted_iota(jnp.int32, (tlen, tlen), 0)
    colpos = lax.broadcasted_iota(jnp.int32, (tlen, tlen), 1)
    lower = (rowpos >= colpos).astype(jnp.float32)
    cum = jnp.dot(lower, -step * rate[None, :], precision=HIGH)
    last = cum[-1]
    tail = jnp.exp(last[None, :] - cum) * step
    fresh = jnp.einsum('th,thp,tn->hpn', tail, inner, b_rows, precision=HIGH)
    return (jnp.exp(last), fresh, jnp.exp(cum))

def block_mix(inner, b_rows, c_rows, step, rate, skip_gain, state):
    tlen = inner.shape[0]
    rowpos = lax.broadcasted_iota(jnp.int32, (tlen, tlen), 0)
    colpos = lax.broadcasted_iota(jnp.int32, (tlen, tlen), 1)
    lower = (rowpos >= colpos).astype(jnp.float32)
    cum = jnp.dot(lower, -step * rate[None, :], precision=HIGH)
    gaps = cum.T[:, :, None] - cum.T[:, None, :]
    weights = lower[None] * jnp.exp(jnp.minimum(gaps, 0.0))
    scores = jnp.dot(c_rows, b_rows.T, precision=HIGH)
    mixing = weights * scores[None] * step.T[:, None, :]
    result = jnp.einsum('hts,shp->thp', mixing, inner, precision=HIGH)
    growth = jnp.exp(cum)
    result = result + growth[:, :, None] * jnp.einsum('tn,hpn->thp', c_rows, state, precision=HIGH)
    result = result + skip_gain[None, :, None] * inner
    last = cum[-1]
    tail = jnp.exp(last[None, :] - cum) * step
    new_state = jnp.exp(last)[:, None, None] * state + jnp.einsum('th,thp,tn->hpn', tail, inner, b_rows, precision=HIGH)
    return (result, new_state)

def chain_combine(earlier, later):
    return (earlier[0] * later[0], later[0][:, None, None] * earlier[1] + later[1])

def slot_table(ids_rows, gate_rows, expert, slots):
    tlen = ids_rows.shape[0]
    match = ids_rows == expert
    hits = lax.optimization_barrier(jnp.sum(match.astype(jnp.float32), axis=1))
    weight = lax.optimization_barrier(jnp.sum(jnp.where(match, gate_rows.astype(jnp.float32), 0.0), axis=1))
    rowpos = lax.broadcasted_iota(jnp.int32, (tlen, tlen), 0)
    colpos = lax.broadcasted_iota(jnp.int32, (tlen, tlen), 1)
    strict = (rowpos > colpos).astype(jnp.float32)
    places = jnp.dot(strict, hits, precision=HIGH)
    slot_pos = lax.broadcasted_iota(jnp.int32, (slots, tlen), 0).astype(jnp.float32)
    table = jnp.where((places[None, :] == slot_pos) & (hits[None, :] > 0.0), 1.0, 0.0).astype(jnp.float32)
    return (table, weight)

def expert_terms(rows, w_gate, w_up, head_vec):
    gate_val = jnp.dot(rows, w_gate, preferred_element_type=jnp.float32)
    up_val = jnp.dot(rows, w_up, preferred_element_type=jnp.float32)
    sig = jax.nn.sigmoid(gate_val)
    first = (head_vec * up_val * sig * (1.0 + gate_val * (1.0 - sig))).astype(jnp.bfloat16)
    second = (head_vec * gate_val * sig).astype(jnp.bfloat16)
    return jnp.dot(first, w_gate.T, preferred_element_type=jnp.float32) + jnp.dot(second, w_up.T, preferred_element_type=jnp.float32)

def reference(candidate, in_proj, bc_proj, step_proj, step_bias, decay_rate, skip_gain, out_proj, expert_ids, gate_weights, expert_gate, expert_up, expert_down, energy_head):
    inner_b = jnp.dot(candidate, in_proj, preferred_element_type=jnp.float32).astype(jnp.bfloat16)
    bc_val = jnp.dot(candidate, bc_proj, preferred_element_type=jnp.float32)
    pre_step = jnp.dot(candidate, step_proj, preferred_element_type=jnp.float32) + step_bias[None, :]
    step = jax.nn.softplus(pre_step)
    inner_blk = inner_b.astype(jnp.float32).reshape(N_SEQ, TOK_DEV, HEADS, HEAD_DIM)
    b_blk = bc_val[:, :STATE].reshape(N_SEQ, TOK_DEV, STATE)
    c_blk = bc_val[:, STATE:].reshape(N_SEQ, TOK_DEV, STATE)
    step_blk = step.reshape(N_SEQ, TOK_DEV, HEADS)

    def mixer(inner_v, b_v, c_v, step_v, state_v):
        return block_mix(inner_v, b_v, c_v, step_v, decay_rate, skip_gain, state_v)

    def forward(state, blk):
        result, new_state = mixer(blk[0], blk[1], blk[2], blk[3], state)
        return (new_state, (result, state))
    start_state = jnp.zeros((HEADS, HEAD_DIM, STATE), jnp.float32)
    _, (mixed_blk, states_in) = lax.scan(forward, start_state, (inner_blk, b_blk, c_blk, step_blk))
    mixed = mixed_blk.reshape(TOKENS, HEADS * HEAD_DIM).astype(jnp.bfloat16)
    mix_sum = jnp.dot(mixed, out_proj, preferred_element_type=jnp.float32)
    hidden = (candidate.astype(jnp.float32) + mix_sum).astype(jnp.bfloat16)
    hidden_f = hidden.astype(jnp.float32)
    scale = jnp.sqrt(lax.optimization_barrier(jnp.mean(hidden_f * hidden_f, axis=-1, keepdims=True)) + EPS)
    normed = hidden_f / scale
    routed = normed.astype(jnp.bfloat16).reshape(N_SEQ, TOK_DEV, D)
    ids_blk = expert_ids.reshape(N_SEQ, TOK_DEV, TOP)
    gates_blk = gate_weights.reshape(N_SEQ, TOK_DEV, TOP)
    token_grad = jnp.zeros((TOKENS, D), jnp.float32)
    for expert in range(EXPERTS):
        tables, weights = jax.vmap(partial(slot_table, expert=expert, slots=CAP))(ids_blk, gates_blk)
        rows = jax.vmap(lambda tab, blk: jnp.dot(tab.astype(jnp.bfloat16), blk, preferred_element_type=jnp.float32))(tables, routed)
        rows = rows.astype(jnp.bfloat16).reshape(N_SEQ * CAP, D)
        head_vec = jnp.dot(expert_down[expert].astype(jnp.float32), energy_head, precision=HIGH)
        terms = expert_terms(rows, expert_gate[expert], expert_up[expert], head_vec).reshape(N_SEQ, CAP, D)
        back = jax.vmap(lambda tab, term: jnp.dot(tab.T, term, precision=HIGH))(tables, terms)
        token_grad = token_grad + (weights[:, :, None] * back).reshape(TOKENS, D)
    along = lax.optimization_barrier(jnp.mean(normed * token_grad, axis=-1, keepdims=True))
    hid_grad = energy_head[None, :] + (token_grad - normed * along) / scale
    out_grad = jnp.dot(hid_grad.astype(jnp.bfloat16), out_proj.T, preferred_element_type=jnp.float32)
    out_blk = out_grad.reshape(N_SEQ, TOK_DEV, HEADS, HEAD_DIM)
    decays, _, growths = jax.vmap(lambda b_v, s_v, i_v: chain_terms(b_v, s_v, i_v, decay_rate))(b_blk, step_blk, inner_blk)
    locals_blk = jnp.einsum('bth,btn,bthp->bhpn', growths, c_blk, out_blk, precision=HIGH)

    def backward(carry, blk):
        return (blk[1] + blk[0][:, None, None] * carry, carry)
    _, later = lax.scan(backward, start_state, (decays, locals_blk), reverse=True)

    def block_grads(inner_v, b_v, c_v, step_v, state_v, grad_v, later_v):
        _, pullback = jax.vjp(mixer, inner_v, b_v, c_v, step_v, state_v)
        return pullback((grad_v, later_v))[:4]
    g_inner, g_b, g_c, g_step = jax.vmap(block_grads)(inner_blk, b_blk, c_blk, step_blk, states_in, out_blk, later)
    g_pre = g_step.reshape(TOKENS, HEADS) * jax.nn.sigmoid(pre_step)
    g_bc = jnp.concatenate([g_b.reshape(TOKENS, STATE), g_c.reshape(TOKENS, STATE)], axis=1)
    cand_grad = hid_grad + jnp.dot(g_inner.reshape(TOKENS, HEADS * HEAD_DIM).astype(jnp.bfloat16), in_proj.T, preferred_element_type=jnp.float32)
    cand_grad = cand_grad + jnp.dot(g_bc.astype(jnp.bfloat16), bc_proj.T, preferred_element_type=jnp.float32)
    cand_grad = cand_grad + jnp.dot(g_pre.astype(jnp.bfloat16), step_proj.T, preferred_element_type=jnp.float32)
    return (candidate.astype(jnp.float32) - DESCENT * cand_grad).astype(jnp.bfloat16)
```

```python
import functools

import jax
import jax.numpy as jnp
import numpy as np
from jax import lax
from jax.experimental import pallas as pl
from jax.experimental.pallas import tpu as pltpu
from jax.sharding import Mesh
from jax.sharding import PartitionSpec as P

CAP = 24
EPS = 1e-05
DESCENT = 0.5
HIGH = lax.Precision.HIGHEST
BF = jnp.bfloat16
F32 = jnp.float32
SEQ = ("x", "z", "c")
PLANE = ("x", "z")
EXTRA = 8


def mm(a, b):
    return jnp.dot(a, b, preferred_element_type=F32)


def mm_t(a, b):
    return lax.dot_general(a, b, (((1,), (1,)), ((), ())), preferred_element_type=F32)


def t_mm(a, b):
    return lax.dot_general(a, b, (((0,), (0,)), ((), ())), preferred_element_type=F32)


def shift(value, axis, by):
    count = lax.axis_size(axis)
    return lax.ppermute(value, axis, [(i, (i + by) % count) for i in range(count)])


def lower_mask(tlen):
    rowpos = lax.broadcasted_iota(jnp.int32, (tlen, tlen), 0)
    colpos = lax.broadcasted_iota(jnp.int32, (tlen, tlen), 1)
    return rowpos >= colpos


def slot_table(ids_rows, gate_rows, expert):
    tlen = ids_rows.shape[0]
    match = ids_rows == expert
    hits = jnp.sum(match.astype(F32), axis=1)
    weight = jnp.sum(jnp.where(match, gate_rows.astype(F32), 0.0), axis=1)
    rowpos = lax.broadcasted_iota(jnp.int32, (tlen, tlen), 0)
    colpos = lax.broadcasted_iota(jnp.int32, (tlen, tlen), 1)
    places = jnp.sum(jnp.where(rowpos > colpos, hits[None, :], 0.0), axis=1)
    slot_pos = lax.broadcasted_iota(jnp.int32, (CAP, tlen), 0).astype(F32)
    table = (places[None, :] == slot_pos) & (hits[None, :] > 0.0)
    return table.astype(F32), weight


def expert_kernel(rows_ref, wg0, wg1, wu0, wu1, hv_ref, out_ref, first, second):
    half = wg0.shape[1]
    rows = rows_ref[...]
    for k, (wg, wu) in enumerate(((wg0, wu0), (wg1, wu1))):
        span = slice(k * half, (k + 1) * half)
        gate = mm(rows, wg[...])
        up = mm(rows, wu[...])
        sig = 1.0 / (1.0 + jnp.exp(-gate))
        hv = hv_ref[k : k + 1, :]
        first[:, span] = (hv * up * sig * (1.0 + gate * (1.0 - sig))).astype(BF)
        second[:, span] = (hv * gate * sig).astype(BF)
    width = rows.shape[1]
    step = min(width, 512)

    @pl.loop(0, width // step)
    def _(i):
        cols = pl.ds(pl.multiple_of(i * step, step), step)
        total = mm_t(first[:, :half], wg0[cols, :]) + mm_t(second[:, :half], wu0[cols, :])
        total += mm_t(first[:, half:], wg1[cols, :]) + mm_t(second[:, half:], wu1[cols, :])
        out_ref[:, cols] = total.astype(BF)


def expert_rows(rows, wg0, wg1, wu0, wu1, head_vec):
    count, width = rows.shape
    half = wg0.shape[1]
    return pl.pallas_call(
        expert_kernel,
        out_shape=jax.ShapeDtypeStruct((count, width), BF),
        in_specs=[pl.BlockSpec(memory_space=pltpu.VMEM)] * 6,
        out_specs=pl.BlockSpec(memory_space=pltpu.VMEM),
        scratch_shapes=[pltpu.VMEM((count, 2 * half), BF)] * 2,
        compiler_params=pltpu.CompilerParams(vmem_limit_bytes=48 << 20),
        cost_estimate=pl.CostEstimate(
            flops=16 * count * width * half,
            bytes_accessed=8 * width * half + 4 * count * width,
            transcendentals=2 * count * half,
        ),
        name="experts",
    )(rows, wg0, wg1, wu0, wu1, head_vec)


def shards(
    candidate,
    in_proj,
    bc_proj,
    step_proj,
    step_bias,
    decay_rate,
    skip_gain,
    out_proj,
    expert_ids,
    gate_weights,
    expert_gate,
    expert_up,
    expert_down,
    energy_head,
):
    tlen, width = candidate.shape
    heads = step_bias.shape[0]
    chan = in_proj.shape[1]
    size = chan // heads
    nstate = bc_proj.shape[1] // 2
    column = lax.axis_index("e")
    n_exp = lax.axis_size("e")
    n_seq = lax.axis_size(SEQ)
    n_plane = lax.axis_size(PLANE)
    col_count = width // n_exp
    slice_rows = chan // n_seq

    def spread(v):
        return jnp.repeat(v, size, axis=1)

    wg0, wu0 = expert_gate[0], expert_up[0]
    head_own = jnp.sum(expert_down[0].astype(F32) * energy_head[None, :], axis=1)
    wg1 = shift(wg0, "c", 1)
    wu1 = shift(wu0, "c", 1)
    head_other = shift(head_own[None, :], "c", 1)
    head_vec = jnp.concatenate([head_own[None, :], head_other], axis=0)

    inner_b = mm(candidate, in_proj).astype(BF)
    bc_val = mm(candidate, bc_proj)
    b_bf = bc_val[:, :nstate].astype(BF)
    c_bf = bc_val[:, nstate:].astype(BF)
    pre = mm(candidate, step_proj) + step_bias[None, :]
    step = jax.nn.softplus(pre)
    lower = lower_mask(tlen)
    cum = jnp.dot(lower.astype(F32), -step * decay_rate[None, :], precision=HIGH)
    last = cum[-1]
    growth = jnp.exp(cum)
    fade = jnp.exp(last[None, :] - cum)
    tail = fade * step
    inner = inner_b.astype(F32)
    fed = (spread(tail) * inner).astype(BF)
    fresh = t_mm(fed, b_bf).astype(BF)

    hi = lax.reduce_precision(last, 8, 7)
    mid = lax.reduce_precision(last - hi, 8, 7)
    low = last - hi - mid
    parts = jnp.stack([hi, mid, low] + [jnp.zeros_like(hi)] * (EXTRA - 3), axis=1)
    parts = jnp.repeat(parts, n_seq // heads, axis=0)[:, :, None]
    payload = jnp.concatenate(
        [
            fresh.reshape(n_seq, slice_rows, nstate),
            jnp.broadcast_to(parts, (n_seq, EXTRA, nstate)).astype(BF),
        ],
        axis=1,
    )
    got = lax.all_to_all(payload, SEQ, 0, 0, tiled=True)
    lasts = jnp.sum(got[:, slice_rows : slice_rows + 3, 0].astype(F32), axis=1)
    blk_row = lax.broadcasted_iota(jnp.int32, (n_seq, n_seq), 0)
    blk_col = lax.broadcasted_iota(jnp.int32, (n_seq, n_seq), 1)
    upto = jnp.sum(jnp.where(blk_row >= blk_col, lasts[None, :], 0.0), axis=1)
    before = jnp.sum(jnp.where(blk_row > blk_col, lasts[None, :], 0.0), axis=1)
    carry = jnp.where(
        blk_row > blk_col, jnp.exp(jnp.minimum(before[:, None] - upto[None, :], 0.0)), 0.0
    )
    entering = jnp.dot(
        carry, got[:, :slice_rows].reshape(n_seq, slice_rows * nstate).astype(F32), precision=HIGH
    )
    state = lax.all_to_all(
        entering.astype(BF).reshape(n_seq, slice_rows, nstate), SEQ, 0, 0, tiled=True
    ).reshape(chan, nstate)

    scores = mm_t(c_bf, b_bf)
    cum_t = cum.T
    weights = jnp.where(
        lower[None], jnp.exp(jnp.minimum(cum_t[:, :, None] - cum_t[:, None, :], 0.0)), 0.0
    )
    step_t = step.T
    mixing = (weights * scores[None] * step_t[:, None, :]).astype(BF)
    inner_h = inner_b.reshape(tlen, heads, size)
    within = jnp.einsum("hts,shp->thp", mixing, inner_h, preferred_element_type=F32)
    reads = mm_t(c_bf, state)
    growth_w = spread(growth)
    mixed = (
        within.reshape(tlen, chan) + growth_w * reads + spread(skip_gain[None, :]) * inner
    ).astype(BF)

    pairs = [
        slot_table(expert_ids, gate_weights, lax.rem(column + k, n_exp)) for k in range(n_exp)
    ]
    table = jnp.concatenate([p[0] for p in pairs], axis=0).astype(BF)
    own_table, own_weight = pairs[0]
    slot_weight = jnp.sum(own_table * own_weight[None, :], axis=1, keepdims=True)
    mixed_slots = mm(table, mixed).astype(BF)
    part = mm(mixed_slots, out_proj)
    mix_sum = part[:CAP]
    for k in range(1, n_exp):
        mix_sum = mix_sum + shift(part[k * CAP : (k + 1) * CAP].astype(BF), "e", k).astype(F32)
    own_rows = mm(own_table.astype(BF), candidate)
    hidden = (own_rows + mix_sum).astype(BF).astype(F32)
    scale = jnp.sqrt(jnp.mean(hidden * hidden, axis=-1, keepdims=True) + EPS)
    normed = hidden / scale
    routed = normed.astype(BF)

    rows = lax.all_to_all(
        jnp.broadcast_to(routed[None], (n_plane, CAP, width)), PLANE, 0, 0, tiled=True
    ).reshape(n_plane * CAP, width)
    terms = expert_rows(rows, wg0, wg1, wu0, wu1, head_vec)
    back = lax.all_to_all(terms.reshape(n_plane, CAP, width), PLANE, 0, 0, tiled=True)
    slot_grad = jnp.sum(back.astype(F32), axis=0)
    along = jnp.mean(normed * slot_grad, axis=-1, keepdims=True)
    slot_term = (slot_weight * (slot_grad - normed * along) / scale).astype(BF)
    all_terms = jnp.concatenate(
        [slot_term] + [shift(slot_term, "e", n_exp - k) for k in range(1, n_exp)], axis=0
    )
    hid_grad = energy_head[None, :] + t_mm(table, all_terms)
    hid_cols = lax.dynamic_slice_in_dim(hid_grad, column * col_count, col_count, 1)
    out_grad = mm_t(hid_grad.astype(BF), out_proj)
    grad_b = out_grad.astype(BF)

    grown = (growth_w * out_grad).astype(BF)
    local_grad = t_mm(grown, c_bf).astype(BF)
    got_grad = lax.all_to_all(
        local_grad.reshape(n_seq, slice_rows, nstate), SEQ, 0, 0, tiled=True
    ).reshape(n_seq, slice_rows * nstate)
    leaving = lax.dot_general(
        carry, got_grad.astype(F32), (((0,), (0,)), ((), ())), precision=HIGH
    )
    later = lax.all_to_all(
        leaving.astype(BF).reshape(n_seq, slice_rows, nstate), SEQ, 0, 0, tiled=True
    ).reshape(chan, nstate)

    def per_head(v):
        return jnp.sum(v.reshape(tlen, heads, size), axis=2)

    grad_h = grad_b.reshape(tlen, heads, size)
    d_mix = jnp.einsum("thp,shp->hts", grad_h, inner_h, preferred_element_type=F32)
    d_w = d_mix * weights
    d_scores = jnp.sum(d_w * step_t[:, None, :], axis=0).astype(BF)
    d_ws = d_w * scores[None]
    d_step_in = jnp.sum(d_ws, axis=1).T
    d_gap_rows = jnp.sum(d_ws * step_t[:, None, :], axis=2).T
    fed_back = mm_t(b_bf, later)
    g_within = jnp.einsum("hts,thp->shp", mixing, grad_h, preferred_element_type=F32)
    g_inner = (
        g_within.reshape(tlen, chan)
        + spread(skip_gain[None, :]) * out_grad
        + spread(tail) * fed_back
    ).astype(BF)
    g_c = mm(d_scores, b_bf) + mm(grown, state)
    g_b = t_mm(d_scores, c_bf) + mm(fed, later)
    d_tail = per_head(inner * fed_back)
    tail_term = d_tail * tail
    kept = jnp.sum(
        (state.astype(F32) * later.astype(F32)).reshape(heads, size * nstate), axis=1
    )
    d_last = jnp.exp(last) * kept + jnp.sum(tail_term, axis=0)
    d_cum = d_gap_rows - step * d_step_in + growth * per_head(out_grad * reads) - tail_term
    is_last = lax.broadcasted_iota(jnp.int32, (tlen, heads), 0) == tlen - 1
    d_cum = d_cum + jnp.where(is_last, d_last[None, :], 0.0)
    d_decay = lax.dot_general(
        lower.astype(F32), d_cum, (((0,), (0,)), ((), ())), precision=HIGH
    )
    g_step = d_step_in + fade * d_tail - decay_rate[None, :] * d_decay
    g_pre = (g_step * jax.nn.sigmoid(pre)).astype(BF)
    g_bc = jnp.concatenate([g_b, g_c], axis=1).astype(BF)
    partial_grad = mm_t(g_inner, in_proj) + mm_t(g_bc, bc_proj) + mm_t(g_pre, step_proj)

    def cols_of(k):
        start = lax.rem(column + k, n_exp) * col_count
        return lax.dynamic_slice_in_dim(partial_grad, start, col_count, 1)

    summed = hid_cols + cols_of(0)
    for k in range(1, n_exp):
        summed = summed + shift(cols_of(k).astype(BF), "e", k).astype(F32)
    own_cand = lax.dynamic_slice_in_dim(candidate, column * col_count, col_count, 1).astype(F32)
    return (own_cand - DESCENT * summed).astype(BF)


def solution(mesh):
    n_seq, n_exp = mesh.devices.shape
    side = int(round((n_seq // 2) ** 0.5))
    grid = Mesh(mesh.devices.reshape(side, side, 2, n_exp), ("x", "z", "c", "e"))
    in_specs = (
        P(SEQ, None),
        P(None, "e"),
        P(),
        P(None, "e"),
        P("e"),
        P("e"),
        P("e"),
        P("e", None),
        P(SEQ, None),
        P(SEQ, None),
        P("e", None, SEQ),
        P("e", None, SEQ),
        P("e", SEQ, None),
        P(),
    )
    return jax.shard_map(
        shards, mesh=grid, in_specs=in_specs, out_specs=P(SEQ, "e"), check_vma=False
    )
```

```python
import functools

import jax
import jax.numpy as jnp
import numpy as np
from jax import lax
from jax.experimental import pallas as pl
from jax.experimental.pallas import tpu as pltpu
from jax.sharding import Mesh
from jax.sharding import PartitionSpec as P

CAP = 24
EPS = 1e-05
DESCENT = 0.5
HIGH = lax.Precision.HIGHEST
BF = jnp.bfloat16
F32 = jnp.float32
SEQ = ("x", "z", "c")
PLANE = ("x", "z")
EXTRA = 16


def mm(a, b):
    return jnp.dot(a, b, preferred_element_type=F32)


def mm_t(a, b):
    return lax.dot_general(a, b, (((1,), (1,)), ((), ())), preferred_element_type=F32)


def t_mm(a, b):
    return lax.dot_general(a, b, (((0,), (0,)), ((), ())), preferred_element_type=F32)


def shift(value, axis, by):
    count = lax.axis_size(axis)
    return lax.ppermute(value, axis, [(i, (i + by) % count) for i in range(count)])


def slot_table(ids_rows, gate_rows, expert):
    tlen = ids_rows.shape[0]
    match = ids_rows == expert
    hits = jnp.sum(match.astype(F32), axis=1)
    weight = jnp.sum(jnp.where(match, gate_rows.astype(F32), 0.0), axis=1)
    rowpos = lax.broadcasted_iota(jnp.int32, (tlen, tlen), 0)
    colpos = lax.broadcasted_iota(jnp.int32, (tlen, tlen), 1)
    places = jnp.sum(jnp.where(rowpos > colpos, hits[None, :], 0.0), axis=1)
    slot_pos = lax.broadcasted_iota(jnp.int32, (CAP, tlen), 0).astype(F32)
    table = (places[None, :] == slot_pos) & (hits[None, :] > 0.0)
    return table.astype(F32), weight


def expert_kernel(rows_ref, wg0, wg1, wu0, wu1, hv_ref, out_ref, first, second):
    half = wg0.shape[1]
    rows = rows_ref[...]
    for k, (wg, wu) in enumerate(((wg0, wu0), (wg1, wu1))):
        span = slice(k * half, (k + 1) * half)
        gate = mm(rows, wg[...])
        up = mm(rows, wu[...])
        sig = 1.0 / (1.0 + jnp.exp(-gate))
        hv = hv_ref[k : k + 1, :]
        first[:, span] = (hv * up * sig * (1.0 + gate * (1.0 - sig))).astype(BF)
        second[:, span] = (hv * gate * sig).astype(BF)
    width = rows.shape[1]
    step = min(width, 512)

    @pl.loop(0, width // step)
    def _(i):
        cols = pl.ds(pl.multiple_of(i * step, step), step)
        total = mm_t(first[:, :half], wg0[cols, :]) + mm_t(second[:, :half], wu0[cols, :])
        total += mm_t(first[:, half:], wg1[cols, :]) + mm_t(second[:, half:], wu1[cols, :])
        out_ref[:, cols] = total.astype(BF)


def expert_rows(rows, wg0, wg1, wu0, wu1, head_vec):
    count, width = rows.shape
    half = wg0.shape[1]
    return pl.pallas_call(
        expert_kernel,
        out_shape=jax.ShapeDtypeStruct((count, width), BF),
        in_specs=[pl.BlockSpec(memory_space=pltpu.VMEM)] * 6,
        out_specs=pl.BlockSpec(memory_space=pltpu.VMEM),
        scratch_shapes=[pltpu.VMEM((count, 2 * half), BF)] * 2,
        compiler_params=pltpu.CompilerParams(vmem_limit_bytes=48 << 20),
        cost_estimate=pl.CostEstimate(
            flops=16 * count * width * half,
            bytes_accessed=8 * width * half + 4 * count * width,
            transcendentals=2 * count * half,
        ),
        name="experts",
    )(rows, wg0, wg1, wu0, wu1, head_vec)


def row_mask(tlen):
    rowpos = lax.broadcasted_iota(jnp.int32, (tlen, tlen), 0)
    colpos = lax.broadcasted_iota(jnp.int32, (tlen, tlen), 1)
    return rowpos >= colpos


def vmem(mib):
    return pltpu.CompilerParams(vmem_limit_bytes=mib << 20)


def whole(count):
    return [pl.BlockSpec(memory_space=pltpu.VMEM)] * count


def cost(flops, moved):
    return pl.CostEstimate(flops=flops, bytes_accessed=moved, transcendentals=0)


def proj_kernel(
    heads, slice_rows, cand, w_in, w_bc, w_step, bias, rate,
    inner_out, bc_out, pre_out, step_out, cum_out, step_t_out, cum_t_out, pay_out,
    acc, acc_bc, acc_pre,
):
    i = pl.program_id(0)

    @pl.when(i == 0)
    def _():
        acc[...] = jnp.zeros_like(acc)
        acc_bc[...] = jnp.zeros_like(acc_bc)
        acc_pre[...] = jnp.zeros_like(acc_pre)

    x = cand[...]
    acc[...] += mm(x, w_in[...])
    acc_bc[...] += mm(x, w_bc[...])
    acc_pre[:, :heads] += mm(x, w_step[...])

    @pl.when(i == pl.num_programs(0) - 1)
    def _():
        tlen, chan = acc.shape
        size = chan // heads
        nstate = acc_bc.shape[1] // 2
        pre = acc_pre[...] + bias[...]
        step = jnp.maximum(pre, 0.0) + jnp.log1p(jnp.exp(-jnp.abs(pre)))
        lower = row_mask(tlen).astype(F32)
        cum = jnp.dot(lower, -step * rate[...], precision=HIGH, preferred_element_type=F32)
        pre_out[...] = pre
        step_out[...] = step
        cum_out[...] = cum
        step_t_out[...] = step.T
        cum_t_out[...] = cum.T
        last = cum[tlen - 1 : tlen, :]
        tail = jnp.exp(last - cum) * step
        inner_b = acc[...].astype(BF)
        inner_out[...] = inner_b
        bc = acc_bc[...].astype(BF)
        bc_out[...] = bc
        b_rows = bc[:, :nstate]
        extra = pay_out.shape[1] - slice_rows
        place = lax.broadcasted_iota(jnp.int32, (extra, nstate), 0)
        per = size // slice_rows
        for h in range(heads):
            span = slice(h * size, (h + 1) * size)
            fed = (tail[:, h : h + 1] * inner_b[:, span].astype(F32)).astype(BF)
            fresh = t_mm(fed, b_rows).astype(BF)
            value = jnp.broadcast_to(last[:, h : h + 1], (extra, nstate))
            scaled = value * 65537.0
            hi = scaled - (scaled - value)
            rest = value - hi
            scaled = rest * 65537.0
            mid = scaled - (scaled - rest)
            low = rest - mid
            parts = jnp.where(place == 0, hi, jnp.where(place == 1, mid, low))
            parts = jnp.where(place < 3, parts, 0.0).astype(BF)
            for q in range(per):
                pay_out[h * per + q, :slice_rows, :] = fresh[q * slice_rows : (q + 1) * slice_rows]
                pay_out[h * per + q, slice_rows:, :] = parts


def project(candidate, in_proj, bc_proj, step_proj, bias, rate, heads, n_seq):
    tlen, width = candidate.shape
    chan = in_proj.shape[1]
    two = bc_proj.shape[1]
    slice_rows = chan // n_seq
    depth = min(width, 1024)
    small = jax.ShapeDtypeStruct((tlen, tlen), F32)
    fixed = lambda *shape: pl.BlockSpec(shape, lambda i: (0,) * len(shape))
    return pl.pallas_call(
        functools.partial(proj_kernel, heads, slice_rows),
        grid=(width // depth,),
        out_shape=(
            jax.ShapeDtypeStruct((tlen, chan), BF),
            jax.ShapeDtypeStruct((tlen, two), BF),
            small, small, small, small, small,
            jax.ShapeDtypeStruct((n_seq, slice_rows + EXTRA, two // 2), BF),
        ),
        in_specs=[
            pl.BlockSpec((tlen, depth), lambda i: (0, i)),
            pl.BlockSpec((depth, chan), lambda i: (i, 0)),
            pl.BlockSpec((depth, two), lambda i: (i, 0)),
            pl.BlockSpec((depth, heads), lambda i: (i, 0)),
            fixed(1, tlen), fixed(1, tlen),
        ],
        out_specs=(
            fixed(tlen, chan), fixed(tlen, two),
            fixed(tlen, tlen), fixed(tlen, tlen), fixed(tlen, tlen), fixed(tlen, tlen),
            fixed(tlen, tlen), fixed(n_seq, slice_rows + EXTRA, two // 2),
        ),
        scratch_shapes=[
            pltpu.VMEM((tlen, chan), F32), pltpu.VMEM((tlen, two), F32), pltpu.VMEM((tlen, tlen), F32)
        ],
        compiler_params=vmem(24),
        cost_estimate=cost(2 * tlen * width * (chan + two), 2 * width * (chan + two + 2 * tlen)),
        name="project",
    )(candidate, in_proj, bc_proj, step_proj, bias, rate)


def enter_kernel(got, out, decay):
    count, rows, nstate = out.shape
    out[0] = jnp.zeros((rows, nstate), BF)
    state = jnp.zeros((rows, nstate), F32)
    for s in range(count):
        tags = got[s, rows:, :].astype(F32)
        fade = jnp.exp(jnp.sum(tags, axis=0, keepdims=True))
        decay[s : s + 1, :] = fade
        if s < count - 1:
            state = fade * state + got[s, :rows, :].astype(F32)
            out[s + 1] = state.astype(BF)


def enter_states(got, slice_rows):
    count, _, nstate = got.shape
    return pl.pallas_call(
        enter_kernel,
        out_shape=(
            jax.ShapeDtypeStruct((count, slice_rows, nstate), BF),
            jax.ShapeDtypeStruct((count, nstate), F32),
        ),
        in_specs=whole(1),
        out_specs=tuple(whole(2)),
        compiler_params=vmem(8),
        name="enter",
    )(got)


def leave_kernel(got, decay, out):
    count, rows, nstate = out.shape
    out[count - 1] = jnp.zeros((rows, nstate), BF)
    state = jnp.zeros((rows, nstate), F32)
    for s in range(count - 1, 0, -1):
        state = decay[s : s + 1, :] * state + got[s].astype(F32)
        out[s - 1] = state.astype(BF)


def leave_states(got, decay):
    return pl.pallas_call(
        leave_kernel,
        out_shape=jax.ShapeDtypeStruct(got.shape, BF),
        in_specs=whole(2),
        out_specs=whole(1)[0],
        compiler_params=vmem(8),
        name="leave",
    )(got, decay)


def decay_weights(cum, cum_t, h):
    tlen = cum.shape[0]
    gaps = jnp.minimum(cum[:, h : h + 1] - cum_t[h : h + 1, :], 0.0)
    return jnp.where(row_mask(tlen), jnp.exp(gaps), 0.0)


def within_kernel(heads, inner_ref, bc_ref, cum_ref, cum_t_ref, step_t_ref, skip_ref, out):
    tlen, chan = out.shape
    size = chan // heads
    bc = bc_ref[...]
    nstate = bc.shape[1] // 2
    scores = mm_t(bc[:, nstate:], bc[:, :nstate])
    cum, cum_t, step_t = cum_ref[...], cum_t_ref[...], step_t_ref[...]
    for h in range(heads):
        span = slice(h * size, (h + 1) * size)
        mixing = (decay_weights(cum, cum_t, h) * scores * step_t[h : h + 1, :]).astype(BF)
        inner = inner_ref[:, span]
        out[:, span] = mm(mixing, inner) + skip_ref[:, span] * inner.astype(F32)


def mix_within(inner_b, bc_bf, cum, cum_t, step_t, skip, heads):
    tlen, chan = inner_b.shape
    return pl.pallas_call(
        functools.partial(within_kernel, heads),
        out_shape=jax.ShapeDtypeStruct((tlen, chan), F32),
        in_specs=whole(6),
        out_specs=whole(1)[0],
        compiler_params=vmem(12),
        cost_estimate=cost(2 * tlen * tlen * chan * 4, 8 * tlen * chan),
        name="mix_within",
    )(inner_b, bc_bf, cum, cum_t, step_t, skip)


def slots_kernel(
    heads, cap, within, bc_ref, cum_ref, state, table, own_table, cand, w_out,
    own_out, send1, send2, send3, reads_out, slots,
):
    @pl.when(pl.program_id(0) == 0)
    def _():
        chan = within.shape[1]
        size = chan // heads
        nstate = bc_ref.shape[1] // 2
        c_rows = bc_ref[:, nstate:]
        growth = jnp.exp(cum_ref[...])
        for h in range(heads):
            span = slice(h * size, (h + 1) * size)
            reads = mm_t(c_rows, state[span, :])
            reads_out[:, span] = reads
            mixed = (within[:, span] + growth[:, h : h + 1] * reads).astype(BF)
            slots[:, span] = mm(table[...], mixed).astype(BF)

    part = mm(slots[...], w_out[...])
    own_out[...] = part[:cap] + mm(own_table[...], cand[...])
    for k, send in enumerate((send1, send2, send3)):
        send[...] = part[(k + 1) * cap : (k + 2) * cap].astype(BF)


def mix_slots(within, bc_bf, cum, state, table, own_table, candidate, out_proj, heads):
    tlen, chan = within.shape
    width = out_proj.shape[1]
    rows = table.shape[0]
    block = min(width, 1024)
    fixed = lambda a: pl.BlockSpec(a.shape, lambda i: (0,) * a.ndim)
    cols = lambda n: pl.BlockSpec((n, block), lambda i: (0, i))
    sent = jax.ShapeDtypeStruct((CAP, width), BF)
    return pl.pallas_call(
        functools.partial(slots_kernel, heads, CAP),
        grid=(width // block,),
        out_shape=(
            jax.ShapeDtypeStruct((CAP, width), F32), sent, sent, sent,
            jax.ShapeDtypeStruct((tlen, chan), F32),
        ),
        in_specs=[fixed(a) for a in (within, bc_bf, cum, state, table, own_table)]
        + [cols(tlen), cols(chan)],
        out_specs=(cols(CAP), cols(CAP), cols(CAP), cols(CAP), fixed(within)),
        scratch_shapes=[pltpu.VMEM((rows, chan), BF)],
        compiler_params=vmem(24),
        cost_estimate=cost(2 * rows * chan * width, 2 * chan * width),
        name="mix_slots",
    )(within, bc_bf, cum, state, table, own_table, candidate, out_proj)


def outgrad_kernel(heads, table, terms, energy, w_out, bc_ref, cum_ref, hid_out, grad_out, local_out, acc):
    i = pl.program_id(0)

    @pl.when(i == 0)
    def _():
        acc[...] = jnp.zeros_like(acc)

    hid = energy[...] + t_mm(table[...], terms[...])
    hid_out[...] = hid
    acc[...] += mm_t(hid.astype(BF), w_out[...])

    @pl.when(i == pl.num_programs(0) - 1)
    def _():
        chan = acc.shape[1]
        size = chan // heads
        nstate = bc_ref.shape[1] // 2
        c_rows = bc_ref[:, nstate:]
        growth = jnp.exp(cum_ref[...])
        for h in range(heads):
            span = slice(h * size, (h + 1) * size)
            grad = acc[:, span]
            grad_out[:, span] = grad
            grown = (growth[:, h : h + 1] * grad).astype(BF)
            local_out[span, :] = t_mm(grown, c_rows).astype(BF)


def out_gradient(table, terms, energy, out_proj, bc_bf, cum, heads):
    tlen = table.shape[1]
    chan, width = out_proj.shape
    nstate = bc_bf.shape[1] // 2
    block = min(width, 1024)
    fixed = lambda *shape: pl.BlockSpec(shape, lambda i: (0,) * len(shape))
    cols = lambda n: pl.BlockSpec((n, block), lambda i: (0, i))
    return pl.pallas_call(
        functools.partial(outgrad_kernel, heads),
        grid=(width // block,),
        out_shape=(
            jax.ShapeDtypeStruct((tlen, width), F32),
            jax.ShapeDtypeStruct((tlen, chan), F32),
            jax.ShapeDtypeStruct((chan, nstate), BF),
        ),
        in_specs=[
            fixed(*table.shape), cols(terms.shape[0]), cols(1), cols(chan),
            fixed(*bc_bf.shape), fixed(*cum.shape),
        ],
        out_specs=(cols(tlen), fixed(tlen, chan), fixed(chan, nstate)),
        scratch_shapes=[pltpu.VMEM((tlen, chan), F32)],
        compiler_params=vmem(24),
        cost_estimate=cost(2 * tlen * chan * width, 2 * chan * width),
        name="out_gradient",
    )(table, terms, energy, out_proj, bc_bf, cum)


def near_kernel(
    heads, grad_ref, inner_ref, bc_ref, cum_ref, cum_t_ref, step_ref, step_t_ref, reads, state, skip_ref,
    g_out, gb_out, gc_out, dcum_out, dstep_out, rows, cols,
):
    tlen, chan = grad_ref.shape
    size = chan // heads
    nstate = bc_ref.shape[1] // 2
    b_rows, c_rows = bc_ref[:, :nstate], bc_ref[:, nstate:]
    scores = mm_t(c_rows, b_rows)
    cum, cum_t, step_t = cum_ref[...], cum_t_ref[...], step_t_ref[...]
    growth = jnp.exp(cum)
    rows[...] = jnp.zeros_like(rows)
    cols[...] = jnp.zeros_like(cols)
    d_scores = jnp.zeros((tlen, tlen), F32)
    g_c = jnp.zeros((tlen, nstate), F32)
    for h in range(heads):
        span = slice(h * size, (h + 1) * size)
        grad = grad_ref[:, span]
        grad_b = grad.astype(BF)
        inner = inner_ref[:, span]
        step_h = step_t[h : h + 1, :]
        weights = decay_weights(cum, cum_t, h)
        d_w = mm_t(grad_b, inner) * weights
        d_scores = d_scores + d_w * step_h
        d_ws = d_w * scores
        rows[h : h + 1, :] = jnp.sum(d_ws, axis=0, keepdims=True)
        grown = growth[:, h : h + 1] * grad
        cols[:, h : h + 1] = jnp.sum(d_ws * step_h, axis=1, keepdims=True) + jnp.sum(
            grown * reads[:, span], axis=1, keepdims=True
        )
        mixing = (weights * scores * step_h).astype(BF)
        g_out[:, span] = t_mm(mixing, grad_b) + skip_ref[:, span] * grad
        g_c = g_c + mm(grown.astype(BF), state[span, :])
    d_scores = d_scores.astype(BF)
    gc_out[...] = g_c + mm(d_scores, b_rows)
    gb_out[...] = t_mm(d_scores, c_rows)
    d_step = rows[...].T
    dstep_out[...] = d_step
    dcum_out[...] = cols[...] - step_ref[...] * d_step


def near_gradient(grad, inner_b, bc_bf, cum, cum_t, step, step_t, reads, state, skip, heads):
    tlen, chan = grad.shape
    small = jax.ShapeDtypeStruct((tlen, tlen), F32)
    return pl.pallas_call(
        functools.partial(near_kernel, heads),
        out_shape=(jax.ShapeDtypeStruct((tlen, chan), F32), small, small, small, small),
        in_specs=whole(10),
        out_specs=tuple(whole(5)),
        scratch_shapes=[pltpu.VMEM((tlen, tlen), F32)] * 2,
        compiler_params=vmem(16),
        cost_estimate=cost(2 * tlen * tlen * chan * 8, 20 * tlen * chan),
        name="near_gradient",
    )(grad, inner_b, bc_bf, cum, cum_t, step, step_t, reads, state, skip)


def far_kernel(
    heads, later, state, inner_ref, bc_ref, cum_ref, step_ref, pre_ref, rate, near, gb_ref, gc_ref,
    dcum_ref, dstep_ref, g_out, gbc_out, gpre_out, kept, cols,
):
    tlen, chan = near.shape
    size = chan // heads
    nstate = bc_ref.shape[1] // 2
    b_rows = bc_ref[:, :nstate]
    cum, step, pre = cum_ref[...], step_ref[...], pre_ref[...]
    last = cum[tlen - 1 : tlen, :]
    fade = jnp.exp(last - cum)
    tail = fade * step
    kept[...] = jnp.zeros_like(kept)
    cols[...] = jnp.zeros_like(cols)
    g_b = gb_ref[...]
    for h in range(heads):
        span = slice(h * size, (h + 1) * size)
        late = later[span, :]
        tail_h = tail[:, h : h + 1]
        fed_back = mm_t(b_rows, late)
        g_out[:, span] = (near[:, span] + tail_h * fed_back).astype(BF)
        inner = inner_ref[:, span].astype(F32)
        cols[:, h : h + 1] = jnp.sum(inner * fed_back, axis=1, keepdims=True)
        g_b = g_b + mm((tail_h * inner).astype(BF), late)
        kept[h : h + 1, :] = jnp.sum(
            state[span, :].astype(F32) * late.astype(F32), axis=0, keepdims=True
        )
    gbc_out[:, :nstate] = g_b.astype(BF)
    gbc_out[:, nstate:] = gc_ref[...].astype(BF)
    d_tail = cols[...]
    tail_term = d_tail * tail
    kept_row = jnp.sum(kept[...].T, axis=0, keepdims=True)
    d_last = jnp.exp(last) * kept_row + jnp.sum(tail_term, axis=0, keepdims=True)
    rowpos = lax.broadcasted_iota(jnp.int32, cum.shape, 0)
    d_cum = dcum_ref[...] - tail_term + jnp.where(rowpos == tlen - 1, d_last, 0.0)
    colpos = lax.broadcasted_iota(jnp.int32, cum.shape, 1)
    upper = (rowpos <= colpos).astype(F32)
    d_decay = jnp.dot(upper, d_cum, precision=HIGH, preferred_element_type=F32)
    g_step = dstep_ref[...] + fade * d_tail - rate[...] * d_decay
    gpre_out[...] = (g_step / (1.0 + jnp.exp(-pre))).astype(BF)


def far_gradient(later, state, inner_b, bc_bf, cum, step, pre, rate, near, gb, gc, dcum, dstep, heads):
    tlen, chan = near.shape
    return pl.pallas_call(
        functools.partial(far_kernel, heads),
        out_shape=(
            jax.ShapeDtypeStruct((tlen, chan), BF),
            jax.ShapeDtypeStruct(bc_bf.shape, BF),
            jax.ShapeDtypeStruct((tlen, tlen), BF),
        ),
        in_specs=whole(13),
        out_specs=tuple(whole(3)),
        scratch_shapes=[pltpu.VMEM((tlen, tlen), F32)] * 2,
        compiler_params=vmem(16),
        cost_estimate=cost(2 * tlen * tlen * chan * 4, 20 * tlen * chan),
        name="far_gradient",
    )(later, state, inner_b, bc_bf, cum, step, pre, rate, near, gb, gc, dcum, dstep)


def back_kernel(heads, which, g_ref, gbc, gpre, w_in, w_bc, w_step, out):
    total = mm_t(g_ref[...], w_in[...]) + mm_t(gbc[...], w_bc[...])
    total += mm_t(gpre[:, :heads], w_step[...])
    out[...] = total.astype(out.dtype)


def back_columns(which, g_inner, g_bc, g_pre, in_proj, bc_proj, step_proj, cols, dtype, heads):
    tlen, chan = g_inner.shape
    two = bc_proj.shape[1]
    block = min(cols, 512)
    per = cols // block
    fixed = lambda a: pl.BlockSpec(a.shape, lambda i, w: (0,) * a.ndim)
    rows = lambda n: pl.BlockSpec((block, n), lambda i, w: (w[0] * per + i, 0))
    return pl.pallas_call(
        functools.partial(back_kernel, heads),
        grid_spec=pltpu.PrefetchScalarGridSpec(
            num_scalar_prefetch=1,
            grid=(per,),
            in_specs=[fixed(g_inner), fixed(g_bc), fixed(g_pre), rows(chan), rows(two), rows(heads)],
            out_specs=pl.BlockSpec((tlen, block), lambda i, w: (0, i)),
        ),
        out_shape=jax.ShapeDtypeStruct((tlen, cols), dtype),
        compiler_params=vmem(12),
        cost_estimate=cost(2 * tlen * (chan + two) * cols, 2 * (chan + two) * cols),
        name="back_columns",
    )(which, g_inner, g_bc, g_pre, in_proj, bc_proj, step_proj)


def shards(
    candidate,
    in_proj,
    bc_proj,
    step_proj,
    step_bias,
    decay_rate,
    skip_gain,
    out_proj,
    expert_ids,
    gate_weights,
    expert_gate,
    expert_up,
    expert_down,
    energy_head,
):
    tlen, width = candidate.shape
    heads = step_bias.shape[0]
    chan = in_proj.shape[1]
    size = chan // heads
    nstate = bc_proj.shape[1] // 2
    column = lax.axis_index("e")
    n_exp = lax.axis_size("e")
    n_seq = lax.axis_size(SEQ)
    n_plane = lax.axis_size(PLANE)
    col_count = width // n_exp
    slice_rows = chan // n_seq
    lanes = lambda v: jnp.pad(v, (0, tlen - heads))[None, :]
    bias, rate = lanes(step_bias), lanes(decay_rate)
    skip = jnp.repeat(skip_gain, size)[None, :]
    energy = energy_head[None, :]

    wg0, wu0 = expert_gate[0], expert_up[0]
    head_own = jnp.sum(expert_down[0].astype(F32) * energy, axis=1)
    wg1 = shift(wg0, "c", 1)
    wu1 = shift(wu0, "c", 1)
    head_other = shift(head_own[None, :], "c", 1)
    head_vec = jnp.concatenate([head_own[None, :], head_other], axis=0)

    pairs = [
        slot_table(expert_ids, gate_weights, lax.rem(column + k, n_exp)) for k in range(n_exp)
    ]
    table = jnp.concatenate([p[0] for p in pairs], axis=0).astype(BF)
    own_table, own_weight = pairs[0]
    slot_weight = jnp.sum(own_table * own_weight[None, :], axis=1, keepdims=True)
    own_table = own_table.astype(BF)

    inner_b, bc_bf, pre, step, cum, step_t, cum_t, payload = project(
        candidate, in_proj, bc_proj, step_proj, bias, rate, heads, n_seq
    )
    payload, wg1, wu1, head_vec, table, own_table, slot_weight = lax.optimization_barrier(
        (payload, wg1, wu1, head_vec, table, own_table, slot_weight)
    )
    got = lax.all_to_all(payload, SEQ, 0, 0, tiled=True)
    within = mix_within(inner_b, bc_bf, cum, cum_t, step_t, skip, heads)
    entering, decay = enter_states(got, slice_rows)
    state = lax.all_to_all(entering, SEQ, 0, 0, tiled=True).reshape(chan, nstate)

    own, send1, send2, send3, reads = mix_slots(
        within, bc_bf, cum, state, table, own_table, candidate, out_proj, heads
    )
    for k, send in enumerate((send1, send2, send3)):
        own = own + shift(send, "e", k + 1).astype(F32)
    hidden = own.astype(BF).astype(F32)
    scale = jnp.sqrt(jnp.mean(hidden * hidden, axis=-1, keepdims=True) + EPS)
    normed = hidden / scale
    routed = normed.astype(BF)

    rows = lax.all_to_all(
        jnp.broadcast_to(routed[None], (n_plane, CAP, width)), PLANE, 0, 0, tiled=True
    ).reshape(n_plane * CAP, width)
    terms = expert_rows(rows, wg0, wg1, wu0, wu1, head_vec)
    back = lax.all_to_all(terms.reshape(n_plane, CAP, width), PLANE, 0, 0, tiled=True)
    slot_grad = jnp.sum(back.astype(F32), axis=0)
    along = jnp.mean(normed * slot_grad, axis=-1, keepdims=True)
    slot_term = (slot_weight * (slot_grad - normed * along) / scale).astype(BF)
    all_terms = jnp.concatenate(
        [slot_term] + [shift(slot_term, "e", n_exp - k) for k in range(1, n_exp)], axis=0
    )
    hid_grad, out_grad, local_grad = out_gradient(
        table, all_terms, energy, out_proj, bc_bf, cum, heads
    )

    got_grad = lax.all_to_all(
        local_grad.reshape(n_seq, slice_rows, nstate), SEQ, 0, 0, tiled=True
    )
    near, gb, gc, dcum, dstep = near_gradient(
        out_grad, inner_b, bc_bf, cum, cum_t, step, step_t, reads, state, skip, heads
    )
    leaving = leave_states(got_grad, decay)
    later = lax.all_to_all(leaving, SEQ, 0, 0, tiled=True).reshape(chan, nstate)
    g_inner, g_bc, g_pre = far_gradient(
        later, state, inner_b, bc_bf, cum, step, pre, rate, near, gb, gc, dcum, dstep, heads
    )

    def columns(k, dtype):
        which = lax.rem(column + k, n_exp)[None]
        return back_columns(
            which, g_inner, g_bc, g_pre, in_proj, bc_proj, step_proj, col_count, dtype, heads
        )

    arrived = [shift(columns(k, BF), "e", k) for k in (2, 1, 3)]
    summed = lax.dynamic_slice_in_dim(hid_grad, column * col_count, col_count, 1) + columns(0, F32)
    for value in arrived:
        summed = summed + value.astype(F32)
    own_cand = lax.dynamic_slice_in_dim(candidate, column * col_count, col_count, 1).astype(F32)
    return (own_cand - DESCENT * summed).astype(BF)


def solution(mesh):
    n_seq, n_exp = mesh.devices.shape
    side = int(round((n_seq // 2) ** 0.5))
    grid = Mesh(mesh.devices.reshape(side, side, 2, n_exp), ("x", "z", "c", "e"))
    in_specs = (
        P(SEQ, None),
        P(None, "e"),
        P(),
        P(None, "e"),
        P("e"),
        P("e"),
        P("e"),
        P("e", None),
        P(SEQ, None),
        P(SEQ, None),
        P("e", None, SEQ),
        P("e", None, SEQ),
        P("e", SEQ, None),
        P(),
    )
    return jax.shard_map(
        shards, mesh=grid, in_specs=in_specs, out_specs=P(SEQ, "e"), check_vma=False
    )
```

```python
import functools

import jax
import jax.numpy as jnp
import numpy as np
from jax import lax
from jax.experimental import pallas as pl
from jax.experimental.pallas import tpu as pltpu
from jax.sharding import Mesh
from jax.sharding import PartitionSpec as P

CAP = 24
EPS = 1e-05
DESCENT = 0.5
HIGH = lax.Precision.HIGHEST
BF = jnp.bfloat16
F32 = jnp.float32
SEQ = ("x", "z", "c")
EXTRA = 16


def mm(a, b):
    return jnp.dot(a, b, preferred_element_type=F32)


def mm_t(a, b):
    return lax.dot_general(a, b, (((1,), (1,)), ((), ())), preferred_element_type=F32)


def t_mm(a, b):
    return lax.dot_general(a, b, (((0,), (0,)), ((), ())), preferred_element_type=F32)


def shift(value, axis, by):
    count = lax.axis_size(axis)
    return lax.ppermute(value, axis, [(i, (i + by) % count) for i in range(count)])


def slot_table(ids_rows, gate_rows, expert):
    tlen = ids_rows.shape[0]
    match = ids_rows == expert
    hits = jnp.sum(match.astype(F32), axis=1)
    weight = jnp.sum(jnp.where(match, gate_rows.astype(F32), 0.0), axis=1)
    rowpos = lax.broadcasted_iota(jnp.int32, (tlen, tlen), 0)
    colpos = lax.broadcasted_iota(jnp.int32, (tlen, tlen), 1)
    places = jnp.sum(jnp.where(rowpos > colpos, hits[None, :], 0.0), axis=1)
    slot_pos = lax.broadcasted_iota(jnp.int32, (CAP, tlen), 0).astype(F32)
    table = (places[None, :] == slot_pos) & (hits[None, :] > 0.0)
    return table.astype(F32), weight


def swap_blocks(value, side, rows):
    return jnp.concatenate(
        [
            value[(b * side + a) * rows : (b * side + a + 1) * rows]
            for a in range(side)
            for b in range(side)
        ],
        axis=0,
    )


def expert_kernel(side, *refs):
    near, far = refs[:side], refs[side : 2 * side]
    wg0, wg1, wu0, wu1, hv_ref = refs[2 * side : 2 * side + 5]
    out_near, out_far, first, second = refs[2 * side + 5 :]
    half = wg0.shape[1]
    depth = out_near.shape[1]
    slot = out_near.shape[0] // (side * side)
    near_rows = jnp.concatenate([r[...] for r in near], axis=0)
    far_rows = jnp.concatenate([r[...] for r in far], axis=0)

    def product(w):
        return mm(near_rows, w[:depth, :]) + swap_blocks(mm(far_rows, w[depth:, :]), side, slot)

    for k, (wg, wu) in enumerate(((wg0, wu0), (wg1, wu1))):
        span = slice(k * half, (k + 1) * half)
        gate = product(wg)
        up = product(wu)
        sig = 1.0 / (1.0 + jnp.exp(-gate))
        hv = hv_ref[k : k + 1, :]
        first[:, span] = (hv * up * sig * (1.0 + gate * (1.0 - sig))).astype(BF)
        second[:, span] = (hv * gate * sig).astype(BF)
    step = min(depth, 512)

    def terms(cols):
        total = mm_t(first[:, :half], wg0[cols, :]) + mm_t(second[:, :half], wu0[cols, :])
        return total + mm_t(first[:, half:], wg1[cols, :]) + mm_t(second[:, half:], wu1[cols, :])

    @pl.loop(0, depth // step)
    def _(i):
        start = pl.multiple_of(i * step, step)
        cols = pl.ds(start, step)
        out_near[:, cols] = terms(cols).astype(BF)
        more = pl.ds(pl.multiple_of(depth + start, step), step)
        out_far[:, cols] = swap_blocks(terms(more), side, slot).astype(BF)


def expert_rows(near, far, wg0, wg1, wu0, wu1, head_vec):
    side = len(near)
    count = side * near[0].shape[0]
    depth = near[0].shape[1]
    half = wg0.shape[1]
    out = jax.ShapeDtypeStruct((count, depth), BF)
    return single(
        functools.partial(expert_kernel, side),
        out_shape=(out, out),
        args=(*near, *far, wg0, wg1, wu0, wu1, head_vec),
        scratch_shapes=[pltpu.VMEM((count, 2 * half), BF)] * 2,
        compiler_params=vmem(56),
        cost_estimate=cost(32 * count * depth * half, 16 * depth * half + 8 * count * depth),
        name="experts",
    )


def gather_around(value, axis):
    count = lax.axis_size(axis)
    if count != 4:
        return [value] + [shift(value, axis, count - k) for k in range(1, count)]
    left, right = shift(value, axis, 1), shift(value, axis, 3)
    cut = value.shape[0] // 2
    across = jnp.concatenate(
        [shift(left[:cut], axis, 1), shift(right[cut:], axis, 3)], axis=0
    )
    return [value, right, across, left]


def gather_direct(value, axis):
    count = lax.axis_size(axis)
    return [value] + [shift(value, axis, count - k) for k in range(1, count)]


def scatter_direct(pieces, axis):
    total = pieces[0].astype(F32)
    for k in range(1, len(pieces)):
        total = total + shift(pieces[k], axis, k).astype(F32)
    return total


def scatter_around(pieces, axis):
    if len(pieces) != 4:
        return scatter_direct(pieces, axis)
    own, right, across, left = pieces
    cut = across.shape[0] // 2
    top = shift(across[:cut], axis, 1)
    bottom = shift(across[cut:], axis, 3)
    right = jnp.concatenate(
        [(right[:cut].astype(F32) + top.astype(F32)).astype(BF), right[cut:]], axis=0
    )
    left = jnp.concatenate(
        [left[:cut], (left[cut:].astype(F32) + bottom.astype(F32)).astype(BF)], axis=0
    )
    return own.astype(F32) + shift(right, axis, 1).astype(F32) + shift(left, axis, 3).astype(F32)


def split_rows(value, count):
    rows = value.shape[0] // count
    return [value[k * rows : (k + 1) * rows] for k in range(count)]


def row_mask(tlen):
    rowpos = lax.broadcasted_iota(jnp.int32, (tlen, tlen), 0)
    colpos = lax.broadcasted_iota(jnp.int32, (tlen, tlen), 1)
    return rowpos >= colpos


def vmem(mib):
    return pltpu.CompilerParams(vmem_limit_bytes=mib << 20)


def whole(arrays):
    return [pl.BlockSpec(a.shape, lambda i, n=len(a.shape): (0,) * n) for a in arrays]


def single(kernel, out_shape, args, **options):
    outs = whole(out_shape) if isinstance(out_shape, tuple) else whole((out_shape,))[0]
    return pl.pallas_call(
        kernel,
        grid=(1,),
        out_shape=out_shape,
        in_specs=whole(args),
        out_specs=tuple(outs) if isinstance(outs, list) else outs,
        **options,
    )(*args)


def cost(flops, moved):
    return pl.CostEstimate(flops=flops, bytes_accessed=moved, transcendentals=0)


def proj_kernel(
    heads, slice_rows, cand, w_in, w_bc, w_step, bias, rate,
    inner_out, bc_out, pre_out, step_out, cum_out, step_t_out, cum_t_out, pay_out,
    acc, acc_bc, acc_pre,
):
    i = pl.program_id(0)

    @pl.when(i == 0)
    def _():
        acc[...] = jnp.zeros_like(acc)
        acc_bc[...] = jnp.zeros_like(acc_bc)
        acc_pre[...] = jnp.zeros_like(acc_pre)

    x = cand[...]
    acc[...] += mm(x, w_in[...])
    acc_bc[...] += mm(x, w_bc[...])
    acc_pre[:, :heads] += mm(x, w_step[...])

    @pl.when(i == pl.num_programs(0) - 1)
    def _():
        tlen, chan = acc.shape
        size = chan // heads
        nstate = acc_bc.shape[1] // 2
        pre = acc_pre[...] + bias[...]
        step = jnp.maximum(pre, 0.0) + jnp.log1p(jnp.exp(-jnp.abs(pre)))
        lower = row_mask(tlen).astype(F32)
        cum = jnp.dot(lower, -step * rate[...], precision=HIGH, preferred_element_type=F32)
        pre_out[...] = pre
        step_out[...] = step
        cum_out[...] = cum
        step_t_out[...] = step.T
        cum_t_out[...] = cum.T
        last = cum[tlen - 1 : tlen, :]
        tail = jnp.exp(last - cum) * step
        inner_b = acc[...].astype(BF)
        inner_out[...] = inner_b
        bc = acc_bc[...].astype(BF)
        bc_out[...] = bc
        b_rows = bc[:, :nstate]
        extra = pay_out.shape[1] - slice_rows
        place = lax.broadcasted_iota(jnp.int32, (extra, nstate), 0)
        per = size // slice_rows
        for h in range(heads):
            span = slice(h * size, (h + 1) * size)
            fed = (tail[:, h : h + 1] * inner_b[:, span].astype(F32)).astype(BF)
            fresh = t_mm(fed, b_rows).astype(BF)
            value = jnp.broadcast_to(last[:, h : h + 1], (extra, nstate))
            scaled = value * 65537.0
            hi = scaled - (scaled - value)
            rest = value - hi
            scaled = rest * 65537.0
            mid = scaled - (scaled - rest)
            low = rest - mid
            parts = jnp.where(place == 0, hi, jnp.where(place == 1, mid, low))
            parts = jnp.where(place < 3, parts, 0.0).astype(BF)
            for q in range(per):
                pay_out[h * per + q, :slice_rows, :] = fresh[q * slice_rows : (q + 1) * slice_rows]
                pay_out[h * per + q, slice_rows:, :] = parts


def project(candidate, in_proj, bc_proj, step_proj, bias, rate, heads, n_seq):
    tlen, width = candidate.shape
    chan = in_proj.shape[1]
    two = bc_proj.shape[1]
    slice_rows = chan // n_seq
    depth = min(width, 1024)
    small = jax.ShapeDtypeStruct((tlen, tlen), F32)
    fixed = lambda *shape: pl.BlockSpec(shape, lambda i: (0,) * len(shape))
    return pl.pallas_call(
        functools.partial(proj_kernel, heads, slice_rows),
        grid=(width // depth,),
        out_shape=(
            jax.ShapeDtypeStruct((tlen, chan), BF),
            jax.ShapeDtypeStruct((tlen, two), BF),
            small, small, small, small, small,
            jax.ShapeDtypeStruct((n_seq, slice_rows + EXTRA, two // 2), BF),
        ),
        in_specs=[
            pl.BlockSpec((tlen, depth), lambda i: (0, i)),
            pl.BlockSpec((depth, chan), lambda i: (i, 0)),
            pl.BlockSpec((depth, two), lambda i: (i, 0)),
            pl.BlockSpec((depth, heads), lambda i: (i, 0)),
            fixed(1, tlen), fixed(1, tlen),
        ],
        out_specs=(
            fixed(tlen, chan), fixed(tlen, two),
            fixed(tlen, tlen), fixed(tlen, tlen), fixed(tlen, tlen), fixed(tlen, tlen),
            fixed(tlen, tlen), fixed(n_seq, slice_rows + EXTRA, two // 2),
        ),
        scratch_shapes=[
            pltpu.VMEM((tlen, chan), F32), pltpu.VMEM((tlen, two), F32), pltpu.VMEM((tlen, tlen), F32)
        ],
        compiler_params=vmem(56),
        cost_estimate=cost(2 * tlen * width * (chan + two), 2 * width * (chan + two + 2 * tlen)),
        name="project",
    )(candidate, in_proj, bc_proj, step_proj, bias, rate)


def enter_kernel(got, out, decay):
    count, rows, nstate = out.shape
    out[0] = jnp.zeros((rows, nstate), BF)
    state = jnp.zeros((rows, nstate), F32)
    for s in range(count):
        tags = got[s, rows:, :].astype(F32)
        fade = jnp.exp(jnp.sum(tags, axis=0, keepdims=True))
        decay[s : s + 1, :] = fade
        if s < count - 1:
            state = fade * state + got[s, :rows, :].astype(F32)
            out[s + 1] = state.astype(BF)


def enter_states(got, slice_rows):
    count, _, nstate = got.shape
    return single(
        enter_kernel,
        out_shape=(
            jax.ShapeDtypeStruct((count, slice_rows, nstate), BF),
            jax.ShapeDtypeStruct((count, nstate), F32),
        ),
        args=(got,),
        compiler_params=vmem(56),
        name="enter",
    )


def leave_kernel(got, decay, out):
    count, rows, nstate = out.shape
    out[count - 1] = jnp.zeros((rows, nstate), BF)
    state = jnp.zeros((rows, nstate), F32)
    for s in range(count - 1, 0, -1):
        state = decay[s : s + 1, :] * state + got[s].astype(F32)
        out[s - 1] = state.astype(BF)


def leave_states(got, decay):
    return single(
        leave_kernel,
        out_shape=jax.ShapeDtypeStruct(got.shape, BF),
        args=(got, decay,),
        compiler_params=vmem(56),
        name="leave",
    )


def decay_weights(cum, cum_t, h):
    tlen = cum.shape[0]
    gaps = jnp.minimum(cum[:, h : h + 1] - cum_t[h : h + 1, :], 0.0)
    return jnp.where(row_mask(tlen), jnp.exp(gaps), 0.0)


def within_kernel(heads, inner_ref, bc_ref, cum_ref, cum_t_ref, step_t_ref, skip_ref, out):
    tlen, chan = out.shape
    size = chan // heads
    bc = bc_ref[...]
    nstate = bc.shape[1] // 2
    scores = mm_t(bc[:, nstate:], bc[:, :nstate])
    cum, cum_t, step_t = cum_ref[...], cum_t_ref[...], step_t_ref[...]
    for h in range(heads):
        span = slice(h * size, (h + 1) * size)
        mixing = (decay_weights(cum, cum_t, h) * scores * step_t[h : h + 1, :]).astype(BF)
        inner = inner_ref[:, span]
        out[:, span] = mm(mixing, inner) + skip_ref[:, span] * inner.astype(F32)


def mix_within(inner_b, bc_bf, cum, cum_t, step_t, skip, heads):
    tlen, chan = inner_b.shape
    return single(
        functools.partial(within_kernel, heads),
        out_shape=jax.ShapeDtypeStruct((tlen, chan), F32),
        args=(inner_b, bc_bf, cum, cum_t, step_t, skip,),
        compiler_params=vmem(56),
        cost_estimate=cost(2 * tlen * tlen * chan * 4, 8 * tlen * chan),
        name="mix_within",
    )


def slots_kernel(
    heads, cap, within, bc_ref, cum_ref, state, table, own_table, cand, w_out,
    own_out, send1, send2, send3, reads_out, slots,
):
    @pl.when(pl.program_id(0) == 0)
    def _():
        chan = within.shape[1]
        size = chan // heads
        nstate = bc_ref.shape[1] // 2
        c_rows = bc_ref[:, nstate:]
        growth = jnp.exp(cum_ref[...])
        for h in range(heads):
            span = slice(h * size, (h + 1) * size)
            reads = mm_t(c_rows, state[span, :])
            reads_out[:, span] = reads
            mixed = (within[:, span] + growth[:, h : h + 1] * reads).astype(BF)
            slots[:, span] = mm(table[...], mixed).astype(BF)

    part = mm(slots[...], w_out[...])
    own_out[...] = part[:cap] + mm(own_table[...], cand[...])
    for k, send in enumerate((send1, send2, send3)):
        send[...] = part[(k + 1) * cap : (k + 2) * cap].astype(BF)


def mix_slots(within, bc_bf, cum, state, table, own_table, candidate, out_proj, heads):
    tlen, chan = within.shape
    width = out_proj.shape[1]
    rows = table.shape[0]
    block = min(width, 1024)
    fixed = lambda a: pl.BlockSpec(a.shape, lambda i: (0,) * a.ndim)
    cols = lambda n: pl.BlockSpec((n, block), lambda i: (0, i))
    sent = jax.ShapeDtypeStruct((CAP, width), BF)
    return pl.pallas_call(
        functools.partial(slots_kernel, heads, CAP),
        grid=(width // block,),
        out_shape=(
            jax.ShapeDtypeStruct((CAP, width), F32), sent, sent, sent,
            jax.ShapeDtypeStruct((tlen, chan), F32),
        ),
        in_specs=[fixed(a) for a in (within, bc_bf, cum, state, table, own_table)]
        + [cols(tlen), cols(chan)],
        out_specs=(cols(CAP), cols(CAP), cols(CAP), cols(CAP), fixed(within)),
        scratch_shapes=[pltpu.VMEM((rows, chan), BF)],
        compiler_params=vmem(56),
        cost_estimate=cost(2 * rows * chan * width, 2 * chan * width),
        name="mix_slots",
    )(within, bc_bf, cum, state, table, own_table, candidate, out_proj)


def outgrad_kernel(heads, table, terms, energy, w_out, bc_ref, cum_ref, hid_out, grad_out, local_out, acc):
    i = pl.program_id(0)

    @pl.when(i == 0)
    def _():
        acc[...] = jnp.zeros_like(acc)

    hid = energy[...] + t_mm(table[...], terms[...])
    hid_out[...] = hid
    acc[...] += mm_t(hid.astype(BF), w_out[...])

    @pl.when(i == pl.num_programs(0) - 1)
    def _():
        chan = acc.shape[1]
        size = chan // heads
        nstate = bc_ref.shape[1] // 2
        c_rows = bc_ref[:, nstate:]
        growth = jnp.exp(cum_ref[...])
        for h in range(heads):
            span = slice(h * size, (h + 1) * size)
            grad = acc[:, span]
            grad_out[:, span] = grad
            grown = (growth[:, h : h + 1] * grad).astype(BF)
            local_out[span, :] = t_mm(grown, c_rows).astype(BF)


def out_gradient(table, terms, energy, out_proj, bc_bf, cum, heads):
    tlen = table.shape[1]
    chan, width = out_proj.shape
    nstate = bc_bf.shape[1] // 2
    block = min(width, 1024)
    fixed = lambda *shape: pl.BlockSpec(shape, lambda i: (0,) * len(shape))
    cols = lambda n: pl.BlockSpec((n, block), lambda i: (0, i))
    return pl.pallas_call(
        functools.partial(outgrad_kernel, heads),
        grid=(width // block,),
        out_shape=(
            jax.ShapeDtypeStruct((tlen, width), F32),
            jax.ShapeDtypeStruct((tlen, chan), F32),
            jax.ShapeDtypeStruct((chan, nstate), BF),
        ),
        in_specs=[
            fixed(*table.shape), cols(terms.shape[0]), cols(1), cols(chan),
            fixed(*bc_bf.shape), fixed(*cum.shape),
        ],
        out_specs=(cols(tlen), fixed(tlen, chan), fixed(chan, nstate)),
        scratch_shapes=[pltpu.VMEM((tlen, chan), F32)],
        compiler_params=vmem(56),
        cost_estimate=cost(2 * tlen * chan * width, 2 * chan * width),
        name="out_gradient",
    )(table, terms, energy, out_proj, bc_bf, cum)


def near_kernel(
    heads, grad_ref, inner_ref, bc_ref, cum_ref, cum_t_ref, step_ref, step_t_ref, reads, state, skip_ref,
    g_out, gb_out, gc_out, dcum_out, dstep_out, rows, cols,
):
    tlen, chan = grad_ref.shape
    size = chan // heads
    nstate = bc_ref.shape[1] // 2
    b_rows, c_rows = bc_ref[:, :nstate], bc_ref[:, nstate:]
    scores = mm_t(c_rows, b_rows)
    cum, cum_t, step_t = cum_ref[...], cum_t_ref[...], step_t_ref[...]
    growth = jnp.exp(cum)
    rows[...] = jnp.zeros_like(rows)
    cols[...] = jnp.zeros_like(cols)
    d_scores = jnp.zeros((tlen, tlen), F32)
    g_c = jnp.zeros((tlen, nstate), F32)
    for h in range(heads):
        span = slice(h * size, (h + 1) * size)
        grad = grad_ref[:, span]
        grad_b = grad.astype(BF)
        inner = inner_ref[:, span]
        step_h = step_t[h : h + 1, :]
        weights = decay_weights(cum, cum_t, h)
        d_w = mm_t(grad_b, inner) * weights
        d_scores = d_scores + d_w * step_h
        d_ws = d_w * scores
        rows[h : h + 1, :] = jnp.sum(d_ws, axis=0, keepdims=True)
        grown = growth[:, h : h + 1] * grad
        cols[:, h : h + 1] = jnp.sum(d_ws * step_h, axis=1, keepdims=True) + jnp.sum(
            grown * reads[:, span], axis=1, keepdims=True
        )
        mixing = (weights * scores * step_h).astype(BF)
        g_out[:, span] = t_mm(mixing, grad_b) + skip_ref[:, span] * grad
        g_c = g_c + mm(grown.astype(BF), state[span, :])
    d_scores = d_scores.astype(BF)
    gc_out[...] = g_c + mm(d_scores, b_rows)
    gb_out[...] = t_mm(d_scores, c_rows)
    d_step = rows[...].T
    dstep_out[...] = d_step
    dcum_out[...] = cols[...] - step_ref[...] * d_step


def near_gradient(grad, inner_b, bc_bf, cum, cum_t, step, step_t, reads, state, skip, heads):
    tlen, chan = grad.shape
    small = jax.ShapeDtypeStruct((tlen, tlen), F32)
    return single(
        functools.partial(near_kernel, heads),
        out_shape=(jax.ShapeDtypeStruct((tlen, chan), F32), small, small, small, small),
        args=(grad, inner_b, bc_bf, cum, cum_t, step, step_t, reads, state, skip,),
        scratch_shapes=[pltpu.VMEM((tlen, tlen), F32)] * 2,
        compiler_params=vmem(56),
        cost_estimate=cost(2 * tlen * tlen * chan * 8, 20 * tlen * chan),
        name="near_gradient",
    )


def far_kernel(
    heads, later, state, inner_ref, bc_ref, cum_ref, step_ref, pre_ref, rate, near, gb_ref, gc_ref,
    dcum_ref, dstep_ref, g_out, gbc_out, gpre_out, kept, cols,
):
    tlen, chan = near.shape
    size = chan // heads
    nstate = bc_ref.shape[1] // 2
    b_rows = bc_ref[:, :nstate]
    cum, step, pre = cum_ref[...], step_ref[...], pre_ref[...]
    last = cum[tlen - 1 : tlen, :]
    fade = jnp.exp(last - cum)
    tail = fade * step
    kept[...] = jnp.zeros_like(kept)
    cols[...] = jnp.zeros_like(cols)
    g_b = gb_ref[...]
    for h in range(heads):
        span = slice(h * size, (h + 1) * size)
        late = later[span, :]
        tail_h = tail[:, h : h + 1]
        fed_back = mm_t(b_rows, late)
        g_out[:, span] = (near[:, span] + tail_h * fed_back).astype(BF)
        inner = inner_ref[:, span].astype(F32)
        cols[:, h : h + 1] = jnp.sum(inner * fed_back, axis=1, keepdims=True)
        g_b = g_b + mm((tail_h * inner).astype(BF), late)
        kept[h : h + 1, :] = jnp.sum(
            state[span, :].astype(F32) * late.astype(F32), axis=0, keepdims=True
        )
    gbc_out[:, :nstate] = g_b.astype(BF)
    gbc_out[:, nstate:] = gc_ref[...].astype(BF)
    d_tail = cols[...]
    tail_term = d_tail * tail
    kept_row = jnp.sum(kept[...].T, axis=0, keepdims=True)
    d_last = jnp.exp(last) * kept_row + jnp.sum(tail_term, axis=0, keepdims=True)
    rowpos = lax.broadcasted_iota(jnp.int32, cum.shape, 0)
    d_cum = dcum_ref[...] - tail_term + jnp.where(rowpos == tlen - 1, d_last, 0.0)
    colpos = lax.broadcasted_iota(jnp.int32, cum.shape, 1)
    upper = (rowpos <= colpos).astype(F32)
    d_decay = jnp.dot(upper, d_cum, precision=HIGH, preferred_element_type=F32)
    g_step = dstep_ref[...] + fade * d_tail - rate[...] * d_decay
    gpre_out[...] = (g_step / (1.0 + jnp.exp(-pre))).astype(BF)


def far_gradient(later, state, inner_b, bc_bf, cum, step, pre, rate, near, gb, gc, dcum, dstep, heads):
    tlen, chan = near.shape
    return single(
        functools.partial(far_kernel, heads),
        out_shape=(
            jax.ShapeDtypeStruct((tlen, chan), BF),
            jax.ShapeDtypeStruct(bc_bf.shape, BF),
            jax.ShapeDtypeStruct((tlen, tlen), BF),
        ),
        args=(later, state, inner_b, bc_bf, cum, step, pre, rate, near, gb, gc, dcum, dstep,),
        scratch_shapes=[pltpu.VMEM((tlen, tlen), F32)] * 2,
        compiler_params=vmem(56),
        cost_estimate=cost(2 * tlen * tlen * chan * 4, 20 * tlen * chan),
        name="far_gradient",
    )


def back_kernel(heads, which, g_ref, gbc, gpre, w_in, w_bc, w_step, out):
    total = mm_t(g_ref[...], w_in[...]) + mm_t(gbc[...], w_bc[...])
    total += mm_t(gpre[:, :heads], w_step[...])
    out[...] = total.astype(out.dtype)


def back_columns(which, g_inner, g_bc, g_pre, in_proj, bc_proj, step_proj, cols, dtype, heads):
    tlen, chan = g_inner.shape
    two = bc_proj.shape[1]
    block = min(cols, 512)
    per = cols // block
    fixed = lambda a: pl.BlockSpec(a.shape, lambda i, w: (0,) * a.ndim)
    rows = lambda n: pl.BlockSpec((block, n), lambda i, w: (w[0] * per + i, 0))
    return pl.pallas_call(
        functools.partial(back_kernel, heads),
        grid_spec=pltpu.PrefetchScalarGridSpec(
            num_scalar_prefetch=1,
            grid=(per,),
            in_specs=[fixed(g_inner), fixed(g_bc), fixed(g_pre), rows(chan), rows(two), rows(heads)],
            out_specs=pl.BlockSpec((tlen, block), lambda i, w: (0, i)),
        ),
        out_shape=jax.ShapeDtypeStruct((tlen, cols), dtype),
        compiler_params=vmem(56),
        cost_estimate=cost(2 * tlen * (chan + two) * cols, 2 * (chan + two) * cols),
        name="back_columns",
    )(which, g_inner, g_bc, g_pre, in_proj, bc_proj, step_proj)


def shards(
    candidate,
    in_proj,
    bc_proj,
    step_proj,
    step_bias,
    decay_rate,
    skip_gain,
    out_proj,
    expert_ids,
    gate_weights,
    expert_gate,
    expert_up,
    expert_down,
    energy_head,
):
    tlen, width = candidate.shape
    heads = step_bias.shape[0]
    chan = in_proj.shape[1]
    size = chan // heads
    nstate = bc_proj.shape[1] // 2
    column = lax.axis_index("e")
    n_exp = lax.axis_size("e")
    n_seq = lax.axis_size(SEQ)
    col_count = width // n_exp
    slice_rows = chan // n_seq
    lanes = lambda v: jnp.pad(v, (0, tlen - heads))[None, :]
    bias, rate = lanes(step_bias), lanes(decay_rate)
    skip = jnp.repeat(skip_gain, size)[None, :]
    energy = energy_head[None, :]

    wg0, wu0 = expert_gate[0], expert_up[0]
    head_own = jnp.sum(expert_down[0].astype(F32) * energy, axis=1)
    wg1 = shift(wg0, "c", 1)
    wu1 = shift(wu0, "c", 1)
    head_other = shift(head_own[None, :], "c", 1)
    head_vec = jnp.concatenate([head_own[None, :], head_other], axis=0)

    pairs = [
        slot_table(expert_ids, gate_weights, lax.rem(column + k, n_exp)) for k in range(n_exp)
    ]
    table = jnp.concatenate([p[0] for p in pairs], axis=0).astype(BF)
    own_table, own_weight = pairs[0]
    slot_weight = jnp.sum(own_table * own_weight[None, :], axis=1, keepdims=True)
    own_table = own_table.astype(BF)

    inner_b, bc_bf, pre, step, cum, step_t, cum_t, payload = project(
        candidate, in_proj, bc_proj, step_proj, bias, rate, heads, n_seq
    )
    payload, wg1, wu1, head_vec, table, own_table, slot_weight = lax.optimization_barrier(
        (payload, wg1, wu1, head_vec, table, own_table, slot_weight)
    )
    got = lax.all_to_all(payload, SEQ, 0, 0, tiled=True)
    within = mix_within(inner_b, bc_bf, cum, cum_t, step_t, skip, heads)
    entering, decay = enter_states(got, slice_rows)
    state = lax.all_to_all(entering, SEQ, 0, 0, tiled=True).reshape(chan, nstate)

    own, send1, send2, send3, reads = mix_slots(
        within, bc_bf, cum, state, table, own_table, candidate, out_proj, heads
    )
    for k, send in enumerate((send1, send2, send3)):
        own = own + shift(send, "e", k + 1).astype(F32)
    hidden = own.astype(BF).astype(F32)
    scale = jnp.sqrt(jnp.mean(hidden * hidden, axis=-1, keepdims=True) + EPS)
    normed = hidden / scale
    routed = normed.astype(BF)

    side = lax.axis_size("x")
    cut = width // 2
    near_own = jnp.concatenate(gather_direct(routed[:, :cut], "z"), axis=0)
    far_own = jnp.concatenate(gather_direct(routed[:, cut:], "x"), axis=0)
    near_rows = gather_around(near_own, "x")
    far_rows = gather_around(far_own, "z")
    out_near, out_far = expert_rows(near_rows, far_rows, wg0, wg1, wu0, wu1, head_vec)
    near_sum = scatter_around(split_rows(out_near, side), "x").astype(BF)
    far_sum = scatter_around(split_rows(out_far, side), "z").astype(BF)
    slot_grad = jnp.concatenate(
        [
            scatter_direct(split_rows(near_sum, side), "z"),
            scatter_direct(split_rows(far_sum, side), "x"),
        ],
        axis=1,
    )
    along = jnp.mean(normed * slot_grad, axis=-1, keepdims=True)
    slot_term = (slot_weight * (slot_grad - normed * along) / scale).astype(BF)
    all_terms = jnp.concatenate(
        [slot_term] + [shift(slot_term, "e", n_exp - k) for k in range(1, n_exp)], axis=0
    )
    hid_grad, out_grad, local_grad = out_gradient(
        table, all_terms, energy, out_proj, bc_bf, cum, heads
    )

    got_grad = lax.all_to_all(
        local_grad.reshape(n_seq, slice_rows, nstate), SEQ, 0, 0, tiled=True
    )
    near, gb, gc, dcum, dstep = near_gradient(
        out_grad, inner_b, bc_bf, cum, cum_t, step, step_t, reads, state, skip, heads
    )
    leaving = leave_states(got_grad, decay)
    later = lax.all_to_all(leaving, SEQ, 0, 0, tiled=True).reshape(chan, nstate)
    g_inner, g_bc, g_pre = far_gradient(
        later, state, inner_b, bc_bf, cum, step, pre, rate, near, gb, gc, dcum, dstep, heads
    )

    def columns(k, dtype):
        which = lax.rem(column + k, n_exp)[None]
        return back_columns(
            which, g_inner, g_bc, g_pre, in_proj, bc_proj, step_proj, col_count, dtype, heads
        )

    arrived = [shift(columns(k, BF), "e", k) for k in (2, 1, 3)]
    summed = lax.dynamic_slice_in_dim(hid_grad, column * col_count, col_count, 1) + columns(0, F32)
    for value in arrived:
        summed = summed + value.astype(F32)
    own_cand = lax.dynamic_slice_in_dim(candidate, column * col_count, col_count, 1).astype(F32)
    return (own_cand - DESCENT * summed).astype(BF)


def solution(mesh):
    n_seq, n_exp = mesh.devices.shape
    side = int(round((n_seq // 2) ** 0.5))
    grid = Mesh(mesh.devices.reshape(side, side, 2, n_exp), ("x", "z", "c", "e"))
    in_specs = (
        P(SEQ, None),
        P(None, "e"),
        P(),
        P(None, "e"),
        P("e"),
        P("e"),
        P("e"),
        P("e", None),
        P(SEQ, None),
        P(SEQ, None),
        P("e", None, SEQ),
        P("e", None, SEQ),
        P("e", SEQ, None),
        P(),
    )
    return jax.shard_map(
        shards, mesh=grid, in_specs=in_specs, out_specs=P(SEQ, "e"), check_vma=False
    )
```

```python
import functools

import jax
import jax.numpy as jnp
import numpy as np
from jax import lax
from jax.experimental import pallas as pl
from jax.experimental.pallas import tpu as pltpu
from jax.sharding import Mesh
from jax.sharding import PartitionSpec as P

CAP = 24
EPS = 1e-05
DESCENT = 0.5
HIGH = lax.Precision.HIGHEST
BF = jnp.bfloat16
F32 = jnp.float32
SEQ = ("x", "z", "c")
EXTRA = 16


def mm(a, b):
    return jnp.dot(a, b, preferred_element_type=F32)


def mm_t(a, b):
    return lax.dot_general(a, b, (((1,), (1,)), ((), ())), preferred_element_type=F32)


def t_mm(a, b):
    return lax.dot_general(a, b, (((0,), (0,)), ((), ())), preferred_element_type=F32)


def shift(value, axis, by):
    count = lax.axis_size(axis)
    return lax.ppermute(value, axis, [(i, (i + by) % count) for i in range(count)])


def slot_table(ids_rows, gate_rows, expert):
    tlen = ids_rows.shape[0]
    match = ids_rows == expert
    hits = jnp.sum(match.astype(F32), axis=1)
    weight = jnp.sum(jnp.where(match, gate_rows.astype(F32), 0.0), axis=1)
    rowpos = lax.broadcasted_iota(jnp.int32, (tlen, tlen), 0)
    colpos = lax.broadcasted_iota(jnp.int32, (tlen, tlen), 1)
    places = jnp.sum(jnp.where(rowpos > colpos, hits[None, :], 0.0), axis=1)
    slot_pos = lax.broadcasted_iota(jnp.int32, (CAP, tlen), 0).astype(F32)
    table = (places[None, :] == slot_pos) & (hits[None, :] > 0.0)
    return table.astype(F32), weight


def expert_kernel(pieces, *refs):
    wg0, wg1, wu0, wu1, hv_ref, out, first, second = refs[pieces:]
    half = wg0.shape[1]
    width = out.shape[1]
    rows = jnp.concatenate([r[...] for r in refs[:pieces]], axis=0)
    for k, (wg, wu) in enumerate(((wg0, wu0), (wg1, wu1))):
        span = slice(k * half, (k + 1) * half)
        gate = mm(rows, wg[...])
        up = mm(rows, wu[...])
        sig = 1.0 / (1.0 + jnp.exp(-gate))
        hv = hv_ref[k : k + 1, :]
        first[:, span] = (hv * up * sig * (1.0 + gate * (1.0 - sig))).astype(BF)
        second[:, span] = (hv * gate * sig).astype(BF)
    step = min(width, 512)

    @pl.loop(0, width // step)
    def _(i):
        cols = pl.ds(pl.multiple_of(i * step, step), step)
        total = mm_t(first[:, :half], wg0[cols, :]) + mm_t(second[:, :half], wu0[cols, :])
        total += mm_t(first[:, half:], wg1[cols, :]) + mm_t(second[:, half:], wu1[cols, :])
        out[:, cols] = total.astype(BF)


def expert_rows(rows, wg0, wg1, wu0, wu1, head_vec):
    count = len(rows) * rows[0].shape[0]
    width = rows[0].shape[1]
    half = wg0.shape[1]
    return single(
        functools.partial(expert_kernel, len(rows)),
        out_shape=jax.ShapeDtypeStruct((count, width), BF),
        args=(*rows, wg0, wg1, wu0, wu1, head_vec),
        scratch_shapes=[pltpu.VMEM((count, 2 * half), BF)] * 2,
        compiler_params=vmem(56),
        cost_estimate=cost(16 * count * width * half, 8 * width * half + 4 * count * width),
        name="experts",
    )


def turn(value, outer, by):
    side = lax.axis_size("x")
    cores = lax.axis_size("c")
    pairs = []
    for x in range(side):
        for z in range(side):
            for c in range(cores):
                along_x = (c == 0) == outer
                to_x = (x + by) % side if along_x else x
                to_z = z if along_x else (z + by) % side
                pairs.append(((x * side + z) * cores + c, (to_x * side + to_z) * cores + c))
    return lax.ppermute(value, SEQ, pairs)


def gather_outer(value, count):
    if count != 4:
        return [value] + [turn(value, True, count - k) for k in range(1, count)]
    left, right = turn(value, True, 1), turn(value, True, 3)
    cut = value.shape[0] // 2
    across = jnp.concatenate([turn(left[:cut], True, 1), turn(right[cut:], True, 3)], axis=0)
    return [value, right, across, left]


def gather_inner(value, count):
    return [value] + [turn(value, False, count - k) for k in range(1, count)]


def scatter_direct(pieces, outer):
    total = pieces[0].astype(F32)
    for k in range(1, len(pieces)):
        total = total + turn(pieces[k], outer, k).astype(F32)
    return total


def scatter_outer(pieces):
    if len(pieces) != 4:
        return scatter_direct(pieces, True)
    own, right, across, left = pieces
    cut = across.shape[0] // 2
    top = turn(across[:cut], True, 1)
    bottom = turn(across[cut:], True, 3)
    right = jnp.concatenate(
        [(right[:cut].astype(F32) + top.astype(F32)).astype(BF), right[cut:]], axis=0
    )
    left = jnp.concatenate(
        [left[:cut], (left[cut:].astype(F32) + bottom.astype(F32)).astype(BF)], axis=0
    )
    return own.astype(F32) + turn(right, True, 1).astype(F32) + turn(left, True, 3).astype(F32)


def split_rows(value, count):
    rows = value.shape[0] // count
    return [value[k * rows : (k + 1) * rows] for k in range(count)]


def row_mask(tlen):
    rowpos = lax.broadcasted_iota(jnp.int32, (tlen, tlen), 0)
    colpos = lax.broadcasted_iota(jnp.int32, (tlen, tlen), 1)
    return rowpos >= colpos


def vmem(mib):
    return pltpu.CompilerParams(vmem_limit_bytes=mib << 20)


def whole(arrays):
    return [pl.BlockSpec(a.shape, lambda i, n=len(a.shape): (0,) * n) for a in arrays]


def single(kernel, out_shape, args, **options):
    outs = whole(out_shape) if isinstance(out_shape, tuple) else whole((out_shape,))[0]
    return pl.pallas_call(
        kernel,
        grid=(1,),
        out_shape=out_shape,
        in_specs=whole(args),
        out_specs=tuple(outs) if isinstance(outs, list) else outs,
        **options,
    )(*args)


def cost(flops, moved):
    return pl.CostEstimate(flops=flops, bytes_accessed=moved, transcendentals=0)


def proj_kernel(
    heads, slice_rows, cand, w_in, w_bc, w_step, bias, rate,
    inner_out, bc_out, pre_out, step_out, cum_out, step_t_out, cum_t_out, pay_out,
    acc, acc_bc, acc_pre,
):
    i = pl.program_id(0)

    @pl.when(i == 0)
    def _():
        acc[...] = jnp.zeros_like(acc)
        acc_bc[...] = jnp.zeros_like(acc_bc)
        acc_pre[...] = jnp.zeros_like(acc_pre)

    x = cand[...]
    acc[...] += mm(x, w_in[...])
    acc_bc[...] += mm(x, w_bc[...])
    acc_pre[:, :heads] += mm_t(x, w_step[...])

    @pl.when(i == pl.num_programs(0) - 1)
    def _():
        tlen, chan = acc.shape
        size = chan // heads
        nstate = acc_bc.shape[1] // 2
        pre = acc_pre[...] + bias[...]
        step = jnp.maximum(pre, 0.0) + jnp.log1p(jnp.exp(-jnp.abs(pre)))
        lower = row_mask(tlen).astype(F32)
        cum = jnp.dot(lower, -step * rate[...], precision=HIGH, preferred_element_type=F32)
        pre_out[...] = pre
        step_out[...] = step
        cum_out[...] = cum
        step_t_out[...] = step.T
        cum_t_out[...] = cum.T
        last = cum[tlen - 1 : tlen, :]
        tail = jnp.exp(last - cum) * step
        inner_b = acc[...].astype(BF)
        inner_out[...] = inner_b
        bc = acc_bc[...].astype(BF)
        bc_out[...] = bc
        b_rows = bc[:, :nstate]
        extra = pay_out.shape[1] - slice_rows
        place = lax.broadcasted_iota(jnp.int32, (extra, nstate), 0)
        per = size // slice_rows
        for h in range(heads):
            span = slice(h * size, (h + 1) * size)
            fed = (tail[:, h : h + 1] * inner_b[:, span].astype(F32)).astype(BF)
            fresh = t_mm(fed, b_rows).astype(BF)
            value = jnp.broadcast_to(last[:, h : h + 1], (extra, nstate))
            scaled = value * 65537.0
            hi = scaled - (scaled - value)
            rest = value - hi
            scaled = rest * 65537.0
            mid = scaled - (scaled - rest)
            low = rest - mid
            parts = jnp.where(place == 0, hi, jnp.where(place == 1, mid, low))
            parts = jnp.where(place < 3, parts, 0.0).astype(BF)
            for q in range(per):
                pay_out[h * per + q, :slice_rows, :] = fresh[q * slice_rows : (q + 1) * slice_rows]
                pay_out[h * per + q, slice_rows:, :] = parts


def project(candidate, in_proj, bc_proj, step_proj, bias, rate, heads, n_seq):
    tlen, width = candidate.shape
    chan = in_proj.shape[1]
    two = bc_proj.shape[1]
    slice_rows = chan // n_seq
    depth = min(width, 512)
    small = jax.ShapeDtypeStruct((tlen, tlen), F32)
    fixed = lambda *shape: pl.BlockSpec(shape, lambda i: (0,) * len(shape))
    return pl.pallas_call(
        functools.partial(proj_kernel, heads, slice_rows),
        grid=(width // depth,),
        out_shape=(
            jax.ShapeDtypeStruct((tlen, chan), BF),
            jax.ShapeDtypeStruct((tlen, two), BF),
            small, small, small, small, small,
            jax.ShapeDtypeStruct((n_seq, slice_rows + EXTRA, two // 2), BF),
        ),
        in_specs=[
            pl.BlockSpec((tlen, depth), lambda i: (0, i)),
            pl.BlockSpec((depth, chan), lambda i: (i, 0)),
            pl.BlockSpec((depth, two), lambda i: (i, 0)),
            pl.BlockSpec((heads, depth), lambda i: (0, i)),
            fixed(1, tlen), fixed(1, tlen),
        ],
        out_specs=(
            fixed(tlen, chan), fixed(tlen, two),
            fixed(tlen, tlen), fixed(tlen, tlen), fixed(tlen, tlen), fixed(tlen, tlen),
            fixed(tlen, tlen), fixed(n_seq, slice_rows + EXTRA, two // 2),
        ),
        scratch_shapes=[
            pltpu.VMEM((tlen, chan), F32), pltpu.VMEM((tlen, two), F32), pltpu.VMEM((tlen, tlen), F32)
        ],
        compiler_params=vmem(56),
        cost_estimate=cost(2 * tlen * width * (chan + two), 2 * width * (chan + two + 2 * tlen)),
        name="project",
    )(candidate, in_proj, bc_proj, step_proj, bias, rate)


def enter_kernel(got, out, decay):
    count, rows, nstate = out.shape
    out[0] = jnp.zeros((rows, nstate), BF)
    state = jnp.zeros((rows, nstate), F32)
    for s in range(count):
        tags = got[s, rows:, :].astype(F32)
        fade = jnp.exp(jnp.sum(tags, axis=0, keepdims=True))
        decay[s : s + 1, :] = fade
        if s < count - 1:
            state = fade * state + got[s, :rows, :].astype(F32)
            out[s + 1] = state.astype(BF)


def enter_states(got, slice_rows):
    count, _, nstate = got.shape
    return single(
        enter_kernel,
        out_shape=(
            jax.ShapeDtypeStruct((count, slice_rows, nstate), BF),
            jax.ShapeDtypeStruct((count, nstate), F32),
        ),
        args=(got,),
        compiler_params=vmem(56),
        name="enter",
    )


def leave_kernel(got, decay, out):
    count, rows, nstate = out.shape
    out[count - 1] = jnp.zeros((rows, nstate), BF)
    state = jnp.zeros((rows, nstate), F32)
    for s in range(count - 1, 0, -1):
        state = decay[s : s + 1, :] * state + got[s].astype(F32)
        out[s - 1] = state.astype(BF)


def leave_states(got, decay):
    return single(
        leave_kernel,
        out_shape=jax.ShapeDtypeStruct(got.shape, BF),
        args=(got, decay,),
        compiler_params=vmem(56),
        name="leave",
    )


def decay_weights(cum, cum_t, h):
    tlen = cum.shape[0]
    gaps = jnp.minimum(cum[:, h : h + 1] - cum_t[h : h + 1, :], 0.0)
    return jnp.where(row_mask(tlen), jnp.exp(gaps), 0.0)


def within_kernel(heads, inner_ref, bc_ref, cum_ref, cum_t_ref, step_t_ref, skip_ref, out):
    tlen, chan = out.shape
    size = chan // heads
    bc = bc_ref[...]
    nstate = bc.shape[1] // 2
    scores = mm_t(bc[:, nstate:], bc[:, :nstate])
    cum, cum_t, step_t = cum_ref[...], cum_t_ref[...], step_t_ref[...]
    for h in range(heads):
        span = slice(h * size, (h + 1) * size)
        mixing = (decay_weights(cum, cum_t, h) * scores * step_t[h : h + 1, :]).astype(BF)
        inner = inner_ref[:, span]
        out[:, span] = mm(mixing, inner) + skip_ref[:, span] * inner.astype(F32)


def mix_within(inner_b, bc_bf, cum, cum_t, step_t, skip, heads):
    tlen, chan = inner_b.shape
    return single(
        functools.partial(within_kernel, heads),
        out_shape=jax.ShapeDtypeStruct((tlen, chan), F32),
        args=(inner_b, bc_bf, cum, cum_t, step_t, skip,),
        compiler_params=vmem(56),
        cost_estimate=cost(2 * tlen * tlen * chan * 4, 8 * tlen * chan),
        name="mix_within",
    )


def slots_kernel(
    heads, cap, within, bc_ref, cum_ref, state, table, own_table, cand, w_out,
    own_out, send1, send2, send3, reads_out, slots,
):
    @pl.when(pl.program_id(0) == 0)
    def _():
        chan = within.shape[1]
        size = chan // heads
        nstate = bc_ref.shape[1] // 2
        c_rows = bc_ref[:, nstate:]
        growth = jnp.exp(cum_ref[...])
        for h in range(heads):
            span = slice(h * size, (h + 1) * size)
            reads = mm_t(c_rows, state[span, :])
            reads_out[:, span] = reads
            mixed = (within[:, span] + growth[:, h : h + 1] * reads).astype(BF)
            slots[:, span] = mm(table[...], mixed).astype(BF)

    part = mm(slots[...], w_out[...])
    own_out[...] = part[:cap] + mm(own_table[...], cand[...])
    for k, send in enumerate((send1, send2, send3)):
        send[...] = part[(k + 1) * cap : (k + 2) * cap].astype(BF)


def mix_slots(within, bc_bf, cum, state, table, own_table, candidate, out_proj, heads):
    tlen, chan = within.shape
    width = out_proj.shape[1]
    rows = table.shape[0]
    block = min(width, 512)
    fixed = lambda a: pl.BlockSpec(a.shape, lambda i: (0,) * a.ndim)
    cols = lambda n: pl.BlockSpec((n, block), lambda i: (0, i))
    sent = jax.ShapeDtypeStruct((CAP, width), BF)
    return pl.pallas_call(
        functools.partial(slots_kernel, heads, CAP),
        grid=(width // block,),
        out_shape=(
            jax.ShapeDtypeStruct((CAP, width), F32), sent, sent, sent,
            jax.ShapeDtypeStruct((tlen, chan), F32),
        ),
        in_specs=[fixed(a) for a in (within, bc_bf, cum, state, table, own_table)]
        + [cols(tlen), cols(chan)],
        out_specs=(cols(CAP), cols(CAP), cols(CAP), cols(CAP), fixed(within)),
        scratch_shapes=[pltpu.VMEM((rows, chan), BF)],
        compiler_params=vmem(56),
        cost_estimate=cost(2 * rows * chan * width, 2 * chan * width),
        name="mix_slots",
    )(within, bc_bf, cum, state, table, own_table, candidate, out_proj)


def outgrad_kernel(heads, table, terms, energy, w_out, bc_ref, cum_ref, hid_out, grad_out, local_out, acc):
    i = pl.program_id(0)

    @pl.when(i == 0)
    def _():
        acc[...] = jnp.zeros_like(acc)

    hid = energy[...] + t_mm(table[...], terms[...])
    hid_out[...] = hid
    acc[...] += mm_t(hid.astype(BF), w_out[...])

    @pl.when(i == pl.num_programs(0) - 1)
    def _():
        chan = acc.shape[1]
        size = chan // heads
        nstate = bc_ref.shape[1] // 2
        c_rows = bc_ref[:, nstate:]
        growth = jnp.exp(cum_ref[...])
        for h in range(heads):
            span = slice(h * size, (h + 1) * size)
            grad = acc[:, span]
            grad_out[:, span] = grad
            grown = (growth[:, h : h + 1] * grad).astype(BF)
            local_out[span, :] = t_mm(grown, c_rows).astype(BF)


def out_gradient(table, terms, energy, out_proj, bc_bf, cum, heads):
    tlen = table.shape[1]
    chan, width = out_proj.shape
    nstate = bc_bf.shape[1] // 2
    block = min(width, 512)
    fixed = lambda *shape: pl.BlockSpec(shape, lambda i: (0,) * len(shape))
    cols = lambda n: pl.BlockSpec((n, block), lambda i: (0, i))
    return pl.pallas_call(
        functools.partial(outgrad_kernel, heads),
        grid=(width // block,),
        out_shape=(
            jax.ShapeDtypeStruct((tlen, width), F32),
            jax.ShapeDtypeStruct((tlen, chan), F32),
            jax.ShapeDtypeStruct((chan, nstate), BF),
        ),
        in_specs=[
            fixed(*table.shape), cols(terms.shape[0]), cols(1), cols(chan),
            fixed(*bc_bf.shape), fixed(*cum.shape),
        ],
        out_specs=(cols(tlen), fixed(tlen, chan), fixed(chan, nstate)),
        scratch_shapes=[pltpu.VMEM((tlen, chan), F32)],
        compiler_params=vmem(56),
        cost_estimate=cost(2 * tlen * chan * width, 2 * chan * width),
        name="out_gradient",
    )(table, terms, energy, out_proj, bc_bf, cum)


def near_kernel(
    heads, grad_ref, inner_ref, bc_ref, cum_ref, cum_t_ref, step_ref, step_t_ref, reads, state, skip_ref,
    g_out, gb_out, gc_out, dcum_out, dstep_out, rows, cols,
):
    tlen, chan = grad_ref.shape
    size = chan // heads
    nstate = bc_ref.shape[1] // 2
    b_rows, c_rows = bc_ref[:, :nstate], bc_ref[:, nstate:]
    scores = mm_t(c_rows, b_rows)
    cum, cum_t, step_t = cum_ref[...], cum_t_ref[...], step_t_ref[...]
    growth = jnp.exp(cum)
    rows[...] = jnp.zeros_like(rows)
    cols[...] = jnp.zeros_like(cols)
    d_scores = jnp.zeros((tlen, tlen), F32)
    g_c = jnp.zeros((tlen, nstate), F32)
    for h in range(heads):
        span = slice(h * size, (h + 1) * size)
        grad = grad_ref[:, span]
        grad_b = grad.astype(BF)
        inner = inner_ref[:, span]
        step_h = step_t[h : h + 1, :]
        weights = decay_weights(cum, cum_t, h)
        d_w = mm_t(grad_b, inner) * weights
        d_scores = d_scores + d_w * step_h
        d_ws = d_w * scores
        rows[h : h + 1, :] = jnp.sum(d_ws, axis=0, keepdims=True)
        grown = growth[:, h : h + 1] * grad
        cols[:, h : h + 1] = jnp.sum(d_ws * step_h, axis=1, keepdims=True) + jnp.sum(
            grown * reads[:, span], axis=1, keepdims=True
        )
        mixing = (weights * scores * step_h).astype(BF)
        g_out[:, span] = t_mm(mixing, grad_b) + skip_ref[:, span] * grad
        g_c = g_c + mm(grown.astype(BF), state[span, :])
    d_scores = d_scores.astype(BF)
    gc_out[...] = g_c + mm(d_scores, b_rows)
    gb_out[...] = t_mm(d_scores, c_rows)
    d_step = rows[...].T
    dstep_out[...] = d_step
    dcum_out[...] = cols[...] - step_ref[...] * d_step


def near_gradient(grad, inner_b, bc_bf, cum, cum_t, step, step_t, reads, state, skip, heads):
    tlen, chan = grad.shape
    small = jax.ShapeDtypeStruct((tlen, tlen), F32)
    return single(
        functools.partial(near_kernel, heads),
        out_shape=(jax.ShapeDtypeStruct((tlen, chan), F32), small, small, small, small),
        args=(grad, inner_b, bc_bf, cum, cum_t, step, step_t, reads, state, skip,),
        scratch_shapes=[pltpu.VMEM((tlen, tlen), F32)] * 2,
        compiler_params=vmem(56),
        cost_estimate=cost(2 * tlen * tlen * chan * 8, 20 * tlen * chan),
        name="near_gradient",
    )


def far_kernel(
    heads, later, state, inner_ref, bc_ref, cum_ref, step_ref, pre_ref, rate, near, gb_ref, gc_ref,
    dcum_ref, dstep_ref, g_out, gbc_out, gpre_out, kept, cols,
):
    tlen, chan = near.shape
    size = chan // heads
    nstate = bc_ref.shape[1] // 2
    b_rows = bc_ref[:, :nstate]
    cum, step, pre = cum_ref[...], step_ref[...], pre_ref[...]
    last = cum[tlen - 1 : tlen, :]
    fade = jnp.exp(last - cum)
    tail = fade * step
    kept[...] = jnp.zeros_like(kept)
    cols[...] = jnp.zeros_like(cols)
    g_b = gb_ref[...]
    for h in range(heads):
        span = slice(h * size, (h + 1) * size)
        late = later[span, :]
        tail_h = tail[:, h : h + 1]
        fed_back = mm_t(b_rows, late)
        g_out[:, span] = (near[:, span] + tail_h * fed_back).astype(BF)
        inner = inner_ref[:, span].astype(F32)
        cols[:, h : h + 1] = jnp.sum(inner * fed_back, axis=1, keepdims=True)
        g_b = g_b + mm((tail_h * inner).astype(BF), late)
        kept[h : h + 1, :] = jnp.sum(
            state[span, :].astype(F32) * late.astype(F32), axis=0, keepdims=True
        )
    gbc_out[:, :nstate] = g_b.astype(BF)
    gbc_out[:, nstate:] = gc_ref[...].astype(BF)
    d_tail = cols[...]
    tail_term = d_tail * tail
    kept_row = jnp.sum(kept[...].T, axis=0, keepdims=True)
    d_last = jnp.exp(last) * kept_row + jnp.sum(tail_term, axis=0, keepdims=True)
    rowpos = lax.broadcasted_iota(jnp.int32, cum.shape, 0)
    d_cum = dcum_ref[...] - tail_term + jnp.where(rowpos == tlen - 1, d_last, 0.0)
    colpos = lax.broadcasted_iota(jnp.int32, cum.shape, 1)
    upper = (rowpos <= colpos).astype(F32)
    d_decay = jnp.dot(upper, d_cum, precision=HIGH, preferred_element_type=F32)
    g_step = dstep_ref[...] + fade * d_tail - rate[...] * d_decay
    gpre_out[...] = (g_step / (1.0 + jnp.exp(-pre))).astype(BF)


def far_gradient(later, state, inner_b, bc_bf, cum, step, pre, rate, near, gb, gc, dcum, dstep, heads):
    tlen, chan = near.shape
    return single(
        functools.partial(far_kernel, heads),
        out_shape=(
            jax.ShapeDtypeStruct((tlen, chan), BF),
            jax.ShapeDtypeStruct(bc_bf.shape, BF),
            jax.ShapeDtypeStruct((tlen, tlen), BF),
        ),
        args=(later, state, inner_b, bc_bf, cum, step, pre, rate, near, gb, gc, dcum, dstep,),
        scratch_shapes=[pltpu.VMEM((tlen, tlen), F32)] * 2,
        compiler_params=vmem(56),
        cost_estimate=cost(2 * tlen * tlen * chan * 4, 20 * tlen * chan),
        name="far_gradient",
    )


def back_kernel(heads, per, which, g_ref, gbc, gpre, w_in, w_bc, w_step, *outs):
    total = mm_t(g_ref[...], w_in[...]) + mm_t(gbc[...], w_bc[...])
    total += mm(gpre[:, :heads], w_step[...])
    for k, out in enumerate(outs):

        @pl.when(pl.program_id(0) // per == k)
        def _():
            out[...] = total.astype(out.dtype)


def back_columns(which, g_inner, g_bc, g_pre, in_proj, bc_proj, step_w, cols, dtype, heads):
    tlen, chan = g_inner.shape
    two = bc_proj.shape[1]
    count = which.shape[0]
    block = min(cols, 512)
    per = cols // block
    fixed = lambda a: pl.BlockSpec(a.shape, lambda i, w: (0,) * a.ndim)
    place = lambda i, w: w[i // per] * per + i % per
    rows = lambda n: pl.BlockSpec((block, n), lambda i, w: (place(i, w), 0))
    return pl.pallas_call(
        functools.partial(back_kernel, heads, per),
        grid_spec=pltpu.PrefetchScalarGridSpec(
            num_scalar_prefetch=1,
            grid=(count * per,),
            in_specs=[
                fixed(g_inner), fixed(g_bc), fixed(g_pre), rows(chan), rows(two),
                pl.BlockSpec((heads, block), lambda i, w: (0, place(i, w))),
            ],
            out_specs=tuple(
                pl.BlockSpec((tlen, block), lambda i, w, k=k: (0, jnp.clip(i - k * per, 0, per - 1)))
                for k in range(count)
            ),
        ),
        out_shape=tuple(jax.ShapeDtypeStruct((tlen, cols), dtype) for _ in range(count)),
        compiler_params=vmem(56),
        cost_estimate=cost(2 * tlen * (chan + two) * cols * count, 2 * (chan + two) * cols * count),
        name="back_columns",
    )(which, g_inner, g_bc, g_pre, in_proj, bc_proj, step_w)


def shards(
    candidate,
    in_proj,
    bc_proj,
    step_proj,
    step_bias,
    decay_rate,
    skip_gain,
    out_proj,
    expert_ids,
    gate_weights,
    expert_gate,
    expert_up,
    expert_down,
    energy_head,
):
    tlen, width = candidate.shape
    heads = step_bias.shape[0]
    step_w = step_proj.T
    chan = in_proj.shape[1]
    size = chan // heads
    nstate = bc_proj.shape[1] // 2
    column = lax.axis_index("e")
    n_exp = lax.axis_size("e")
    n_seq = lax.axis_size(SEQ)
    col_count = width // n_exp
    slice_rows = chan // n_seq
    lanes = lambda v: jnp.pad(v, (0, tlen - heads))[None, :]
    bias, rate = lanes(step_bias), lanes(decay_rate)
    skip = jnp.repeat(skip_gain, size)[None, :]
    energy = energy_head[None, :]

    wg0, wu0 = expert_gate[0], expert_up[0]
    wg1 = shift(wg0, "c", 1)
    wu1 = shift(wu0, "c", 1)

    pairs = [
        slot_table(expert_ids, gate_weights, lax.rem(column + k, n_exp)) for k in range(n_exp)
    ]
    table = jnp.concatenate([p[0] for p in pairs], axis=0).astype(BF)
    own_table, own_weight = pairs[0]
    slot_weight = jnp.sum(own_table * own_weight[None, :], axis=1, keepdims=True)
    own_table = own_table.astype(BF)

    inner_b, bc_bf, pre, step, cum, step_t, cum_t, payload = project(
        candidate, in_proj, bc_proj, step_w, bias, rate, heads, n_seq
    )
    payload, wg1, wu1, table, own_table, slot_weight = lax.optimization_barrier(
        (payload, wg1, wu1, table, own_table, slot_weight)
    )
    got = lax.all_to_all(payload, SEQ, 0, 0, tiled=True)
    within = mix_within(inner_b, bc_bf, cum, cum_t, step_t, skip, heads)
    entering, decay = enter_states(got, slice_rows)
    entering, down = lax.optimization_barrier((entering, expert_down[0]))
    head_own = jnp.sum(down.astype(F32) * energy, axis=1)
    head_other = shift(head_own[None, :], "c", 1)
    head_vec = jnp.concatenate([head_own[None, :], head_other], axis=0)
    state = lax.all_to_all(entering, SEQ, 0, 0, tiled=True).reshape(chan, nstate)

    own, send1, send2, send3, reads = mix_slots(
        within, bc_bf, cum, state, table, own_table, candidate, out_proj, heads
    )
    for k, send in enumerate((send1, send2, send3)):
        own = own + shift(send, "e", k + 1).astype(F32)
    hidden = own.astype(BF).astype(F32)
    scale = jnp.sqrt(jnp.mean(hidden * hidden, axis=-1, keepdims=True) + EPS)
    normed = hidden / scale
    routed = normed.astype(BF)

    side = lax.axis_size("x")
    rows = gather_outer(jnp.concatenate(gather_inner(routed, side), axis=0), side)
    terms = expert_rows(rows, wg0, wg1, wu0, wu1, head_vec)
    line_sum = scatter_outer(split_rows(terms, side)).astype(BF)
    slot_grad = scatter_direct(split_rows(line_sum, side), False)
    along = jnp.mean(normed * slot_grad, axis=-1, keepdims=True)
    slot_term = (slot_weight * (slot_grad - normed * along) / scale).astype(BF)
    all_terms = jnp.concatenate(
        [slot_term] + [shift(slot_term, "e", n_exp - k) for k in range(1, n_exp)], axis=0
    )
    hid_grad, out_grad, local_grad = out_gradient(
        table, all_terms, energy, out_proj, bc_bf, cum, heads
    )

    got_grad = lax.all_to_all(
        local_grad.reshape(n_seq, slice_rows, nstate), SEQ, 0, 0, tiled=True
    )
    near, gb, gc, dcum, dstep = near_gradient(
        out_grad, inner_b, bc_bf, cum, cum_t, step, step_t, reads, state, skip, heads
    )
    leaving = leave_states(got_grad, decay)
    later = lax.all_to_all(leaving, SEQ, 0, 0, tiled=True).reshape(chan, nstate)
    g_inner, g_bc, g_pre = far_gradient(
        later, state, inner_b, bc_bf, cum, step, pre, rate, near, gb, gc, dcum, dstep, heads
    )

    def columns(places, dtype):
        which = jnp.stack([lax.rem(column + k, n_exp) for k in places])
        return back_columns(
            which, g_inner, g_bc, g_pre, in_proj, bc_proj, step_w, col_count, dtype, heads
        )

    order = (2, 1, 3)
    arrived = [shift(part, "e", k) for k, part in zip(order, columns(order, BF))]
    (own_part,) = columns((0,), F32)
    summed = lax.dynamic_slice_in_dim(hid_grad, column * col_count, col_count, 1) + own_part
    for value in arrived:
        summed = summed + value.astype(F32)
    own_cand = lax.dynamic_slice_in_dim(candidate, column * col_count, col_count, 1).astype(F32)
    return (own_cand - DESCENT * summed).astype(BF)


def solution(mesh):
    n_seq, n_exp = mesh.devices.shape
    side = int(round((n_seq // 2) ** 0.5))
    grid = Mesh(mesh.devices.reshape(side, side, 2, n_exp), ("x", "z", "c", "e"))
    in_specs = (
        P(SEQ, None),
        P(None, "e"),
        P(),
        P(None, "e"),
        P("e"),
        P("e"),
        P("e"),
        P("e", None),
        P(SEQ, None),
        P(SEQ, None),
        P("e", None, SEQ),
        P("e", None, SEQ),
        P("e", SEQ, None),
        P(),
    )
    return jax.shard_map(
        shards, mesh=grid, in_specs=in_specs, out_specs=P(SEQ, "e"), check_vma=False
    )
```

```python
import functools

import jax
import jax.numpy as jnp
import numpy as np
from jax import lax
from jax.experimental import pallas as pl
from jax.experimental.pallas import tpu as pltpu
from jax.sharding import Mesh
from jax.sharding import PartitionSpec as P

CAP = 24
EPS = 1e-05
DESCENT = 0.5
HIGH = lax.Precision.HIGHEST
BF = jnp.bfloat16
F32 = jnp.float32
SEQ = ("x", "z", "c")
EXTRA = 16


def mm(a, b):
    return jnp.dot(a, b, preferred_element_type=F32)


def mm_t(a, b):
    return lax.dot_general(a, b, (((1,), (1,)), ((), ())), preferred_element_type=F32)


def t_mm(a, b):
    return lax.dot_general(a, b, (((0,), (0,)), ((), ())), preferred_element_type=F32)


def shift(value, axis, by):
    count = lax.axis_size(axis)
    return lax.ppermute(value, axis, [(i, (i + by) % count) for i in range(count)])


def slot_table(ids_rows, gate_rows, expert):
    tlen = ids_rows.shape[0]
    match = ids_rows == expert
    hits = jnp.sum(match.astype(F32), axis=1)
    weight = jnp.sum(jnp.where(match, gate_rows.astype(F32), 0.0), axis=1)
    rowpos = lax.broadcasted_iota(jnp.int32, (tlen, tlen), 0)
    colpos = lax.broadcasted_iota(jnp.int32, (tlen, tlen), 1)
    places = jnp.sum(jnp.where(rowpos > colpos, hits[None, :], 0.0), axis=1)
    slot_pos = lax.broadcasted_iota(jnp.int32, (CAP, tlen), 0).astype(F32)
    table = (places[None, :] == slot_pos) & (hits[None, :] > 0.0)
    return table.astype(F32), weight


def swap_blocks(value, side, rows):
    return jnp.concatenate(
        [
            value[(b * side + a) * rows : (b * side + a + 1) * rows]
            for a in range(side)
            for b in range(side)
        ],
        axis=0,
    )


def expert_kernel(side, *refs):
    near, far = refs[:side], refs[side : 2 * side]
    wg0, wg1, wu0, wu1, hv_ref = refs[2 * side : 2 * side + 5]
    out_near, out_far, first, second = refs[2 * side + 5 :]
    half = wg0.shape[1]
    depth = out_near.shape[1]
    slot = out_near.shape[0] // (side * side)
    near_rows = jnp.concatenate([r[...] for r in near], axis=0)
    far_rows = jnp.concatenate([r[...] for r in far], axis=0)

    def product(w):
        return mm(near_rows, w[:depth, :]) + swap_blocks(mm(far_rows, w[depth:, :]), side, slot)

    for k, (wg, wu) in enumerate(((wg0, wu0), (wg1, wu1))):
        span = slice(k * half, (k + 1) * half)
        gate = product(wg)
        up = product(wu)
        sig = 1.0 / (1.0 + jnp.exp(-gate))
        hv = hv_ref[k : k + 1, :]
        first[:, span] = (hv * up * sig * (1.0 + gate * (1.0 - sig))).astype(BF)
        second[:, span] = (hv * gate * sig).astype(BF)
    step = min(depth, 512)

    def terms(cols):
        total = mm_t(first[:, :half], wg0[cols, :]) + mm_t(second[:, :half], wu0[cols, :])
        return total + mm_t(first[:, half:], wg1[cols, :]) + mm_t(second[:, half:], wu1[cols, :])

    @pl.loop(0, depth // step)
    def _(i):
        start = pl.multiple_of(i * step, step)
        cols = pl.ds(start, step)
        out_near[:, cols] = terms(cols).astype(BF)
        more = pl.ds(pl.multiple_of(depth + start, step), step)
        out_far[:, cols] = swap_blocks(terms(more), side, slot).astype(BF)


def expert_rows(near, far, wg0, wg1, wu0, wu1, head_vec):
    side = len(near)
    count = side * near[0].shape[0]
    depth = near[0].shape[1]
    half = wg0.shape[1]
    out = jax.ShapeDtypeStruct((count, depth), BF)
    args = (*near, *far, wg0, wg1, wu0, wu1, head_vec)
    held = pl.BlockSpec(memory_space=pltpu.VMEM)
    return pl.pallas_call(
        functools.partial(expert_kernel, side),
        out_shape=(out, out),
        in_specs=[held] * len(args),
        out_specs=(held, held),
        scratch_shapes=[pltpu.VMEM((count, 2 * half), BF)] * 2,
        compiler_params=vmem(26),
        cost_estimate=cost(32 * count * depth * half, 16 * depth * half + 8 * count * depth),
        name="experts",
    )(*args)


def gather_around(value, axis):
    count = lax.axis_size(axis)
    if count != 4:
        return [value] + [shift(value, axis, count - k) for k in range(1, count)]
    left, right = shift(value, axis, 1), shift(value, axis, 3)
    cut = value.shape[0] // 2
    across = jnp.concatenate(
        [shift(left[:cut], axis, 1), shift(right[cut:], axis, 3)], axis=0
    )
    return [value, right, across, left]


def gather_direct(value, axis):
    count = lax.axis_size(axis)
    return [value] + [shift(value, axis, count - k) for k in range(1, count)]


def scatter_direct(pieces, axis):
    total = pieces[0].astype(F32)
    for k in range(1, len(pieces)):
        total = total + shift(pieces[k], axis, k).astype(F32)
    return total


def scatter_around(pieces, axis):
    if len(pieces) != 4:
        return scatter_direct(pieces, axis)
    own, right, across, left = pieces
    cut = across.shape[0] // 2
    top = shift(across[:cut], axis, 1)
    bottom = shift(across[cut:], axis, 3)
    right = jnp.concatenate(
        [(right[:cut].astype(F32) + top.astype(F32)).astype(BF), right[cut:]], axis=0
    )
    left = jnp.concatenate(
        [left[:cut], (left[cut:].astype(F32) + bottom.astype(F32)).astype(BF)], axis=0
    )
    return own.astype(F32) + shift(right, axis, 1).astype(F32) + shift(left, axis, 3).astype(F32)


def split_rows(value, count):
    rows = value.shape[0] // count
    return [value[k * rows : (k + 1) * rows] for k in range(count)]


def row_mask(tlen):
    rowpos = lax.broadcasted_iota(jnp.int32, (tlen, tlen), 0)
    colpos = lax.broadcasted_iota(jnp.int32, (tlen, tlen), 1)
    return rowpos >= colpos


def vmem(mib):
    return pltpu.CompilerParams(vmem_limit_bytes=mib << 20)


def whole(arrays):
    return [pl.BlockSpec(a.shape, lambda i, n=len(a.shape): (0,) * n) for a in arrays]


def single(kernel, out_shape, args, **options):
    outs = whole(out_shape) if isinstance(out_shape, tuple) else whole((out_shape,))[0]
    return pl.pallas_call(
        kernel,
        grid=(1,),
        out_shape=out_shape,
        in_specs=whole(args),
        out_specs=tuple(outs) if isinstance(outs, list) else outs,
        **options,
    )(*args)


def cost(flops, moved):
    return pl.CostEstimate(flops=flops, bytes_accessed=moved, transcendentals=0)


def proj_kernel(
    heads, slice_rows, cand, w_in, w_bc, w_step, bias, rate,
    inner_out, bc_out, pre_out, step_out, cum_out, step_t_out, cum_t_out, pay_out,
    acc, acc_bc, acc_pre,
):
    i = pl.program_id(0)

    @pl.when(i == 0)
    def _():
        acc[...] = jnp.zeros_like(acc)
        acc_bc[...] = jnp.zeros_like(acc_bc)
        acc_pre[...] = jnp.zeros_like(acc_pre)

    x = cand[...]
    acc[...] += mm(x, w_in[...])
    acc_bc[...] += mm(x, w_bc[...])
    acc_pre[:, :heads] += mm_t(x, w_step[...])

    @pl.when(i == pl.num_programs(0) - 1)
    def _():
        tlen, chan = acc.shape
        size = chan // heads
        nstate = acc_bc.shape[1] // 2
        pre = acc_pre[...] + bias[...]
        step = jnp.maximum(pre, 0.0) + jnp.log1p(jnp.exp(-jnp.abs(pre)))
        lower = row_mask(tlen).astype(F32)
        cum = jnp.dot(lower, -step * rate[...], precision=HIGH, preferred_element_type=F32)
        pre_out[...] = pre
        step_out[...] = step
        cum_out[...] = cum
        step_t_out[...] = step.T
        cum_t_out[...] = cum.T
        last = cum[tlen - 1 : tlen, :]
        tail = jnp.exp(last - cum) * step
        inner_b = acc[...].astype(BF)
        inner_out[...] = inner_b
        bc = acc_bc[...].astype(BF)
        bc_out[...] = bc
        b_rows = bc[:, :nstate]
        extra = pay_out.shape[1] - slice_rows
        place = lax.broadcasted_iota(jnp.int32, (extra, nstate), 0)
        per = size // slice_rows
        for h in range(heads):
            span = slice(h * size, (h + 1) * size)
            fed = (tail[:, h : h + 1] * inner_b[:, span].astype(F32)).astype(BF)
            fresh = t_mm(fed, b_rows).astype(BF)
            value = jnp.broadcast_to(last[:, h : h + 1], (extra, nstate))
            scaled = value * 65537.0
            hi = scaled - (scaled - value)
            rest = value - hi
            scaled = rest * 65537.0
            mid = scaled - (scaled - rest)
            low = rest - mid
            parts = jnp.where(place == 0, hi, jnp.where(place == 1, mid, low))
            parts = jnp.where(place < 3, parts, 0.0).astype(BF)
            for q in range(per):
                pay_out[h * per + q, :slice_rows, :] = fresh[q * slice_rows : (q + 1) * slice_rows]
                pay_out[h * per + q, slice_rows:, :] = parts


def project(candidate, in_proj, bc_proj, step_proj, bias, rate, heads, n_seq):
    tlen, width = candidate.shape
    chan = in_proj.shape[1]
    two = bc_proj.shape[1]
    slice_rows = chan // n_seq
    depth = min(width, 1024)
    small = jax.ShapeDtypeStruct((tlen, tlen), F32)
    fixed = lambda *shape: pl.BlockSpec(shape, lambda i: (0,) * len(shape))
    return pl.pallas_call(
        functools.partial(proj_kernel, heads, slice_rows),
        grid=(width // depth,),
        out_shape=(
            jax.ShapeDtypeStruct((tlen, chan), BF),
            jax.ShapeDtypeStruct((tlen, two), BF),
            small, small, small, small, small,
            jax.ShapeDtypeStruct((n_seq, slice_rows + EXTRA, two // 2), BF),
        ),
        in_specs=[
            pl.BlockSpec((tlen, depth), lambda i: (0, i)),
            pl.BlockSpec((depth, chan), lambda i: (i, 0)),
            pl.BlockSpec((depth, two), lambda i: (i, 0)),
            pl.BlockSpec((heads, depth), lambda i: (0, i)),
            fixed(1, tlen), fixed(1, tlen),
        ],
        out_specs=(
            fixed(tlen, chan), fixed(tlen, two),
            fixed(tlen, tlen), fixed(tlen, tlen), fixed(tlen, tlen), fixed(tlen, tlen),
            fixed(tlen, tlen), fixed(n_seq, slice_rows + EXTRA, two // 2),
        ),
        scratch_shapes=[
            pltpu.VMEM((tlen, chan), F32), pltpu.VMEM((tlen, two), F32), pltpu.VMEM((tlen, tlen), F32)
        ],
        compiler_params=vmem(56),
        cost_estimate=cost(2 * tlen * width * (chan + two), 2 * width * (chan + two + 2 * tlen)),
        name="project",
    )(candidate, in_proj, bc_proj, step_proj, bias, rate)


def enter_kernel(got, out, decay):
    count, rows, nstate = out.shape
    out[0] = jnp.zeros((rows, nstate), BF)
    state = jnp.zeros((rows, nstate), F32)
    for s in range(count):
        tags = got[s, rows:, :].astype(F32)
        fade = jnp.exp(jnp.sum(tags, axis=0, keepdims=True))
        decay[s : s + 1, :] = fade
        if s < count - 1:
            state = fade * state + got[s, :rows, :].astype(F32)
            out[s + 1] = state.astype(BF)


def enter_states(got, slice_rows):
    count, _, nstate = got.shape
    return single(
        enter_kernel,
        out_shape=(
            jax.ShapeDtypeStruct((count, slice_rows, nstate), BF),
            jax.ShapeDtypeStruct((count, nstate), F32),
        ),
        args=(got,),
        compiler_params=vmem(56),
        name="enter",
    )


def leave_kernel(got, decay, out):
    count, rows, nstate = out.shape
    out[count - 1] = jnp.zeros((rows, nstate), BF)
    state = jnp.zeros((rows, nstate), F32)
    for s in range(count - 1, 0, -1):
        state = decay[s : s + 1, :] * state + got[s].astype(F32)
        out[s - 1] = state.astype(BF)


def leave_states(got, decay):
    return single(
        leave_kernel,
        out_shape=jax.ShapeDtypeStruct(got.shape, BF),
        args=(got, decay,),
        compiler_params=vmem(56),
        name="leave",
    )


def decay_weights(cum, cum_t, h):
    tlen = cum.shape[0]
    gaps = jnp.minimum(cum[:, h : h + 1] - cum_t[h : h + 1, :], 0.0)
    return jnp.where(row_mask(tlen), jnp.exp(gaps), 0.0)


def within_kernel(heads, inner_ref, bc_ref, cum_ref, cum_t_ref, step_t_ref, skip_ref, out):
    tlen, chan = out.shape
    size = chan // heads
    bc = bc_ref[...]
    nstate = bc.shape[1] // 2
    scores = mm_t(bc[:, nstate:], bc[:, :nstate])
    cum, cum_t, step_t = cum_ref[...], cum_t_ref[...], step_t_ref[...]
    for h in range(heads):
        span = slice(h * size, (h + 1) * size)
        mixing = (decay_weights(cum, cum_t, h) * scores * step_t[h : h + 1, :]).astype(BF)
        inner = inner_ref[:, span]
        out[:, span] = mm(mixing, inner) + skip_ref[:, span] * inner.astype(F32)


def mix_within(inner_b, bc_bf, cum, cum_t, step_t, skip, heads):
    tlen, chan = inner_b.shape
    return single(
        functools.partial(within_kernel, heads),
        out_shape=jax.ShapeDtypeStruct((tlen, chan), F32),
        args=(inner_b, bc_bf, cum, cum_t, step_t, skip,),
        compiler_params=vmem(56),
        cost_estimate=cost(2 * tlen * tlen * chan * 4, 8 * tlen * chan),
        name="mix_within",
    )


def slots_kernel(
    heads, cap, within, bc_ref, cum_ref, state, table, own_table, cand, w_out,
    own_out, send1, send2, send3, reads_out, slots,
):
    @pl.when(pl.program_id(0) == 0)
    def _():
        chan = within.shape[1]
        size = chan // heads
        nstate = bc_ref.shape[1] // 2
        c_rows = bc_ref[:, nstate:]
        growth = jnp.exp(cum_ref[...])
        for h in range(heads):
            span = slice(h * size, (h + 1) * size)
            reads = mm_t(c_rows, state[span, :])
            reads_out[:, span] = reads
            mixed = (within[:, span] + growth[:, h : h + 1] * reads).astype(BF)
            slots[:, span] = mm(table[...], mixed).astype(BF)

    part = mm(slots[...], w_out[...])
    own_out[...] = part[:cap] + mm(own_table[...], cand[...])
    for k, send in enumerate((send1, send2, send3)):
        send[...] = part[(k + 1) * cap : (k + 2) * cap].astype(BF)


def mix_slots(within, bc_bf, cum, state, table, own_table, candidate, out_proj, heads):
    tlen, chan = within.shape
    width = out_proj.shape[1]
    rows = table.shape[0]
    block = min(width, 2048)
    fixed = lambda a: pl.BlockSpec(a.shape, lambda i: (0,) * a.ndim)
    cols = lambda n: pl.BlockSpec((n, block), lambda i: (0, i))
    sent = jax.ShapeDtypeStruct((CAP, width), BF)
    return pl.pallas_call(
        functools.partial(slots_kernel, heads, CAP),
        grid=(width // block,),
        out_shape=(
            jax.ShapeDtypeStruct((CAP, width), F32), sent, sent, sent,
            jax.ShapeDtypeStruct((tlen, chan), F32),
        ),
        in_specs=[fixed(a) for a in (within, bc_bf, cum, state, table, own_table)]
        + [cols(tlen), cols(chan)],
        out_specs=(cols(CAP), cols(CAP), cols(CAP), cols(CAP), fixed(within)),
        scratch_shapes=[pltpu.VMEM((rows, chan), BF)],
        compiler_params=vmem(56),
        cost_estimate=cost(2 * rows * chan * width, 2 * chan * width),
        name="mix_slots",
    )(within, bc_bf, cum, state, table, own_table, candidate, out_proj)


def outgrad_kernel(heads, table, terms, energy, w_out, bc_ref, cum_ref, hid_out, grad_out, local_out, acc):
    i = pl.program_id(0)

    @pl.when(i == 0)
    def _():
        acc[...] = jnp.zeros_like(acc)

    hid = energy[...] + t_mm(table[...], terms[...])
    hid_out[...] = hid
    acc[...] += mm_t(hid.astype(BF), w_out[...])

    @pl.when(i == pl.num_programs(0) - 1)
    def _():
        chan = acc.shape[1]
        size = chan // heads
        nstate = bc_ref.shape[1] // 2
        c_rows = bc_ref[:, nstate:]
        growth = jnp.exp(cum_ref[...])
        for h in range(heads):
            span = slice(h * size, (h + 1) * size)
            grad = acc[:, span]
            grad_out[:, span] = grad
            grown = (growth[:, h : h + 1] * grad).astype(BF)
            local_out[span, :] = t_mm(grown, c_rows).astype(BF)


def out_gradient(table, terms, energy, out_proj, bc_bf, cum, heads):
    tlen = table.shape[1]
    chan, width = out_proj.shape
    nstate = bc_bf.shape[1] // 2
    block = min(width, 2048)
    fixed = lambda *shape: pl.BlockSpec(shape, lambda i: (0,) * len(shape))
    cols = lambda n: pl.BlockSpec((n, block), lambda i: (0, i))
    return pl.pallas_call(
        functools.partial(outgrad_kernel, heads),
        grid=(width // block,),
        out_shape=(
            jax.ShapeDtypeStruct((tlen, width), F32),
            jax.ShapeDtypeStruct((tlen, chan), F32),
            jax.ShapeDtypeStruct((chan, nstate), BF),
        ),
        in_specs=[
            fixed(*table.shape), cols(terms.shape[0]), cols(1), cols(chan),
            fixed(*bc_bf.shape), fixed(*cum.shape),
        ],
        out_specs=(cols(tlen), fixed(tlen, chan), fixed(chan, nstate)),
        scratch_shapes=[pltpu.VMEM((tlen, chan), F32)],
        compiler_params=vmem(56),
        cost_estimate=cost(2 * tlen * chan * width, 2 * chan * width),
        name="out_gradient",
    )(table, terms, energy, out_proj, bc_bf, cum)


def near_kernel(
    heads, grad_ref, inner_ref, bc_ref, cum_ref, cum_t_ref, step_ref, step_t_ref, reads, state, skip_ref,
    g_out, gb_out, gc_out, dcum_out, dstep_out, rows, cols,
):
    tlen, chan = grad_ref.shape
    size = chan // heads
    nstate = bc_ref.shape[1] // 2
    b_rows, c_rows = bc_ref[:, :nstate], bc_ref[:, nstate:]
    scores = mm_t(c_rows, b_rows)
    cum, cum_t, step_t = cum_ref[...], cum_t_ref[...], step_t_ref[...]
    growth = jnp.exp(cum)
    rows[...] = jnp.zeros_like(rows)
    cols[...] = jnp.zeros_like(cols)
    d_scores = jnp.zeros((tlen, tlen), F32)
    g_c = jnp.zeros((tlen, nstate), F32)
    for h in range(heads):
        span = slice(h * size, (h + 1) * size)
        grad = grad_ref[:, span]
        grad_b = grad.astype(BF)
        inner = inner_ref[:, span]
        step_h = step_t[h : h + 1, :]
        weights = decay_weights(cum, cum_t, h)
        d_w = mm_t(grad_b, inner) * weights
        d_scores = d_scores + d_w * step_h
        d_ws = d_w * scores
        rows[h : h + 1, :] = jnp.sum(d_ws, axis=0, keepdims=True)
        grown = growth[:, h : h + 1] * grad
        cols[:, h : h + 1] = jnp.sum(d_ws * step_h, axis=1, keepdims=True) + jnp.sum(
            grown * reads[:, span], axis=1, keepdims=True
        )
        mixing = (weights * scores * step_h).astype(BF)
        g_out[:, span] = t_mm(mixing, grad_b) + skip_ref[:, span] * grad
        g_c = g_c + mm(grown.astype(BF), state[span, :])
    d_scores = d_scores.astype(BF)
    gc_out[...] = g_c + mm(d_scores, b_rows)
    gb_out[...] = t_mm(d_scores, c_rows)
    d_step = rows[...].T
    dstep_out[...] = d_step
    dcum_out[...] = cols[...] - step_ref[...] * d_step


def near_gradient(grad, inner_b, bc_bf, cum, cum_t, step, step_t, reads, state, skip, heads):
    tlen, chan = grad.shape
    small = jax.ShapeDtypeStruct((tlen, tlen), F32)
    return single(
        functools.partial(near_kernel, heads),
        out_shape=(jax.ShapeDtypeStruct((tlen, chan), F32), small, small, small, small),
        args=(grad, inner_b, bc_bf, cum, cum_t, step, step_t, reads, state, skip,),
        scratch_shapes=[pltpu.VMEM((tlen, tlen), F32)] * 2,
        compiler_params=vmem(56),
        cost_estimate=cost(2 * tlen * tlen * chan * 8, 20 * tlen * chan),
        name="near_gradient",
    )


def far_kernel(
    heads, later, state, inner_ref, bc_ref, cum_ref, step_ref, pre_ref, rate, near, gb_ref, gc_ref,
    dcum_ref, dstep_ref, g_out, gbc_out, gpre_out, kept, cols,
):
    tlen, chan = near.shape
    size = chan // heads
    nstate = bc_ref.shape[1] // 2
    b_rows = bc_ref[:, :nstate]
    cum, step, pre = cum_ref[...], step_ref[...], pre_ref[...]
    last = cum[tlen - 1 : tlen, :]
    fade = jnp.exp(last - cum)
    tail = fade * step
    kept[...] = jnp.zeros_like(kept)
    cols[...] = jnp.zeros_like(cols)
    g_b = gb_ref[...]
    for h in range(heads):
        span = slice(h * size, (h + 1) * size)
        late = later[span, :]
        tail_h = tail[:, h : h + 1]
        fed_back = mm_t(b_rows, late)
        g_out[:, span] = (near[:, span] + tail_h * fed_back).astype(BF)
        inner = inner_ref[:, span].astype(F32)
        cols[:, h : h + 1] = jnp.sum(inner * fed_back, axis=1, keepdims=True)
        g_b = g_b + mm((tail_h * inner).astype(BF), late)
        kept[h : h + 1, :] = jnp.sum(
            state[span, :].astype(F32) * late.astype(F32), axis=0, keepdims=True
        )
    gbc_out[:, :nstate] = g_b.astype(BF)
    gbc_out[:, nstate:] = gc_ref[...].astype(BF)
    d_tail = cols[...]
    tail_term = d_tail * tail
    kept_row = jnp.sum(kept[...].T, axis=0, keepdims=True)
    d_last = jnp.exp(last) * kept_row + jnp.sum(tail_term, axis=0, keepdims=True)
    rowpos = lax.broadcasted_iota(jnp.int32, cum.shape, 0)
    d_cum = dcum_ref[...] - tail_term + jnp.where(rowpos == tlen - 1, d_last, 0.0)
    colpos = lax.broadcasted_iota(jnp.int32, cum.shape, 1)
    upper = (rowpos <= colpos).astype(F32)
    d_decay = jnp.dot(upper, d_cum, precision=HIGH, preferred_element_type=F32)
    g_step = dstep_ref[...] + fade * d_tail - rate[...] * d_decay
    gpre_out[...] = (g_step / (1.0 + jnp.exp(-pre))).astype(BF)


def far_gradient(later, state, inner_b, bc_bf, cum, step, pre, rate, near, gb, gc, dcum, dstep, heads):
    tlen, chan = near.shape
    return single(
        functools.partial(far_kernel, heads),
        out_shape=(
            jax.ShapeDtypeStruct((tlen, chan), BF),
            jax.ShapeDtypeStruct(bc_bf.shape, BF),
            jax.ShapeDtypeStruct((tlen, tlen), BF),
        ),
        args=(later, state, inner_b, bc_bf, cum, step, pre, rate, near, gb, gc, dcum, dstep,),
        scratch_shapes=[pltpu.VMEM((tlen, tlen), F32)] * 2,
        compiler_params=vmem(56),
        cost_estimate=cost(2 * tlen * tlen * chan * 4, 20 * tlen * chan),
        name="far_gradient",
    )


def back_kernel(heads, per, which, g_ref, gbc, gpre, w_in, w_bc, w_step, *outs):
    total = mm_t(g_ref[...], w_in[...]) + mm_t(gbc[...], w_bc[...])
    total += mm(gpre[:, :heads], w_step[...])
    for k, out in enumerate(outs):

        @pl.when(pl.program_id(0) // per == k)
        def _():
            out[...] = total.astype(out.dtype)


def back_columns(which, g_inner, g_bc, g_pre, in_proj, bc_proj, step_w, cols, dtype, heads):
    tlen, chan = g_inner.shape
    two = bc_proj.shape[1]
    count = which.shape[0]
    block = min(cols, 1024)
    per = cols // block
    fixed = lambda a: pl.BlockSpec(a.shape, lambda i, w: (0,) * a.ndim)
    place = lambda i, w: w[i // per] * per + i % per
    rows = lambda n: pl.BlockSpec((block, n), lambda i, w: (place(i, w), 0))
    return pl.pallas_call(
        functools.partial(back_kernel, heads, per),
        grid_spec=pltpu.PrefetchScalarGridSpec(
            num_scalar_prefetch=1,
            grid=(count * per,),
            in_specs=[
                fixed(g_inner), fixed(g_bc), fixed(g_pre), rows(chan), rows(two),
                pl.BlockSpec((heads, block), lambda i, w: (0, place(i, w))),
            ],
            out_specs=tuple(
                pl.BlockSpec((tlen, block), lambda i, w, k=k: (0, jnp.clip(i - k * per, 0, per - 1)))
                for k in range(count)
            ),
        ),
        out_shape=tuple(jax.ShapeDtypeStruct((tlen, cols), dtype) for _ in range(count)),
        compiler_params=vmem(56),
        cost_estimate=cost(2 * tlen * (chan + two) * cols * count, 2 * (chan + two) * cols * count),
        name="back_columns",
    )(which, g_inner, g_bc, g_pre, in_proj, bc_proj, step_w)


def shards(
    candidate,
    in_proj,
    bc_proj,
    step_proj,
    step_bias,
    decay_rate,
    skip_gain,
    out_proj,
    expert_ids,
    gate_weights,
    expert_gate,
    expert_up,
    expert_down,
    energy_head,
):
    tlen, width = candidate.shape
    heads = step_bias.shape[0]
    step_w = step_proj.T
    chan = in_proj.shape[1]
    size = chan // heads
    nstate = bc_proj.shape[1] // 2
    column = lax.axis_index("e")
    n_exp = lax.axis_size("e")
    n_seq = lax.axis_size(SEQ)
    col_count = width // n_exp
    slice_rows = chan // n_seq
    lanes = lambda v: jnp.pad(v, (0, tlen - heads))[None, :]
    bias, rate = lanes(step_bias), lanes(decay_rate)
    skip = jnp.repeat(skip_gain, size)[None, :]
    energy = energy_head[None, :]

    wg0, wu0 = expert_gate[0], expert_up[0]
    wg1 = shift(wg0, "c", 1)
    wu1 = shift(wu0, "c", 1)

    pairs = [
        slot_table(expert_ids, gate_weights, lax.rem(column + k, n_exp)) for k in range(n_exp)
    ]
    table = jnp.concatenate([p[0] for p in pairs], axis=0).astype(BF)
    own_table, own_weight = pairs[0]
    slot_weight = jnp.sum(own_table * own_weight[None, :], axis=1, keepdims=True)
    own_table = own_table.astype(BF)

    inner_b, bc_bf, pre, step, cum, step_t, cum_t, payload = project(
        candidate, in_proj, bc_proj, step_w, bias, rate, heads, n_seq
    )
    payload, wg1, wu1, table, own_table, slot_weight = lax.optimization_barrier(
        (payload, wg1, wu1, table, own_table, slot_weight)
    )
    got = lax.all_to_all(payload, SEQ, 0, 0, tiled=True)
    within = mix_within(inner_b, bc_bf, cum, cum_t, step_t, skip, heads)
    entering, decay = enter_states(got, slice_rows)
    entering, down = lax.optimization_barrier((entering, expert_down[0]))
    head_own = jnp.sum(down.astype(F32) * energy, axis=1)
    head_other = shift(head_own[None, :], "c", 1)
    head_vec = jnp.concatenate([head_own[None, :], head_other], axis=0)
    state = lax.all_to_all(entering, SEQ, 0, 0, tiled=True).reshape(chan, nstate)

    own, send1, send2, send3, reads = mix_slots(
        within, bc_bf, cum, state, table, own_table, candidate, out_proj, heads
    )
    for k, send in enumerate((send1, send2, send3)):
        own = own + shift(send, "e", k + 1).astype(F32)
    hidden = own.astype(BF).astype(F32)
    scale = jnp.sqrt(jnp.mean(hidden * hidden, axis=-1, keepdims=True) + EPS)
    normed = hidden / scale
    routed = normed.astype(BF)

    side = lax.axis_size("x")
    cut = width // 2
    near_own = jnp.concatenate(gather_direct(routed[:, :cut], "z"), axis=0)
    far_own = jnp.concatenate(gather_direct(routed[:, cut:], "x"), axis=0)
    near_rows = gather_around(near_own, "x")
    far_rows = gather_around(far_own, "z")
    out_near, out_far = expert_rows(near_rows, far_rows, wg0, wg1, wu0, wu1, head_vec)
    near_sum = scatter_around(split_rows(out_near, side), "x").astype(BF)
    far_sum = scatter_around(split_rows(out_far, side), "z").astype(BF)
    slot_grad = jnp.concatenate(
        [
            scatter_direct(split_rows(near_sum, side), "z"),
            scatter_direct(split_rows(far_sum, side), "x"),
        ],
        axis=1,
    )
    along = jnp.mean(normed * slot_grad, axis=-1, keepdims=True)
    slot_term = (slot_weight * (slot_grad - normed * along) / scale).astype(BF)
    all_terms = jnp.concatenate(
        [slot_term] + [shift(slot_term, "e", n_exp - k) for k in range(1, n_exp)], axis=0
    )
    hid_grad, out_grad, local_grad = out_gradient(
        table, all_terms, energy, out_proj, bc_bf, cum, heads
    )

    got_grad = lax.all_to_all(
        local_grad.reshape(n_seq, slice_rows, nstate), SEQ, 0, 0, tiled=True
    )
    near, gb, gc, dcum, dstep = near_gradient(
        out_grad, inner_b, bc_bf, cum, cum_t, step, step_t, reads, state, skip, heads
    )
    leaving = leave_states(got_grad, decay)
    later = lax.all_to_all(leaving, SEQ, 0, 0, tiled=True).reshape(chan, nstate)
    g_inner, g_bc, g_pre = far_gradient(
        later, state, inner_b, bc_bf, cum, step, pre, rate, near, gb, gc, dcum, dstep, heads
    )

    def columns(places, dtype):
        which = jnp.stack([lax.rem(column + k, n_exp) for k in places])
        return back_columns(
            which, g_inner, g_bc, g_pre, in_proj, bc_proj, step_w, col_count, dtype, heads
        )

    order = (2, 1, 3)
    arrived = [shift(part, "e", k) for k, part in zip(order, columns(order, BF))]
    (own_part,) = columns((0,), F32)
    summed = lax.dynamic_slice_in_dim(hid_grad, column * col_count, col_count, 1) + own_part
    for value in arrived:
        summed = summed + value.astype(F32)
    own_cand = lax.dynamic_slice_in_dim(candidate, column * col_count, col_count, 1).astype(F32)
    return (own_cand - DESCENT * summed).astype(BF)


def solution(mesh):
    n_seq, n_exp = mesh.devices.shape
    side = int(round((n_seq // 2) ** 0.5))
    grid = Mesh(mesh.devices.reshape(side, side, 2, n_exp), ("x", "z", "c", "e"))
    in_specs = (
        P(SEQ, None),
        P(None, "e"),
        P(),
        P(None, "e"),
        P("e"),
        P("e"),
        P("e"),
        P("e", None),
        P(SEQ, None),
        P(SEQ, None),
        P("e", None, SEQ),
        P("e", None, SEQ),
        P("e", SEQ, None),
        P(),
    )
    return jax.shard_map(
        shards, mesh=grid, in_specs=in_specs, out_specs=P(SEQ, "e"), check_vma=False
    )
```

```python
import functools

import jax
import jax.numpy as jnp
import numpy as np
from jax import lax
from jax.experimental import pallas as pl
from jax.experimental.pallas import tpu as pltpu
from jax.sharding import Mesh
from jax.sharding import PartitionSpec as P

CAP = 24
EPS = 1e-05
DESCENT = 0.5
HIGH = lax.Precision.HIGHEST
BF = jnp.bfloat16
F32 = jnp.float32
SEQ = ("x", "z", "c")
EXTRA = 16


def mm(a, b):
    return jnp.dot(a, b, preferred_element_type=F32)


def mm_t(a, b):
    return lax.dot_general(a, b, (((1,), (1,)), ((), ())), preferred_element_type=F32)


def t_mm(a, b):
    return lax.dot_general(a, b, (((0,), (0,)), ((), ())), preferred_element_type=F32)


def shift(value, axis, by):
    count = lax.axis_size(axis)
    return lax.ppermute(value, axis, [(i, (i + by) % count) for i in range(count)])


def slot_table(ids_rows, gate_rows, expert):
    tlen = ids_rows.shape[0]
    match = ids_rows == expert
    hits = jnp.sum(match.astype(F32), axis=1)
    weight = jnp.sum(jnp.where(match, gate_rows.astype(F32), 0.0), axis=1)
    rowpos = lax.broadcasted_iota(jnp.int32, (tlen, tlen), 0)
    colpos = lax.broadcasted_iota(jnp.int32, (tlen, tlen), 1)
    places = jnp.sum(jnp.where(rowpos > colpos, hits[None, :], 0.0), axis=1)
    slot_pos = lax.broadcasted_iota(jnp.int32, (CAP, tlen), 0).astype(F32)
    table = (places[None, :] == slot_pos) & (hits[None, :] > 0.0)
    return table.astype(F32), weight


def swap_blocks(value, side, rows):
    return jnp.concatenate(
        [
            value[(b * side + a) * rows : (b * side + a + 1) * rows]
            for a in range(side)
            for b in range(side)
        ],
        axis=0,
    )


def expert_kernel(side, *refs):
    near, far = refs[:side], refs[side : 2 * side]
    wg0, wg1, wu0, wu1, hv_ref = refs[2 * side : 2 * side + 5]
    out_near, out_far, first, second = refs[2 * side + 5 :]
    half = wg0.shape[1]
    depth = out_near.shape[1]
    slot = out_near.shape[0] // (side * side)
    near_rows = jnp.concatenate([r[...] for r in near], axis=0)
    far_rows = jnp.concatenate([r[...] for r in far], axis=0)

    def product(w):
        return mm(near_rows, w[:depth, :]) + swap_blocks(mm(far_rows, w[depth:, :]), side, slot)

    for k, (wg, wu) in enumerate(((wg0, wu0), (wg1, wu1))):
        span = slice(k * half, (k + 1) * half)
        gate = product(wg)
        up = product(wu)
        sig = 1.0 / (1.0 + jnp.exp(-gate))
        hv = hv_ref[k : k + 1, :]
        first[:, span] = (hv * up * sig * (1.0 + gate * (1.0 - sig))).astype(BF)
        second[:, span] = (hv * gate * sig).astype(BF)
    step = min(depth, 512)

    def terms(cols):
        total = mm_t(first[:, :half], wg0[cols, :]) + mm_t(second[:, :half], wu0[cols, :])
        return total + mm_t(first[:, half:], wg1[cols, :]) + mm_t(second[:, half:], wu1[cols, :])

    @pl.loop(0, depth // step)
    def _(i):
        start = pl.multiple_of(i * step, step)
        cols = pl.ds(start, step)
        out_near[:, cols] = terms(cols).astype(BF)
        more = pl.ds(pl.multiple_of(depth + start, step), step)
        out_far[:, cols] = swap_blocks(terms(more), side, slot).astype(BF)


def expert_rows(near, far, wg0, wg1, wu0, wu1, head_vec):
    side = len(near)
    count = side * near[0].shape[0]
    depth = near[0].shape[1]
    half = wg0.shape[1]
    out = jax.ShapeDtypeStruct((count, depth), BF)
    args = (*near, *far, wg0, wg1, wu0, wu1, head_vec)
    held = pl.BlockSpec(memory_space=pltpu.VMEM)
    return pl.pallas_call(
        functools.partial(expert_kernel, side),
        out_shape=(out, out),
        in_specs=[held] * len(args),
        out_specs=(held, held),
        scratch_shapes=[pltpu.VMEM((count, 2 * half), BF)] * 2,
        compiler_params=vmem(26),
        cost_estimate=cost(32 * count * depth * half, 16 * depth * half + 8 * count * depth),
        name="experts",
    )(*args)


def gather_around(near, far):
    count = lax.axis_size("x")
    if count != 4:
        return gather_direct(near, "x"), gather_direct(far, "z")
    cut = near.shape[0] // 2
    sides = (shift(near, "x", 1), shift(near, "x", 3), shift(far, "z", 1), shift(far, "z", 3))
    near_l, near_r, far_l, far_r = lax.optimization_barrier(sides)
    near_a = [shift(near_l[:cut], "x", 1), shift(near_r[cut:], "x", 3)]
    far_a = [shift(far_l[:cut], "z", 1), shift(far_r[cut:], "z", 3)]
    return (
        [near, near_r, jnp.concatenate(near_a, axis=0), near_l],
        [far, far_r, jnp.concatenate(far_a, axis=0), far_l],
    )


def gather_direct(value, axis):
    count = lax.axis_size(axis)
    return [value] + [shift(value, axis, count - k) for k in range(1, count)]


def scatter_direct(pieces, axis):
    total = pieces[0].astype(F32)
    for k in range(1, len(pieces)):
        total = total + shift(pieces[k], axis, k).astype(F32)
    return total


def scatter_around(near, far):
    if len(near) != 4:
        return scatter_direct(near, "x"), scatter_direct(far, "z")
    cut = near[2].shape[0] // 2
    crossed = (
        shift(near[2][:cut], "x", 1), shift(near[2][cut:], "x", 3),
        shift(far[2][:cut], "z", 1), shift(far[2][cut:], "z", 3),
    )
    crossed = lax.optimization_barrier(crossed)

    def added(pieces, top, bottom):
        _, right, _, left = pieces
        right = jnp.concatenate(
            [(right[:cut].astype(F32) + top.astype(F32)).astype(BF), right[cut:]], axis=0
        )
        left = jnp.concatenate(
            [left[:cut], (left[cut:].astype(F32) + bottom.astype(F32)).astype(BF)], axis=0
        )
        return right, left

    near_r, near_l = added(near, crossed[0], crossed[1])
    far_r, far_l = added(far, crossed[2], crossed[3])
    near_r, near_l, far_r, far_l = lax.optimization_barrier((near_r, near_l, far_r, far_l))
    sums = (shift(near_r, "x", 1), shift(near_l, "x", 3), shift(far_r, "z", 1), shift(far_l, "z", 3))
    sums = [v.astype(F32) for v in lax.optimization_barrier(sums)]
    return near[0].astype(F32) + sums[0] + sums[1], far[0].astype(F32) + sums[2] + sums[3]


def split_rows(value, count):
    rows = value.shape[0] // count
    return [value[k * rows : (k + 1) * rows] for k in range(count)]


def row_mask(tlen):
    rowpos = lax.broadcasted_iota(jnp.int32, (tlen, tlen), 0)
    colpos = lax.broadcasted_iota(jnp.int32, (tlen, tlen), 1)
    return rowpos >= colpos


def vmem(mib):
    return pltpu.CompilerParams(vmem_limit_bytes=mib << 20)


def whole(arrays):
    return [pl.BlockSpec(a.shape, lambda i, n=len(a.shape): (0,) * n) for a in arrays]


def single(kernel, out_shape, args, **options):
    outs = whole(out_shape) if isinstance(out_shape, tuple) else whole((out_shape,))[0]
    return pl.pallas_call(
        kernel,
        grid=(1,),
        out_shape=out_shape,
        in_specs=whole(args),
        out_specs=tuple(outs) if isinstance(outs, list) else outs,
        **options,
    )(*args)


def cost(flops, moved):
    return pl.CostEstimate(flops=flops, bytes_accessed=moved, transcendentals=0)


def proj_kernel(
    heads, slice_rows, cand, w_in, w_bc, w_step, bias, rate,
    inner_out, bc_out, pre_out, step_out, cum_out, step_t_out, cum_t_out, pay_out,
    acc, acc_bc, acc_pre,
):
    i = pl.program_id(0)

    @pl.when(i == 0)
    def _():
        acc[...] = jnp.zeros_like(acc)
        acc_bc[...] = jnp.zeros_like(acc_bc)
        acc_pre[...] = jnp.zeros_like(acc_pre)

    x = cand[...]
    acc[...] += mm(x, w_in[...])
    acc_bc[...] += mm(x, w_bc[...])
    acc_pre[:, :heads] += mm_t(x, w_step[...])

    @pl.when(i == pl.num_programs(0) - 1)
    def _():
        tlen, chan = acc.shape
        size = chan // heads
        nstate = acc_bc.shape[1] // 2
        pre = acc_pre[...] + bias[...]
        step = jnp.maximum(pre, 0.0) + jnp.log1p(jnp.exp(-jnp.abs(pre)))
        lower = row_mask(tlen).astype(F32)
        cum = jnp.dot(lower, -step * rate[...], precision=HIGH, preferred_element_type=F32)
        pre_out[...] = pre
        step_out[...] = step
        cum_out[...] = cum
        step_t_out[...] = step.T
        cum_t_out[...] = cum.T
        last = cum[tlen - 1 : tlen, :]
        tail = jnp.exp(last - cum) * step
        inner_b = acc[...].astype(BF)
        inner_out[...] = inner_b
        bc = acc_bc[...].astype(BF)
        bc_out[...] = bc
        b_rows = bc[:, :nstate]
        extra = pay_out.shape[1] - slice_rows
        place = lax.broadcasted_iota(jnp.int32, (extra, nstate), 0)
        per = size // slice_rows
        for h in range(heads):
            span = slice(h * size, (h + 1) * size)
            fed = (tail[:, h : h + 1] * inner_b[:, span].astype(F32)).astype(BF)
            fresh = t_mm(fed, b_rows).astype(BF)
            value = jnp.broadcast_to(last[:, h : h + 1], (extra, nstate))
            scaled = value * 65537.0
            hi = scaled - (scaled - value)
            rest = value - hi
            scaled = rest * 65537.0
            mid = scaled - (scaled - rest)
            low = rest - mid
            parts = jnp.where(place == 0, hi, jnp.where(place == 1, mid, low))
            parts = jnp.where(place < 3, parts, 0.0).astype(BF)
            for q in range(per):
                pay_out[h * per + q, :slice_rows, :] = fresh[q * slice_rows : (q + 1) * slice_rows]
                pay_out[h * per + q, slice_rows:, :] = parts


def project(candidate, in_proj, bc_proj, step_proj, bias, rate, heads, n_seq):
    tlen, width = candidate.shape
    chan = in_proj.shape[1]
    two = bc_proj.shape[1]
    slice_rows = chan // n_seq
    depth = min(width, 1024)
    small = jax.ShapeDtypeStruct((tlen, tlen), F32)
    fixed = lambda *shape: pl.BlockSpec(shape, lambda i: (0,) * len(shape))
    return pl.pallas_call(
        functools.partial(proj_kernel, heads, slice_rows),
        grid=(width // depth,),
        out_shape=(
            jax.ShapeDtypeStruct((tlen, chan), BF),
            jax.ShapeDtypeStruct((tlen, two), BF),
            small, small, small, small, small,
            jax.ShapeDtypeStruct((n_seq, slice_rows + EXTRA, two // 2), BF),
        ),
        in_specs=[
            pl.BlockSpec((tlen, depth), lambda i: (0, i)),
            pl.BlockSpec((depth, chan), lambda i: (i, 0)),
            pl.BlockSpec((depth, two), lambda i: (i, 0)),
            pl.BlockSpec((heads, depth), lambda i: (0, i)),
            fixed(1, tlen), fixed(1, tlen),
        ],
        out_specs=(
            fixed(tlen, chan), fixed(tlen, two),
            fixed(tlen, tlen), fixed(tlen, tlen), fixed(tlen, tlen), fixed(tlen, tlen),
            fixed(tlen, tlen), fixed(n_seq, slice_rows + EXTRA, two // 2),
        ),
        scratch_shapes=[
            pltpu.VMEM((tlen, chan), F32), pltpu.VMEM((tlen, two), F32), pltpu.VMEM((tlen, tlen), F32)
        ],
        compiler_params=vmem(56),
        cost_estimate=cost(2 * tlen * width * (chan + two), 2 * width * (chan + two + 2 * tlen)),
        name="project",
    )(candidate, in_proj, bc_proj, step_proj, bias, rate)


def enter_kernel(got, out, decay):
    count, rows, nstate = out.shape
    out[0] = jnp.zeros((rows, nstate), BF)
    state = jnp.zeros((rows, nstate), F32)
    for s in range(count):
        tags = got[s, rows:, :].astype(F32)
        fade = jnp.exp(jnp.sum(tags, axis=0, keepdims=True))
        decay[s : s + 1, :] = fade
        if s < count - 1:
            state = fade * state + got[s, :rows, :].astype(F32)
            out[s + 1] = state.astype(BF)


def enter_states(got, slice_rows):
    count, _, nstate = got.shape
    return single(
        enter_kernel,
        out_shape=(
            jax.ShapeDtypeStruct((count, slice_rows, nstate), BF),
            jax.ShapeDtypeStruct((count, nstate), F32),
        ),
        args=(got,),
        compiler_params=vmem(56),
        name="enter",
    )


def leave_kernel(got, decay, out):
    count, rows, nstate = out.shape
    out[count - 1] = jnp.zeros((rows, nstate), BF)
    state = jnp.zeros((rows, nstate), F32)
    for s in range(count - 1, 0, -1):
        state = decay[s : s + 1, :] * state + got[s].astype(F32)
        out[s - 1] = state.astype(BF)


def leave_states(got, decay):
    return single(
        leave_kernel,
        out_shape=jax.ShapeDtypeStruct(got.shape, BF),
        args=(got, decay,),
        compiler_params=vmem(56),
        name="leave",
    )


def decay_weights(cum, cum_t, h):
    tlen = cum.shape[0]
    gaps = jnp.minimum(cum[:, h : h + 1] - cum_t[h : h + 1, :], 0.0)
    return jnp.where(row_mask(tlen), jnp.exp(gaps), 0.0)


def within_kernel(heads, inner_ref, bc_ref, cum_ref, cum_t_ref, step_t_ref, skip_ref, out):
    tlen, chan = out.shape
    size = chan // heads
    bc = bc_ref[...]
    nstate = bc.shape[1] // 2
    scores = mm_t(bc[:, nstate:], bc[:, :nstate])
    cum, cum_t, step_t = cum_ref[...], cum_t_ref[...], step_t_ref[...]
    for h in range(heads):
        span = slice(h * size, (h + 1) * size)
        mixing = (decay_weights(cum, cum_t, h) * scores * step_t[h : h + 1, :]).astype(BF)
        inner = inner_ref[:, span]
        out[:, span] = mm(mixing, inner) + skip_ref[:, span] * inner.astype(F32)


def mix_within(inner_b, bc_bf, cum, cum_t, step_t, skip, heads):
    tlen, chan = inner_b.shape
    return single(
        functools.partial(within_kernel, heads),
        out_shape=jax.ShapeDtypeStruct((tlen, chan), F32),
        args=(inner_b, bc_bf, cum, cum_t, step_t, skip,),
        compiler_params=vmem(56),
        cost_estimate=cost(2 * tlen * tlen * chan * 4, 8 * tlen * chan),
        name="mix_within",
    )


def slots_kernel(
    heads, cap, within, bc_ref, cum_ref, state, table, own_table, cand, w_out,
    own_out, send1, send2, send3, reads_out, slots,
):
    @pl.when(pl.program_id(0) == 0)
    def _():
        chan = within.shape[1]
        size = chan // heads
        nstate = bc_ref.shape[1] // 2
        c_rows = bc_ref[:, nstate:]
        growth = jnp.exp(cum_ref[...])
        for h in range(heads):
            span = slice(h * size, (h + 1) * size)
            reads = mm_t(c_rows, state[span, :])
            reads_out[:, span] = reads
            mixed = (within[:, span] + growth[:, h : h + 1] * reads).astype(BF)
            slots[:, span] = mm(table[...], mixed).astype(BF)

    part = mm(slots[...], w_out[...])
    own_out[...] = part[:cap] + mm(own_table[...], cand[...])
    for k, send in enumerate((send1, send2, send3)):
        send[...] = part[(k + 1) * cap : (k + 2) * cap].astype(BF)


def mix_slots(within, bc_bf, cum, state, table, own_table, candidate, out_proj, heads):
    tlen, chan = within.shape
    width = out_proj.shape[1]
    rows = table.shape[0]
    block = min(width, 2048)
    fixed = lambda a: pl.BlockSpec(a.shape, lambda i: (0,) * a.ndim)
    cols = lambda n: pl.BlockSpec((n, block), lambda i: (0, i))
    sent = jax.ShapeDtypeStruct((CAP, width), BF)
    return pl.pallas_call(
        functools.partial(slots_kernel, heads, CAP),
        grid=(width // block,),
        out_shape=(
            jax.ShapeDtypeStruct((CAP, width), F32), sent, sent, sent,
            jax.ShapeDtypeStruct((tlen, chan), F32),
        ),
        in_specs=[fixed(a) for a in (within, bc_bf, cum, state, table, own_table)]
        + [cols(tlen), cols(chan)],
        out_specs=(cols(CAP), cols(CAP), cols(CAP), cols(CAP), fixed(within)),
        scratch_shapes=[pltpu.VMEM((rows, chan), BF)],
        compiler_params=vmem(56),
        cost_estimate=cost(2 * rows * chan * width, 2 * chan * width),
        name="mix_slots",
    )(within, bc_bf, cum, state, table, own_table, candidate, out_proj)


def outgrad_kernel(heads, table, terms, energy, w_out, bc_ref, cum_ref, hid_out, grad_out, local_out, acc):
    i = pl.program_id(0)

    @pl.when(i == 0)
    def _():
        acc[...] = jnp.zeros_like(acc)

    hid = energy[...] + t_mm(table[...], terms[...])
    hid_out[...] = hid
    acc[...] += mm_t(hid.astype(BF), w_out[...])

    @pl.when(i == pl.num_programs(0) - 1)
    def _():
        chan = acc.shape[1]
        size = chan // heads
        nstate = bc_ref.shape[1] // 2
        c_rows = bc_ref[:, nstate:]
        growth = jnp.exp(cum_ref[...])
        for h in range(heads):
            span = slice(h * size, (h + 1) * size)
            grad = acc[:, span]
            grad_out[:, span] = grad
            grown = (growth[:, h : h + 1] * grad).astype(BF)
            local_out[span, :] = t_mm(grown, c_rows).astype(BF)


def out_gradient(table, terms, energy, out_proj, bc_bf, cum, heads):
    tlen = table.shape[1]
    chan, width = out_proj.shape
    nstate = bc_bf.shape[1] // 2
    block = min(width, 2048)
    fixed = lambda *shape: pl.BlockSpec(shape, lambda i: (0,) * len(shape))
    cols = lambda n: pl.BlockSpec((n, block), lambda i: (0, i))
    return pl.pallas_call(
        functools.partial(outgrad_kernel, heads),
        grid=(width // block,),
        out_shape=(
            jax.ShapeDtypeStruct((tlen, width), F32),
            jax.ShapeDtypeStruct((tlen, chan), F32),
            jax.ShapeDtypeStruct((chan, nstate), BF),
        ),
        in_specs=[
            fixed(*table.shape), cols(terms.shape[0]), cols(1), cols(chan),
            fixed(*bc_bf.shape), fixed(*cum.shape),
        ],
        out_specs=(cols(tlen), fixed(tlen, chan), fixed(chan, nstate)),
        scratch_shapes=[pltpu.VMEM((tlen, chan), F32)],
        compiler_params=vmem(56),
        cost_estimate=cost(2 * tlen * chan * width, 2 * chan * width),
        name="out_gradient",
    )(table, terms, energy, out_proj, bc_bf, cum)


def near_kernel(
    heads, grad_ref, inner_ref, bc_ref, cum_ref, cum_t_ref, step_ref, step_t_ref, reads, state, skip_ref,
    g_out, gb_out, gc_out, dcum_out, dstep_out, rows, cols,
):
    tlen, chan = grad_ref.shape
    size = chan // heads
    nstate = bc_ref.shape[1] // 2
    b_rows, c_rows = bc_ref[:, :nstate], bc_ref[:, nstate:]
    scores = mm_t(c_rows, b_rows)
    cum, cum_t, step_t = cum_ref[...], cum_t_ref[...], step_t_ref[...]
    growth = jnp.exp(cum)
    rows[...] = jnp.zeros_like(rows)
    cols[...] = jnp.zeros_like(cols)
    d_scores = jnp.zeros((tlen, tlen), F32)
    g_c = jnp.zeros((tlen, nstate), F32)
    for h in range(heads):
        span = slice(h * size, (h + 1) * size)
        grad = grad_ref[:, span]
        grad_b = grad.astype(BF)
        inner = inner_ref[:, span]
        step_h = step_t[h : h + 1, :]
        weights = decay_weights(cum, cum_t, h)
        d_w = mm_t(grad_b, inner) * weights
        d_scores = d_scores + d_w * step_h
        d_ws = d_w * scores
        rows[h : h + 1, :] = jnp.sum(d_ws, axis=0, keepdims=True)
        grown = growth[:, h : h + 1] * grad
        cols[:, h : h + 1] = jnp.sum(d_ws * step_h, axis=1, keepdims=True) + jnp.sum(
            grown * reads[:, span], axis=1, keepdims=True
        )
        mixing = (weights * scores * step_h).astype(BF)
        g_out[:, span] = t_mm(mixing, grad_b) + skip_ref[:, span] * grad
        g_c = g_c + mm(grown.astype(BF), state[span, :])
    d_scores = d_scores.astype(BF)
    gc_out[...] = g_c + mm(d_scores, b_rows)
    gb_out[...] = t_mm(d_scores, c_rows)
    d_step = rows[...].T
    dstep_out[...] = d_step
    dcum_out[...] = cols[...] - step_ref[...] * d_step


def near_gradient(grad, inner_b, bc_bf, cum, cum_t, step, step_t, reads, state, skip, heads):
    tlen, chan = grad.shape
    small = jax.ShapeDtypeStruct((tlen, tlen), F32)
    return single(
        functools.partial(near_kernel, heads),
        out_shape=(jax.ShapeDtypeStruct((tlen, chan), F32), small, small, small, small),
        args=(grad, inner_b, bc_bf, cum, cum_t, step, step_t, reads, state, skip,),
        scratch_shapes=[pltpu.VMEM((tlen, tlen), F32)] * 2,
        compiler_params=vmem(56),
        cost_estimate=cost(2 * tlen * tlen * chan * 8, 20 * tlen * chan),
        name="near_gradient",
    )


def far_kernel(
    heads, later, state, inner_ref, bc_ref, cum_ref, step_ref, pre_ref, rate, near, gb_ref, gc_ref,
    dcum_ref, dstep_ref, g_out, gbc_out, gpre_out, kept, cols,
):
    tlen, chan = near.shape
    size = chan // heads
    nstate = bc_ref.shape[1] // 2
    b_rows = bc_ref[:, :nstate]
    cum, step, pre = cum_ref[...], step_ref[...], pre_ref[...]
    last = cum[tlen - 1 : tlen, :]
    fade = jnp.exp(last - cum)
    tail = fade * step
    kept[...] = jnp.zeros_like(kept)
    cols[...] = jnp.zeros_like(cols)
    g_b = gb_ref[...]
    for h in range(heads):
        span = slice(h * size, (h + 1) * size)
        late = later[span, :]
        tail_h = tail[:, h : h + 1]
        fed_back = mm_t(b_rows, late)
        g_out[:, span] = (near[:, span] + tail_h * fed_back).astype(BF)
        inner = inner_ref[:, span].astype(F32)
        cols[:, h : h + 1] = jnp.sum(inner * fed_back, axis=1, keepdims=True)
        g_b = g_b + mm((tail_h * inner).astype(BF), late)
        kept[h : h + 1, :] = jnp.sum(
            state[span, :].astype(F32) * late.astype(F32), axis=0, keepdims=True
        )
    gbc_out[:, :nstate] = g_b.astype(BF)
    gbc_out[:, nstate:] = gc_ref[...].astype(BF)
    d_tail = cols[...]
    tail_term = d_tail * tail
    kept_row = jnp.sum(kept[...].T, axis=0, keepdims=True)
    d_last = jnp.exp(last) * kept_row + jnp.sum(tail_term, axis=0, keepdims=True)
    rowpos = lax.broadcasted_iota(jnp.int32, cum.shape, 0)
    d_cum = dcum_ref[...] - tail_term + jnp.where(rowpos == tlen - 1, d_last, 0.0)
    colpos = lax.broadcasted_iota(jnp.int32, cum.shape, 1)
    upper = (rowpos <= colpos).astype(F32)
    d_decay = jnp.dot(upper, d_cum, precision=HIGH, preferred_element_type=F32)
    g_step = dstep_ref[...] + fade * d_tail - rate[...] * d_decay
    gpre_out[...] = (g_step / (1.0 + jnp.exp(-pre))).astype(BF)


def far_gradient(later, state, inner_b, bc_bf, cum, step, pre, rate, near, gb, gc, dcum, dstep, heads):
    tlen, chan = near.shape
    return single(
        functools.partial(far_kernel, heads),
        out_shape=(
            jax.ShapeDtypeStruct((tlen, chan), BF),
            jax.ShapeDtypeStruct(bc_bf.shape, BF),
            jax.ShapeDtypeStruct((tlen, tlen), BF),
        ),
        args=(later, state, inner_b, bc_bf, cum, step, pre, rate, near, gb, gc, dcum, dstep,),
        scratch_shapes=[pltpu.VMEM((tlen, tlen), F32)] * 2,
        compiler_params=vmem(56),
        cost_estimate=cost(2 * tlen * tlen * chan * 4, 20 * tlen * chan),
        name="far_gradient",
    )


def back_kernel(heads, per, which, g_ref, gbc, gpre, w_in, w_bc, w_step, *outs):
    total = mm_t(g_ref[...], w_in[...]) + mm_t(gbc[...], w_bc[...])
    total += mm(gpre[:, :heads], w_step[...])
    for k, out in enumerate(outs):

        @pl.when(pl.program_id(0) // per == k)
        def _():
            out[...] = total.astype(out.dtype)


def back_columns(which, g_inner, g_bc, g_pre, in_proj, bc_proj, step_w, cols, dtype, heads):
    tlen, chan = g_inner.shape
    two = bc_proj.shape[1]
    count = which.shape[0]
    block = min(cols, 1024)
    per = cols // block
    fixed = lambda a: pl.BlockSpec(a.shape, lambda i, w: (0,) * a.ndim)
    place = lambda i, w: w[i // per] * per + i % per
    rows = lambda n: pl.BlockSpec((block, n), lambda i, w: (place(i, w), 0))
    return pl.pallas_call(
        functools.partial(back_kernel, heads, per),
        grid_spec=pltpu.PrefetchScalarGridSpec(
            num_scalar_prefetch=1,
            grid=(count * per,),
            in_specs=[
                fixed(g_inner), fixed(g_bc), fixed(g_pre), rows(chan), rows(two),
                pl.BlockSpec((heads, block), lambda i, w: (0, place(i, w))),
            ],
            out_specs=tuple(
                pl.BlockSpec((tlen, block), lambda i, w, k=k: (0, jnp.clip(i - k * per, 0, per - 1)))
                for k in range(count)
            ),
        ),
        out_shape=tuple(jax.ShapeDtypeStruct((tlen, cols), dtype) for _ in range(count)),
        compiler_params=vmem(56),
        cost_estimate=cost(2 * tlen * (chan + two) * cols * count, 2 * (chan + two) * cols * count),
        name="back_columns",
    )(which, g_inner, g_bc, g_pre, in_proj, bc_proj, step_w)


def shards(
    candidate,
    in_proj,
    bc_proj,
    step_proj,
    step_bias,
    decay_rate,
    skip_gain,
    out_proj,
    expert_ids,
    gate_weights,
    expert_gate,
    expert_up,
    expert_down,
    energy_head,
):
    tlen, width = candidate.shape
    heads = step_bias.shape[0]
    step_w = step_proj.T
    chan = in_proj.shape[1]
    size = chan // heads
    nstate = bc_proj.shape[1] // 2
    column = lax.axis_index("e")
    n_exp = lax.axis_size("e")
    n_seq = lax.axis_size(SEQ)
    col_count = width // n_exp
    slice_rows = chan // n_seq
    lanes = lambda v: jnp.pad(v, (0, tlen - heads))[None, :]
    bias, rate = lanes(step_bias), lanes(decay_rate)
    skip = jnp.repeat(skip_gain, size)[None, :]
    energy = energy_head[None, :]

    wg0, wu0 = expert_gate[0], expert_up[0]
    wg1 = shift(wg0, "c", 1)
    wu1 = shift(wu0, "c", 1)

    pairs = [
        slot_table(expert_ids, gate_weights, lax.rem(column + k, n_exp)) for k in range(n_exp)
    ]
    table = jnp.concatenate([p[0] for p in pairs], axis=0).astype(BF)
    own_table, own_weight = pairs[0]
    slot_weight = jnp.sum(own_table * own_weight[None, :], axis=1, keepdims=True)
    own_table = own_table.astype(BF)

    inner_b, bc_bf, pre, step, cum, step_t, cum_t, payload = project(
        candidate, in_proj, bc_proj, step_w, bias, rate, heads, n_seq
    )
    payload, wg1, wu1, table, own_table, slot_weight = lax.optimization_barrier(
        (payload, wg1, wu1, table, own_table, slot_weight)
    )
    got = lax.all_to_all(payload, SEQ, 0, 0, tiled=True)
    within = mix_within(inner_b, bc_bf, cum, cum_t, step_t, skip, heads)
    entering, decay = enter_states(got, slice_rows)
    entering, down = lax.optimization_barrier((entering, expert_down[0]))
    head_own = jnp.sum(down.astype(F32) * energy, axis=1)
    head_other = shift(head_own[None, :], "c", 1)
    head_vec = jnp.concatenate([head_own[None, :], head_other], axis=0)
    state = lax.all_to_all(entering, SEQ, 0, 0, tiled=True).reshape(chan, nstate)

    own, send1, send2, send3, reads = mix_slots(
        within, bc_bf, cum, state, table, own_table, candidate, out_proj, heads
    )
    for k, send in enumerate((send1, send2, send3)):
        own = own + shift(send, "e", k + 1).astype(F32)
    hidden = own.astype(BF).astype(F32)
    scale = jnp.sqrt(jnp.mean(hidden * hidden, axis=-1, keepdims=True) + EPS)
    normed = hidden / scale
    routed = normed.astype(BF)

    side = lax.axis_size("x")
    cut = width // 2
    routed, head_vec = lax.optimization_barrier((routed, head_vec))
    near_own = jnp.concatenate(gather_direct(routed[:, :cut], "z"), axis=0)
    far_own = jnp.concatenate(gather_direct(routed[:, cut:], "x"), axis=0)
    near_own, far_own = lax.optimization_barrier((near_own, far_own))
    near_rows, far_rows = gather_around(near_own, far_own)
    out_near, out_far = expert_rows(near_rows, far_rows, wg0, wg1, wu0, wu1, head_vec)
    near_sum, far_sum = scatter_around(split_rows(out_near, side), split_rows(out_far, side))
    near_sum, far_sum = near_sum.astype(BF), far_sum.astype(BF)
    slot_grad = jnp.concatenate(
        [
            scatter_direct(split_rows(near_sum, side), "z"),
            scatter_direct(split_rows(far_sum, side), "x"),
        ],
        axis=1,
    )
    along = jnp.mean(normed * slot_grad, axis=-1, keepdims=True)
    slot_term = (slot_weight * (slot_grad - normed * along) / scale).astype(BF)
    all_terms = jnp.concatenate(
        [slot_term] + [shift(slot_term, "e", n_exp - k) for k in range(1, n_exp)], axis=0
    )
    hid_grad, out_grad, local_grad = out_gradient(
        table, all_terms, energy, out_proj, bc_bf, cum, heads
    )

    got_grad = lax.all_to_all(
        local_grad.reshape(n_seq, slice_rows, nstate), SEQ, 0, 0, tiled=True
    )
    near, gb, gc, dcum, dstep = near_gradient(
        out_grad, inner_b, bc_bf, cum, cum_t, step, step_t, reads, state, skip, heads
    )
    leaving = leave_states(got_grad, decay)
    later = lax.all_to_all(leaving, SEQ, 0, 0, tiled=True).reshape(chan, nstate)
    g_inner, g_bc, g_pre = far_gradient(
        later, state, inner_b, bc_bf, cum, step, pre, rate, near, gb, gc, dcum, dstep, heads
    )

    def columns(places, dtype):
        which = jnp.stack([lax.rem(column + k, n_exp) for k in places])
        return back_columns(
            which, g_inner, g_bc, g_pre, in_proj, bc_proj, step_w, col_count, dtype, heads
        )

    order = (2, 1, 3)
    arrived = [shift(part, "e", k) for k, part in zip(order, columns(order, BF))]
    (own_part,) = columns((0,), F32)
    summed = lax.dynamic_slice_in_dim(hid_grad, column * col_count, col_count, 1) + own_part
    for value in arrived:
        summed = summed + value.astype(F32)
    own_cand = lax.dynamic_slice_in_dim(candidate, column * col_count, col_count, 1).astype(F32)
    return (own_cand - DESCENT * summed).astype(BF)


def solution(mesh):
    n_seq, n_exp = mesh.devices.shape
    side = int(round((n_seq // 2) ** 0.5))
    grid = Mesh(mesh.devices.reshape(side, side, 2, n_exp), ("x", "z", "c", "e"))
    in_specs = (
        P(SEQ, None),
        P(None, "e"),
        P(),
        P(None, "e"),
        P("e"),
        P("e"),
        P("e"),
        P("e", None),
        P(SEQ, None),
        P(SEQ, None),
        P("e", None, SEQ),
        P("e", None, SEQ),
        P("e", SEQ, None),
        P(),
    )
    return jax.shard_map(
        shards, mesh=grid, in_specs=in_specs, out_specs=P(SEQ, "e"), check_vma=False
    )
```

```python
import functools

import jax
import jax.numpy as jnp
import numpy as np
from jax import lax
from jax.experimental import pallas as pl
from jax.experimental.pallas import tpu as pltpu
from jax.sharding import Mesh
from jax.sharding import PartitionSpec as P

CAP = 24
EPS = 1e-05
DESCENT = 0.5
HIGH = lax.Precision.HIGHEST
BF = jnp.bfloat16
F32 = jnp.float32
SEQ = ("x", "z", "c")
EXTRA = 16


def mm(a, b):
    return jnp.dot(a, b, preferred_element_type=F32)


def mm_t(a, b):
    return lax.dot_general(a, b, (((1,), (1,)), ((), ())), preferred_element_type=F32)


def t_mm(a, b):
    return lax.dot_general(a, b, (((0,), (0,)), ((), ())), preferred_element_type=F32)


def shift(value, axis, by):
    count = lax.axis_size(axis)
    return lax.ppermute(value, axis, [(i, (i + by) % count) for i in range(count)])


def slot_table(ids_rows, gate_rows, expert):
    tlen = ids_rows.shape[0]
    match = ids_rows == expert
    hits = jnp.sum(match.astype(F32), axis=1)
    weight = jnp.sum(jnp.where(match, gate_rows.astype(F32), 0.0), axis=1)
    rowpos = lax.broadcasted_iota(jnp.int32, (tlen, tlen), 0)
    colpos = lax.broadcasted_iota(jnp.int32, (tlen, tlen), 1)
    places = jnp.sum(jnp.where(rowpos > colpos, hits[None, :], 0.0), axis=1)
    slot_pos = lax.broadcasted_iota(jnp.int32, (CAP, tlen), 0).astype(F32)
    table = (places[None, :] == slot_pos) & (hits[None, :] > 0.0)
    return table.astype(F32), weight


def swap_blocks(value, side, rows):
    return jnp.concatenate(
        [
            value[(b * side + a) * rows : (b * side + a + 1) * rows]
            for a in range(side)
            for b in range(side)
        ],
        axis=0,
    )


def expert_kernel(side, *refs):
    near, far = refs[:side], refs[side : 2 * side]
    wg0, wg1, wu0, wu1, hv_ref = refs[2 * side : 2 * side + 5]
    out_near, out_far, first, second = refs[2 * side + 5 :]
    half = wg0.shape[1]
    depth = out_near.shape[1]
    slot = out_near.shape[0] // (side * side)
    near_rows = jnp.concatenate([r[...] for r in near], axis=0)
    far_rows = jnp.concatenate([r[...] for r in far], axis=0)

    def product(w):
        return mm(near_rows, w[:depth, :]) + swap_blocks(mm(far_rows, w[depth:, :]), side, slot)

    for k, (wg, wu) in enumerate(((wg0, wu0), (wg1, wu1))):
        span = slice(k * half, (k + 1) * half)
        gate = product(wg)
        up = product(wu)
        sig = 1.0 / (1.0 + jnp.exp(-gate))
        hv = hv_ref[k : k + 1, :]
        first[:, span] = (hv * up * sig * (1.0 + gate * (1.0 - sig))).astype(BF)
        second[:, span] = (hv * gate * sig).astype(BF)
    step = min(depth, 512)

    def terms(cols):
        total = mm_t(first[:, :half], wg0[cols, :]) + mm_t(second[:, :half], wu0[cols, :])
        return total + mm_t(first[:, half:], wg1[cols, :]) + mm_t(second[:, half:], wu1[cols, :])

    @pl.loop(0, depth // step)
    def _(i):
        start = pl.multiple_of(i * step, step)
        cols = pl.ds(start, step)
        out_near[:, cols] = terms(cols).astype(BF)
        more = pl.ds(pl.multiple_of(depth + start, step), step)
        out_far[:, cols] = swap_blocks(terms(more), side, slot).astype(BF)


def expert_rows(near, far, wg0, wg1, wu0, wu1, head_vec):
    side = len(near)
    count = side * near[0].shape[0]
    depth = near[0].shape[1]
    half = wg0.shape[1]
    out = jax.ShapeDtypeStruct((count, depth), BF)
    args = (*near, *far, wg0, wg1, wu0, wu1, head_vec)
    held = pl.BlockSpec(memory_space=pltpu.VMEM)
    return pl.pallas_call(
        functools.partial(expert_kernel, side),
        out_shape=(out, out),
        in_specs=[held] * len(args),
        out_specs=(held, held),
        scratch_shapes=[pltpu.VMEM((count, 2 * half), BF)] * 2,
        compiler_params=vmem(26),
        cost_estimate=cost(32 * count * depth * half, 16 * depth * half + 8 * count * depth),
        name="experts",
    )(*args)


def gather_around(value, axis):
    count = lax.axis_size(axis)
    if count != 4:
        return [value] + [shift(value, axis, count - k) for k in range(1, count)]
    left, right = shift(value, axis, 1), shift(value, axis, 3)
    cut = value.shape[0] // 2
    across = jnp.concatenate(
        [shift(left[:cut], axis, 1), shift(right[cut:], axis, 3)], axis=0
    )
    return [value, right, across, left]


def gather_direct(value, axis):
    count = lax.axis_size(axis)
    return [value] + [shift(value, axis, count - k) for k in range(1, count)]


def scatter_direct(pieces, axis):
    total = pieces[0].astype(F32)
    for k in range(1, len(pieces)):
        total = total + shift(pieces[k], axis, k).astype(F32)
    return total


def scatter_around(pieces, axis):
    if len(pieces) != 4:
        return scatter_direct(pieces, axis)
    own, right, across, left = pieces
    cut = across.shape[0] // 2
    top = shift(across[:cut], axis, 1)
    bottom = shift(across[cut:], axis, 3)
    right = jnp.concatenate(
        [(right[:cut].astype(F32) + top.astype(F32)).astype(BF), right[cut:]], axis=0
    )
    left = jnp.concatenate(
        [left[:cut], (left[cut:].astype(F32) + bottom.astype(F32)).astype(BF)], axis=0
    )
    return own.astype(F32) + shift(right, axis, 1).astype(F32) + shift(left, axis, 3).astype(F32)


def split_rows(value, count):
    rows = value.shape[0] // count
    return [value[k * rows : (k + 1) * rows] for k in range(count)]


def row_mask(tlen):
    rowpos = lax.broadcasted_iota(jnp.int32, (tlen, tlen), 0)
    colpos = lax.broadcasted_iota(jnp.int32, (tlen, tlen), 1)
    return rowpos >= colpos


def vmem(mib):
    return pltpu.CompilerParams(vmem_limit_bytes=mib << 20)


def whole(arrays):
    return [pl.BlockSpec(a.shape, lambda i, n=len(a.shape): (0,) * n) for a in arrays]


def single(kernel, out_shape, args, **options):
    outs = whole(out_shape) if isinstance(out_shape, tuple) else whole((out_shape,))[0]
    return pl.pallas_call(
        kernel,
        grid=(1,),
        out_shape=out_shape,
        in_specs=whole(args),
        out_specs=tuple(outs) if isinstance(outs, list) else outs,
        **options,
    )(*args)


def cost(flops, moved):
    return pl.CostEstimate(flops=flops, bytes_accessed=moved, transcendentals=0)


def proj_kernel(
    heads, slice_rows, cand, w_in, w_bc, w_step, bias, rate,
    inner_out, bc_out, pre_out, step_out, cum_out, step_t_out, cum_t_out, pay_out,
    acc, acc_bc, acc_pre,
):
    i = pl.program_id(0)

    @pl.when(i == 0)
    def _():
        acc[...] = jnp.zeros_like(acc)
        acc_bc[...] = jnp.zeros_like(acc_bc)
        acc_pre[...] = jnp.zeros_like(acc_pre)

    x = cand[...]
    acc[...] += mm(x, w_in[...])
    acc_bc[...] += mm(x, w_bc[...])
    acc_pre[:, :heads] += mm_t(x, w_step[...])

    @pl.when(i == pl.num_programs(0) - 1)
    def _():
        tlen, chan = acc.shape
        size = chan // heads
        nstate = acc_bc.shape[1] // 2
        pre = acc_pre[...] + bias[...]
        step = jnp.maximum(pre, 0.0) + jnp.log1p(jnp.exp(-jnp.abs(pre)))
        lower = row_mask(tlen).astype(F32)
        cum = jnp.dot(lower, -step * rate[...], precision=HIGH, preferred_element_type=F32)
        pre_out[...] = pre
        step_out[...] = step
        cum_out[...] = cum
        step_t_out[...] = step.T
        cum_t_out[...] = cum.T
        last = cum[tlen - 1 : tlen, :]
        tail = jnp.exp(last - cum) * step
        inner_b = acc[...].astype(BF)
        inner_out[...] = inner_b
        bc = acc_bc[...].astype(BF)
        bc_out[...] = bc
        b_rows = bc[:, :nstate]
        extra = pay_out.shape[1] - slice_rows
        place = lax.broadcasted_iota(jnp.int32, (extra, nstate), 0)
        per = size // slice_rows
        for h in range(heads):
            span = slice(h * size, (h + 1) * size)
            fed = (tail[:, h : h + 1] * inner_b[:, span].astype(F32)).astype(BF)
            fresh = t_mm(fed, b_rows).astype(BF)
            value = jnp.broadcast_to(last[:, h : h + 1], (extra, nstate))
            scaled = value * 65537.0
            hi = scaled - (scaled - value)
            rest = value - hi
            scaled = rest * 65537.0
            mid = scaled - (scaled - rest)
            low = rest - mid
            parts = jnp.where(place == 0, hi, jnp.where(place == 1, mid, low))
            parts = jnp.where(place < 3, parts, 0.0).astype(BF)
            for q in range(per):
                pay_out[h * per + q, :slice_rows, :] = fresh[q * slice_rows : (q + 1) * slice_rows]
                pay_out[h * per + q, slice_rows:, :] = parts


def project(candidate, in_proj, bc_proj, step_proj, bias, rate, heads, n_seq):
    tlen, width = candidate.shape
    chan = in_proj.shape[1]
    two = bc_proj.shape[1]
    slice_rows = chan // n_seq
    depth = min(width, 1024)
    small = jax.ShapeDtypeStruct((tlen, tlen), F32)
    fixed = lambda *shape: pl.BlockSpec(shape, lambda i: (0,) * len(shape))
    return pl.pallas_call(
        functools.partial(proj_kernel, heads, slice_rows),
        grid=(width // depth,),
        out_shape=(
            jax.ShapeDtypeStruct((tlen, chan), BF),
            jax.ShapeDtypeStruct((tlen, two), BF),
            small, small, small, small, small,
            jax.ShapeDtypeStruct((n_seq, slice_rows + EXTRA, two // 2), BF),
        ),
        in_specs=[
            pl.BlockSpec((tlen, depth), lambda i: (0, i)),
            pl.BlockSpec((depth, chan), lambda i: (i, 0)),
            pl.BlockSpec((depth, two), lambda i: (i, 0)),
            pl.BlockSpec((heads, depth), lambda i: (0, i)),
            fixed(1, tlen), fixed(1, tlen),
        ],
        out_specs=(
            fixed(tlen, chan), fixed(tlen, two),
            fixed(tlen, tlen), fixed(tlen, tlen), fixed(tlen, tlen), fixed(tlen, tlen),
            fixed(tlen, tlen), fixed(n_seq, slice_rows + EXTRA, two // 2),
        ),
        scratch_shapes=[
            pltpu.VMEM((tlen, chan), F32), pltpu.VMEM((tlen, two), F32), pltpu.VMEM((tlen, tlen), F32)
        ],
        compiler_params=vmem(56),
        cost_estimate=cost(2 * tlen * width * (chan + two), 2 * width * (chan + two + 2 * tlen)),
        name="project",
    )(candidate, in_proj, bc_proj, step_proj, bias, rate)


def enter_kernel(got, out, decay):
    count, rows, nstate = out.shape
    out[0] = jnp.zeros((rows, nstate), BF)
    state = jnp.zeros((rows, nstate), F32)
    for s in range(count):
        tags = got[s, rows:, :].astype(F32)
        fade = jnp.exp(jnp.sum(tags, axis=0, keepdims=True))
        decay[s : s + 1, :] = fade
        if s < count - 1:
            state = fade * state + got[s, :rows, :].astype(F32)
            out[s + 1] = state.astype(BF)


def enter_states(got, slice_rows):
    count, _, nstate = got.shape
    return single(
        enter_kernel,
        out_shape=(
            jax.ShapeDtypeStruct((count, slice_rows, nstate), BF),
            jax.ShapeDtypeStruct((count, nstate), F32),
        ),
        args=(got,),
        compiler_params=vmem(56),
        name="enter",
    )


def leave_kernel(got, decay, out):
    count, rows, nstate = out.shape
    out[count - 1] = jnp.zeros((rows, nstate), BF)
    state = jnp.zeros((rows, nstate), F32)
    for s in range(count - 1, 0, -1):
        state = decay[s : s + 1, :] * state + got[s].astype(F32)
        out[s - 1] = state.astype(BF)


def leave_states(got, decay):
    return single(
        leave_kernel,
        out_shape=jax.ShapeDtypeStruct(got.shape, BF),
        args=(got, decay,),
        compiler_params=vmem(56),
        name="leave",
    )


def decay_weights(cum, cum_t, h):
    tlen = cum.shape[0]
    gaps = jnp.minimum(cum[:, h : h + 1] - cum_t[h : h + 1, :], 0.0)
    return jnp.where(row_mask(tlen), jnp.exp(gaps), 0.0)


def within_kernel(heads, inner_ref, bc_ref, cum_ref, cum_t_ref, step_t_ref, skip_ref, out):
    tlen, chan = out.shape
    size = chan // heads
    bc = bc_ref[...]
    nstate = bc.shape[1] // 2
    scores = mm_t(bc[:, nstate:], bc[:, :nstate])
    cum, cum_t, step_t = cum_ref[...], cum_t_ref[...], step_t_ref[...]
    for h in range(heads):
        span = slice(h * size, (h + 1) * size)
        mixing = (decay_weights(cum, cum_t, h) * scores * step_t[h : h + 1, :]).astype(BF)
        inner = inner_ref[:, span]
        out[:, span] = mm(mixing, inner) + skip_ref[:, span] * inner.astype(F32)


def mix_within(inner_b, bc_bf, cum, cum_t, step_t, skip, heads):
    tlen, chan = inner_b.shape
    return single(
        functools.partial(within_kernel, heads),
        out_shape=jax.ShapeDtypeStruct((tlen, chan), F32),
        args=(inner_b, bc_bf, cum, cum_t, step_t, skip,),
        compiler_params=vmem(56),
        cost_estimate=cost(2 * tlen * tlen * chan * 4, 8 * tlen * chan),
        name="mix_within",
    )


def slots_kernel(
    heads, cap, within, bc_ref, cum_ref, state, table, own_table, cand, w_out,
    own_out, send1, send2, send3, reads_out, slots,
):
    @pl.when(pl.program_id(0) == 0)
    def _():
        chan = within.shape[1]
        size = chan // heads
        nstate = bc_ref.shape[1] // 2
        c_rows = bc_ref[:, nstate:]
        growth = jnp.exp(cum_ref[...])
        for h in range(heads):
            span = slice(h * size, (h + 1) * size)
            reads = mm_t(c_rows, state[span, :])
            reads_out[:, span] = reads
            mixed = (within[:, span] + growth[:, h : h + 1] * reads).astype(BF)
            slots[:, span] = mm(table[...], mixed).astype(BF)

    part = mm(slots[...], w_out[...])
    own_out[...] = part[:cap] + mm(own_table[...], cand[...])
    for k, send in enumerate((send1, send2, send3)):
        send[...] = part[(k + 1) * cap : (k + 2) * cap].astype(BF)


def mix_slots(within, bc_bf, cum, state, table, own_table, candidate, out_proj, heads):
    tlen, chan = within.shape
    width = out_proj.shape[1]
    rows = table.shape[0]
    block = min(width, 2048)
    fixed = lambda a: pl.BlockSpec(a.shape, lambda i: (0,) * a.ndim)
    cols = lambda n: pl.BlockSpec((n, block), lambda i: (0, i))
    sent = jax.ShapeDtypeStruct((CAP, width), BF)
    return pl.pallas_call(
        functools.partial(slots_kernel, heads, CAP),
        grid=(width // block,),
        out_shape=(
            jax.ShapeDtypeStruct((CAP, width), F32), sent, sent, sent,
            jax.ShapeDtypeStruct((tlen, chan), F32),
        ),
        in_specs=[fixed(a) for a in (within, bc_bf, cum, state, table, own_table)]
        + [cols(tlen), cols(chan)],
        out_specs=(cols(CAP), cols(CAP), cols(CAP), cols(CAP), fixed(within)),
        scratch_shapes=[pltpu.VMEM((rows, chan), BF)],
        compiler_params=vmem(56),
        cost_estimate=cost(2 * rows * chan * width, 2 * chan * width),
        name="mix_slots",
    )(within, bc_bf, cum, state, table, own_table, candidate, out_proj)


def outgrad_kernel(heads, table, terms, energy, w_out, bc_ref, cum_ref, hid_out, grad_out, local_out, acc):
    i = pl.program_id(0)

    @pl.when(i == 0)
    def _():
        acc[...] = jnp.zeros_like(acc)

    hid = energy[...] + t_mm(table[...], terms[...])
    hid_out[...] = hid
    acc[...] += mm_t(hid.astype(BF), w_out[...])

    @pl.when(i == pl.num_programs(0) - 1)
    def _():
        chan = acc.shape[1]
        size = chan // heads
        nstate = bc_ref.shape[1] // 2
        c_rows = bc_ref[:, nstate:]
        growth = jnp.exp(cum_ref[...])
        for h in range(heads):
            span = slice(h * size, (h + 1) * size)
            grad = acc[:, span]
            grad_out[:, span] = grad
            grown = (growth[:, h : h + 1] * grad).astype(BF)
            local_out[span, :] = t_mm(grown, c_rows).astype(BF)


def out_gradient(table, terms, energy, out_proj, bc_bf, cum, heads):
    tlen = table.shape[1]
    chan, width = out_proj.shape
    nstate = bc_bf.shape[1] // 2
    block = min(width, 2048)
    fixed = lambda *shape: pl.BlockSpec(shape, lambda i: (0,) * len(shape))
    cols = lambda n: pl.BlockSpec((n, block), lambda i: (0, i))
    return pl.pallas_call(
        functools.partial(outgrad_kernel, heads),
        grid=(width // block,),
        out_shape=(
            jax.ShapeDtypeStruct((tlen, width), F32),
            jax.ShapeDtypeStruct((tlen, chan), F32),
            jax.ShapeDtypeStruct((chan, nstate), BF),
        ),
        in_specs=[
            fixed(*table.shape), cols(terms.shape[0]), cols(1), cols(chan),
            fixed(*bc_bf.shape), fixed(*cum.shape),
        ],
        out_specs=(cols(tlen), fixed(tlen, chan), fixed(chan, nstate)),
        scratch_shapes=[pltpu.VMEM((tlen, chan), F32)],
        compiler_params=vmem(56),
        cost_estimate=cost(2 * tlen * chan * width, 2 * chan * width),
        name="out_gradient",
    )(table, terms, energy, out_proj, bc_bf, cum)


def near_kernel(
    heads, grad_ref, inner_ref, bc_ref, cum_ref, cum_t_ref, step_ref, step_t_ref, reads, state, skip_ref,
    g_out, gb_out, gc_out, dcum_out, dstep_out, rows, cols,
):
    tlen, chan = grad_ref.shape
    size = chan // heads
    nstate = bc_ref.shape[1] // 2
    b_rows, c_rows = bc_ref[:, :nstate], bc_ref[:, nstate:]
    scores = mm_t(c_rows, b_rows)
    cum, cum_t, step_t = cum_ref[...], cum_t_ref[...], step_t_ref[...]
    growth = jnp.exp(cum)
    rows[...] = jnp.zeros_like(rows)
    cols[...] = jnp.zeros_like(cols)
    d_scores = jnp.zeros((tlen, tlen), F32)
    g_c = jnp.zeros((tlen, nstate), F32)
    for h in range(heads):
        span = slice(h * size, (h + 1) * size)
        grad = grad_ref[:, span]
        grad_b = grad.astype(BF)
        inner = inner_ref[:, span]
        step_h = step_t[h : h + 1, :]
        weights = decay_weights(cum, cum_t, h)
        d_w = mm_t(grad_b, inner) * weights
        d_scores = d_scores + d_w * step_h
        d_ws = d_w * scores
        rows[h : h + 1, :] = jnp.sum(d_ws, axis=0, keepdims=True)
        grown = growth[:, h : h + 1] * grad
        cols[:, h : h + 1] = jnp.sum(d_ws * step_h, axis=1, keepdims=True) + jnp.sum(
            grown * reads[:, span], axis=1, keepdims=True
        )
        mixing = (weights * scores * step_h).astype(BF)
        g_out[:, span] = t_mm(mixing, grad_b) + skip_ref[:, span] * grad
        g_c = g_c + mm(grown.astype(BF), state[span, :])
    d_scores = d_scores.astype(BF)
    gc_out[...] = g_c + mm(d_scores, b_rows)
    gb_out[...] = t_mm(d_scores, c_rows)
    d_step = rows[...].T
    dstep_out[...] = d_step
    dcum_out[...] = cols[...] - step_ref[...] * d_step


def near_gradient(grad, inner_b, bc_bf, cum, cum_t, step, step_t, reads, state, skip, heads):
    tlen, chan = grad.shape
    small = jax.ShapeDtypeStruct((tlen, tlen), F32)
    return single(
        functools.partial(near_kernel, heads),
        out_shape=(jax.ShapeDtypeStruct((tlen, chan), F32), small, small, small, small),
        args=(grad, inner_b, bc_bf, cum, cum_t, step, step_t, reads, state, skip,),
        scratch_shapes=[pltpu.VMEM((tlen, tlen), F32)] * 2,
        compiler_params=vmem(56),
        cost_estimate=cost(2 * tlen * tlen * chan * 8, 20 * tlen * chan),
        name="near_gradient",
    )


def far_kernel(
    heads, later, state, inner_ref, bc_ref, cum_ref, step_ref, pre_ref, rate, near, gb_ref, gc_ref,
    dcum_ref, dstep_ref, g_out, gbc_out, gpre_out, kept, cols,
):
    tlen, chan = near.shape
    size = chan // heads
    nstate = bc_ref.shape[1] // 2
    b_rows = bc_ref[:, :nstate]
    cum, step, pre = cum_ref[...], step_ref[...], pre_ref[...]
    last = cum[tlen - 1 : tlen, :]
    fade = jnp.exp(last - cum)
    tail = fade * step
    kept[...] = jnp.zeros_like(kept)
    cols[...] = jnp.zeros_like(cols)
    g_b = gb_ref[...]
    for h in range(heads):
        span = slice(h * size, (h + 1) * size)
        late = later[span, :]
        tail_h = tail[:, h : h + 1]
        fed_back = mm_t(b_rows, late)
        g_out[:, span] = (near[:, span] + tail_h * fed_back).astype(BF)
        inner = inner_ref[:, span].astype(F32)
        cols[:, h : h + 1] = jnp.sum(inner * fed_back, axis=1, keepdims=True)
        g_b = g_b + mm((tail_h * inner).astype(BF), late)
        kept[h : h + 1, :] = jnp.sum(
            state[span, :].astype(F32) * late.astype(F32), axis=0, keepdims=True
        )
    gbc_out[:, :nstate] = g_b.astype(BF)
    gbc_out[:, nstate:] = gc_ref[...].astype(BF)
    d_tail = cols[...]
    tail_term = d_tail * tail
    kept_row = jnp.sum(kept[...].T, axis=0, keepdims=True)
    d_last = jnp.exp(last) * kept_row + jnp.sum(tail_term, axis=0, keepdims=True)
    rowpos = lax.broadcasted_iota(jnp.int32, cum.shape, 0)
    d_cum = dcum_ref[...] - tail_term + jnp.where(rowpos == tlen - 1, d_last, 0.0)
    colpos = lax.broadcasted_iota(jnp.int32, cum.shape, 1)
    upper = (rowpos <= colpos).astype(F32)
    d_decay = jnp.dot(upper, d_cum, precision=HIGH, preferred_element_type=F32)
    g_step = dstep_ref[...] + fade * d_tail - rate[...] * d_decay
    gpre_out[...] = (g_step / (1.0 + jnp.exp(-pre))).astype(BF)


def far_gradient(later, state, inner_b, bc_bf, cum, step, pre, rate, near, gb, gc, dcum, dstep, heads):
    tlen, chan = near.shape
    return single(
        functools.partial(far_kernel, heads),
        out_shape=(
            jax.ShapeDtypeStruct((tlen, chan), BF),
            jax.ShapeDtypeStruct(bc_bf.shape, BF),
            jax.ShapeDtypeStruct((tlen, tlen), BF),
        ),
        args=(later, state, inner_b, bc_bf, cum, step, pre, rate, near, gb, gc, dcum, dstep,),
        scratch_shapes=[pltpu.VMEM((tlen, tlen), F32)] * 2,
        compiler_params=vmem(56),
        cost_estimate=cost(2 * tlen * tlen * chan * 4, 20 * tlen * chan),
        name="far_gradient",
    )


def back_kernel(heads, per, which, g_ref, gbc, gpre, w_in, w_bc, w_step, *outs):
    total = mm_t(g_ref[...], w_in[...]) + mm_t(gbc[...], w_bc[...])
    total += mm(gpre[:, :heads], w_step[...])
    for k, out in enumerate(outs):

        @pl.when(pl.program_id(0) // per == k)
        def _():
            out[...] = total.astype(out.dtype)


def back_columns(which, g_inner, g_bc, g_pre, in_proj, bc_proj, step_w, cols, dtype, heads):
    tlen, chan = g_inner.shape
    two = bc_proj.shape[1]
    count = which.shape[0]
    block = min(cols, 1024)
    per = cols // block
    fixed = lambda a: pl.BlockSpec(a.shape, lambda i, w: (0,) * a.ndim)
    place = lambda i, w: w[i // per] * per + i % per
    rows = lambda n: pl.BlockSpec((block, n), lambda i, w: (place(i, w), 0))
    return pl.pallas_call(
        functools.partial(back_kernel, heads, per),
        grid_spec=pltpu.PrefetchScalarGridSpec(
            num_scalar_prefetch=1,
            grid=(count * per,),
            in_specs=[
                fixed(g_inner), fixed(g_bc), fixed(g_pre), rows(chan), rows(two),
                pl.BlockSpec((heads, block), lambda i, w: (0, place(i, w))),
            ],
            out_specs=tuple(
                pl.BlockSpec((tlen, block), lambda i, w, k=k: (0, jnp.clip(i - k * per, 0, per - 1)))
                for k in range(count)
            ),
        ),
        out_shape=tuple(jax.ShapeDtypeStruct((tlen, cols), dtype) for _ in range(count)),
        compiler_params=vmem(56),
        cost_estimate=cost(2 * tlen * (chan + two) * cols * count, 2 * (chan + two) * cols * count),
        name="back_columns",
    )(which, g_inner, g_bc, g_pre, in_proj, bc_proj, step_w)


def shards(
    candidate,
    in_proj,
    bc_proj,
    step_proj,
    step_bias,
    decay_rate,
    skip_gain,
    out_proj,
    expert_ids,
    gate_weights,
    expert_gate,
    expert_up,
    expert_down,
    energy_head,
):
    tlen, width = candidate.shape
    heads = step_bias.shape[0]
    step_w = step_proj.T
    chan = in_proj.shape[1]
    size = chan // heads
    nstate = bc_proj.shape[1] // 2
    column = lax.axis_index("e")
    n_exp = lax.axis_size("e")
    n_seq = lax.axis_size(SEQ)
    col_count = width // n_exp
    slice_rows = chan // n_seq
    lanes = lambda v: jnp.pad(v, (0, tlen - heads))[None, :]
    bias, rate = lanes(step_bias), lanes(decay_rate)
    skip = jnp.repeat(skip_gain, size)[None, :]
    energy = energy_head[None, :]

    wg0, wu0 = expert_gate[0], expert_up[0]
    wg1 = shift(wg0, "c", 1)
    wu1 = shift(wu0, "c", 1)

    pairs = [
        slot_table(expert_ids, gate_weights, lax.rem(column + k, n_exp)) for k in range(n_exp)
    ]
    table = jnp.concatenate([p[0] for p in pairs], axis=0).astype(BF)
    own_table, own_weight = pairs[0]
    slot_weight = jnp.sum(own_table * own_weight[None, :], axis=1, keepdims=True)
    own_table = own_table.astype(BF)

    inner_b, bc_bf, pre, step, cum, step_t, cum_t, payload = project(
        candidate, in_proj, bc_proj, step_w, bias, rate, heads, n_seq
    )
    payload, wg1, wu1, table, own_table, slot_weight = lax.optimization_barrier(
        (payload, wg1, wu1, table, own_table, slot_weight)
    )
    got = lax.all_to_all(payload, SEQ, 0, 0, tiled=True)
    within = mix_within(inner_b, bc_bf, cum, cum_t, step_t, skip, heads)
    entering, decay = enter_states(got, slice_rows)
    entering, down = lax.optimization_barrier((entering, expert_down[0]))
    head_own = jnp.sum(down.astype(F32) * energy, axis=1)
    head_other = shift(head_own[None, :], "c", 1)
    head_vec = jnp.concatenate([head_own[None, :], head_other], axis=0)
    state = lax.all_to_all(entering, SEQ, 0, 0, tiled=True).reshape(chan, nstate)

    own, send1, send2, send3, reads = mix_slots(
        within, bc_bf, cum, state, table, own_table, candidate, out_proj, heads
    )
    for k, send in enumerate((send1, send2, send3)):
        own = own + shift(send, "e", k + 1).astype(F32)
    hidden = own.astype(BF).astype(F32)
    scale = jnp.sqrt(jnp.mean(hidden * hidden, axis=-1, keepdims=True) + EPS)
    normed = hidden / scale
    routed = normed.astype(BF)

    side = lax.axis_size("x")
    cut = width // 2
    routed, head_vec = lax.optimization_barrier((routed, head_vec))
    near_own = jnp.concatenate(gather_direct(routed[:, :cut], "z"), axis=0)
    far_own = jnp.concatenate(gather_direct(routed[:, cut:], "x"), axis=0)
    near_rows = gather_around(near_own, "x")
    far_rows = gather_around(far_own, "z")
    out_near, out_far = expert_rows(near_rows, far_rows, wg0, wg1, wu0, wu1, head_vec)
    near_sum = scatter_around(split_rows(out_near, side), "x").astype(BF)
    far_sum = scatter_around(split_rows(out_far, side), "z").astype(BF)
    slot_grad = jnp.concatenate(
        [
            scatter_direct(split_rows(near_sum, side), "z"),
            scatter_direct(split_rows(far_sum, side), "x"),
        ],
        axis=1,
    )
    along = jnp.mean(normed * slot_grad, axis=-1, keepdims=True)
    slot_term = (slot_weight * (slot_grad - normed * along) / scale).astype(BF)
    all_terms = jnp.concatenate(
        [slot_term] + [shift(slot_term, "e", n_exp - k) for k in range(1, n_exp)], axis=0
    )
    hid_grad, out_grad, local_grad = out_gradient(
        table, all_terms, energy, out_proj, bc_bf, cum, heads
    )

    got_grad = lax.all_to_all(
        local_grad.reshape(n_seq, slice_rows, nstate), SEQ, 0, 0, tiled=True
    )
    near, gb, gc, dcum, dstep = near_gradient(
        out_grad, inner_b, bc_bf, cum, cum_t, step, step_t, reads, state, skip, heads
    )
    leaving = leave_states(got_grad, decay)
    later = lax.all_to_all(leaving, SEQ, 0, 0, tiled=True).reshape(chan, nstate)
    g_inner, g_bc, g_pre = far_gradient(
        later, state, inner_b, bc_bf, cum, step, pre, rate, near, gb, gc, dcum, dstep, heads
    )

    def columns(places, dtype):
        which = jnp.stack([lax.rem(column + k, n_exp) for k in places])
        return back_columns(
            which, g_inner, g_bc, g_pre, in_proj, bc_proj, step_w, col_count, dtype, heads
        )

    order = (2, 1, 3)
    arrived = [shift(part, "e", k) for k, part in zip(order, columns(order, BF))]
    (own_part,) = columns((0,), F32)
    summed = lax.dynamic_slice_in_dim(hid_grad, column * col_count, col_count, 1) + own_part
    for value in arrived:
        summed = summed + value.astype(F32)
    own_cand = lax.dynamic_slice_in_dim(candidate, column * col_count, col_count, 1).astype(F32)
    return (own_cand - DESCENT * summed).astype(BF)


def solution(mesh):
    n_seq, n_exp = mesh.devices.shape
    side = int(round((n_seq // 2) ** 0.5))
    grid = Mesh(mesh.devices.reshape(side, side, 2, n_exp), ("x", "z", "c", "e"))
    in_specs = (
        P(SEQ, None),
        P(None, "e"),
        P(),
        P(None, "e"),
        P("e"),
        P("e"),
        P("e"),
        P("e", None),
        P(SEQ, None),
        P(SEQ, None),
        P("e", None, SEQ),
        P("e", None, SEQ),
        P("e", SEQ, None),
        P(),
    )
    return jax.shard_map(
        shards, mesh=grid, in_specs=in_specs, out_specs=P(SEQ, "e"), check_vma=False
    )
```
